32 devices in a mesh: fsdp: 8 (over z, y), tensor: 4 (over x, core).
Axes of the slice: x: 2, y: 2, z: 4, core: 2. Of those that a mesh axis runs over, the one named last changes fastest.
Arguments:
- tokens: bfloat16 [8192, 2560], P(('fsdp', 'tensor')), may hold values from -6 to 6
- segments: int32 [8192], P('fsdp'), may hold values from 0 to 3, as said below
- positions: int32 [8192], P('fsdp'), may hold values from 0 to 2046, as said below
- norm_input: bfloat16 [2560], P(('fsdp', 'tensor')), may hold values from 0.5 to 1.5
- norm_query: bfloat16 [768], P(('fsdp', 'tensor')), may hold values from 0.5 to 1.5
- norm_latent: bfloat16 [256], P(('fsdp', 'tensor')), may hold values from 0.5 to 1.5
- norm_hidden: bfloat16 [2560], P(('fsdp', 'tensor')), may hold values from 0.5 to 1.5
- query_down: bfloat16 [2560, 768], P(('fsdp', 'tensor')), may hold values from -0.125 to 0.125
- latent_down: bfloat16 [2560, 288], P(('fsdp', 'tensor')), may hold values from -0.125 to 0.125
- query_up: bfloat16 [768, 3840], P('fsdp', 'tensor'), may hold values from -0.3125 to 0.3125
- latent_up: bfloat16 [256, 5120], P('fsdp', 'tensor'), may hold values from -0.375 to 0.375
- attention_out: bfloat16 [2560, 2560], P('tensor', 'fsdp'), may hold values from -2 to 2
- gate_weight: bfloat16 [2560, 6400], P('fsdp', 'tensor'), may hold values from -0.125 to 0.125
- up_weight: bfloat16 [2560, 6400], P('fsdp', 'tensor'), may hold values from -0.125 to 0.125
- down_weight: bfloat16 [6400, 2560], P('tensor', 'fsdp'), may hold values from -0.4375 to 0.4375
- cotangent: bfloat16 [8192, 2560], P(('fsdp', 'tensor')), may hold values from -6 to 6
Outputs:
- output: bfloat16 [8192, 2560], P(('fsdp', 'tensor'))
- token_grad: float32 [8192, 2560], P(('fsdp', 'tensor'))
- grad_norm_input: float32 [2560], P(('fsdp', 'tensor'))
- grad_norm_query: float32 [768], P(('fsdp', 'tensor'))
- grad_norm_latent: float32 [256], P(('fsdp', 'tensor'))
- grad_norm_hidden: float32 [2560], P(('fsdp', 'tensor'))
- grad_query_down: float32 [2560, 768], P(('fsdp', 'tensor'))
- grad_latent_down: float32 [2560, 288], P(('fsdp', 'tensor'))
- grad_query_up: float32 [768, 3840], P('fsdp', 'tensor')
- grad_latent_up: float32 [256, 5120], P('fsdp', 'tensor')
- grad_attention_out: float32 [2560, 2560], P('tensor', 'fsdp')
- grad_gate_weight: float32 [2560, 6400], P('fsdp', 'tensor')
- grad_up_weight: float32 [2560, 6400], P('fsdp', 'tensor')
- grad_down_weight: float32 [6400, 2560], P('tensor', 'fsdp')
The draws below stay inside these ranges and needn't reach their ends.
Inputs may be any that keep to these rules, and one draw needn't show every extreme that they name: `segments`: within each sequence of 1024 tokens the ids never fall and each of 0, 1, 2, 3 occurs; document 1 begins within the first 256 tokens and ends within the last 256. Within a document the positions count up by one; in every sequence the last token of document 1 has position 2046.
All inputs are finite; a program needn't handle non-finite values.
Results may differ from the reference program's by a relative error of at most 0.028.
Values may be sent and summed in bfloat16 or wider, within the bound.
No kernel may reach another device: no remote copies, remote signals or barrier semaphores. Data moves between devices by JAX's collectives and lax.ppermute only.
A program may use at most 256 MiB of HBM per device.

```python
import math
import jax
import jax.numpy as jnp
from jax import lax

D = 2560
HEADS = 40
NOPE = 64
ROPE = 32
VDIM = 64
QR = 768
KVR = 256
FF = 6400
TOK_DEV = 256
SEQ = 1024
TOKENS = 8192


def document_layout(key):
    count = TOKENS // SEQ
    first, second, third = jax.random.split(key, 3)
    head_end = jax.random.randint(first, (count, 1), 1, TOK_DEV)
    long_end = jax.random.randint(second, (count, 1), SEQ - TOK_DEV + 1, SEQ - 1)
    tail_cut = jax.random.randint(third, (count, 1), long_end + 1, SEQ)
    place = jnp.arange(SEQ, dtype=jnp.int32)[None, :]
    ident = (place >= head_end).astype(jnp.int32) + (place >= long_end).astype(jnp.int32) + (place >= tail_cut).astype(jnp.int32)
    begins = jnp.where(ident == 0, 0, jnp.where(ident == 1, head_end, jnp.where(ident == 2, long_end, tail_cut)))
    return (ident, place - begins, head_end, long_end)


def draw_segments(key, part):
    ident, inside, head_end, long_end = document_layout(key)
    return ident.reshape(TOKENS).astype(jnp.int32)


def draw_positions(key, part):
    ident, inside, head_end, long_end = document_layout(key)
    key = jax.random.fold_in(key, 7)
    starts = jax.random.randint(key, (TOKENS // SEQ, 4), 0, 1024)
    chosen = jnp.take_along_axis(starts, ident, axis=1)
    long_start = SEQ + 1023 - long_end + head_end
    chosen = jnp.where(ident == 1, long_start, chosen)
    return (chosen + inside).reshape(TOKENS).astype(jnp.int32)


def shard_levels(stream_key, shape, cuts, least, largest):
    level = 1.0
    for position, blocks in cuts:
        draws = jax.random.uniform(jax.random.fold_in(jax.random.fold_in(stream_key, 6), position), (blocks,), jnp.float32, least / len(cuts), largest / len(cuts))
        level = level * jnp.repeat(jnp.exp(draws), shape[position] // blocks).reshape((-1,) + (1,) * (len(shape) - 1 - position))
    return level


def gaussian(own_key, shape, spread, most, cuts=(), held_as=jnp.bfloat16):
    factor_of = shard_levels(own_key, shape, cuts, -0.22, 0.18) if cuts else 1.0
    values = jax.random.normal(own_key, shape, jnp.float32) * spread * factor_of
    return jnp.minimum(jnp.maximum(values, -most), most).astype(held_as)


def setup_inputs(seed: int = 0) -> dict:
    streams_of = jax.random.split(jax.random.key(seed), 17)
    return {
        "tokens": gaussian(streams_of[0], (TOKENS, D), 1.0, 6.0, ((0, 32),)),
        "segments": draw_segments(jax.random.fold_in(streams_of[16], 71), 0),
        "positions": draw_positions(jax.random.fold_in(streams_of[16], 71), 0),
        "norm_input": jnp.clip(1.0 + 0.1 * jax.random.normal(streams_of[3], (D,), jnp.float32), 0.5, 1.5).astype(jnp.bfloat16),
        "norm_query": jnp.clip(1.0 + 0.1 * jax.random.normal(streams_of[4], (QR,), jnp.float32), 0.5, 1.5).astype(jnp.bfloat16),
        "norm_latent": jnp.clip(1.0 + 0.1 * jax.random.normal(streams_of[5], (KVR,), jnp.float32), 0.5, 1.5).astype(jnp.bfloat16),
        "norm_hidden": jnp.clip(1.0 + 0.1 * jax.random.normal(streams_of[6], (D,), jnp.float32), 0.5, 1.5).astype(jnp.bfloat16),
        "query_down": gaussian(streams_of[7], (D, QR), D ** -0.5, 0.125, ((0, 32),)),
        "latent_down": gaussian(streams_of[8], (D, KVR + ROPE), D ** -0.5, 0.125, ((0, 32),)),
        "query_up": gaussian(streams_of[9], (QR, HEADS * (NOPE + ROPE)), (QR // 2) ** -0.5, 0.3125, ((0, 8), (1, 4))),
        "latent_up": gaussian(streams_of[10], (KVR, HEADS * (NOPE + VDIM)), KVR ** -0.5, 0.375, ((0, 8), (1, 4))),
        "attention_out": gaussian(streams_of[11], (HEADS * VDIM, D), 8 ** -0.5, 2.0, ((0, 4), (1, 8))),
        "gate_weight": gaussian(streams_of[12], (D, FF), D ** -0.5, 0.125, ((0, 8), (1, 4))),
        "up_weight": gaussian(streams_of[13], (D, FF), D ** -0.5, 0.125, ((0, 8), (1, 4))),
        "down_weight": gaussian(streams_of[14], (FF, D), (FF // 32) ** -0.5, 0.4375, ((0, 4), (1, 8))),
        "cotangent": gaussian(streams_of[15], (TOKENS, D), 1.0, 6.0, ((0, 32),)),
    }


EPSILON = 1e-05
RESIDUAL = 1.4 / math.sqrt(62.0)
NEGATIVE = -1e+30
HIGH = lax.Precision.HIGHEST

@jax.custom_vjp
def low(v):
    return lax.optimization_barrier(v.astype(jnp.bfloat16)).astype(jnp.float32)

@jax.custom_vjp
def low_back(v):
    return v

def low_keep(v):
    return (low(v), None)

def low_pass(kept, grad):
    return (grad,)

def back_keep(v):
    return (v, None)

def back_low(kept, grad):
    return (low(grad),)
low.defvjp(low_keep, low_pass)
low_back.defvjp(back_keep, back_low)

def normalize(values, gain):
    return values * lax.rsqrt(lax.optimization_barrier(jnp.mean(values * values, axis=-1, keepdims=True)) + EPSILON) * gain

def rotary_tables(positions):
    steps = jnp.arange(ROPE // 2, dtype=jnp.float32)
    frequency = jnp.exp(steps * (-2.0 * math.log(10000.0) / ROPE))
    angles = positions.astype(jnp.float32)[:, None] * frequency[None, :]
    return (jnp.cos(angles), jnp.sin(angles))

def rotate(values, cosine, sine):
    half = values.shape[-1] // 2
    first = values[..., :half]
    second = values[..., half:]
    return jnp.concatenate([first * cosine - second * sine, second * cosine + first * sine], axis=-1)

def multiply(left, right):
    return jnp.dot(left, right, precision=HIGH, preferred_element_type=jnp.float32)

def attend(query_heads, keys, values, segment_ids):
    length = query_heads.shape[0]
    block = min(512, length)
    count = length // block
    scale = 1.0 / math.sqrt(NOPE + ROPE)
    columns = jnp.arange(length, dtype=jnp.int32)

    def one_block(item):
        query_block, start = item
        rows_here = start + jnp.arange(block, dtype=jnp.int32)
        segment_block = lax.dynamic_slice_in_dim(segment_ids, start, block)
        scores = jnp.einsum('qhd,khd->hqk', query_block, keys, precision=HIGH) * scale
        scores = low_back(scores)
        allowed = (segment_block[:, None] == segment_ids[None, :]) & (columns[None, :] <= rows_here[:, None])
        scores = jnp.where(allowed[None], scores, NEGATIVE)
        top = lax.optimization_barrier(jnp.max(scores, axis=-1, keepdims=True))
        weights = jnp.exp(scores - top)
        probability = weights / lax.optimization_barrier(jnp.sum(weights, axis=-1, keepdims=True))
        return jnp.einsum('hqk,khd->qhd', low(probability), values, precision=HIGH)
    starts = (jnp.arange(count, dtype=jnp.int32) * block).astype(jnp.int32)
    blocks = query_heads.reshape(count, block, HEADS, NOPE + ROPE)
    result = lax.map(jax.checkpoint(one_block), (blocks, starts))
    return result.reshape(length, HEADS, VDIM)

def layer(token_values, weights, segment_ids, cosine, sine):
    gain_in, gain_query, gain_latent, gain_hidden, query_down, latent_down, query_up, latent_up, attention_out, gate_weight, up_weight, down_weight = weights
    length = token_values.shape[0]
    width = NOPE + ROPE
    attention_input = low(normalize(token_values, gain_in))
    query_latent = low_back(multiply(attention_input, query_down))
    latent_all = low_back(multiply(attention_input, latent_down))
    query_normed = low(normalize(query_latent, gain_query))
    key_latent = low(normalize(latent_all[:, :KVR], gain_latent))
    key_rope = low(rotate(latent_all[:, KVR:], cosine, sine))
    query_raw = low_back(multiply(query_normed, query_up)).reshape(length, HEADS, width)
    query_heads = low(jnp.concatenate([query_raw[..., :NOPE], rotate(query_raw[..., NOPE:], cosine[:, None, :], sine[:, None, :])], axis=-1))
    key_value = low_back(multiply(key_latent, latent_up)).reshape(length, HEADS, NOPE + VDIM)
    key_nope = low(key_value[..., :NOPE])
    values = low(key_value[..., NOPE:])
    keys = jnp.concatenate([key_nope, jnp.broadcast_to(key_rope[:, None, :], (length, HEADS, ROPE))], axis=-1)
    heads = attend(query_heads, keys, values, segment_ids)
    heads = low(low_back(heads.reshape(length, HEADS * VDIM)))
    hidden = token_values + RESIDUAL * low_back(multiply(heads, attention_out))
    feed_input = low(normalize(hidden, gain_hidden))
    gate = low_back(multiply(feed_input, gate_weight))
    up_values = low_back(multiply(feed_input, up_weight))
    activated = low(jax.nn.silu(gate) * up_values)
    return hidden + RESIDUAL * low_back(multiply(activated, down_weight))

def reference(tokens, segments, positions, norm_input, norm_query, norm_latent, norm_hidden, query_down, latent_down, query_up, latent_up, attention_out, gate_weight, up_weight, down_weight, cotangent):
    count = TOKENS // SEQ
    weights = tuple((w.astype(jnp.float32) for w in (norm_input, norm_query, norm_latent, norm_hidden, query_down, latent_down, query_up, latent_up, attention_out, gate_weight, up_weight, down_weight)))
    token_seqs = tokens.astype(jnp.float32).reshape(count, SEQ, D)
    upstream_seqs = cotangent.astype(jnp.float32).reshape(count, SEQ, D)
    segment_seqs = segments.reshape(count, SEQ)
    position_seqs = positions.reshape(count, SEQ)

    def step(totals, item):
        token_values, segment_ids, position_ids, upstream = item
        cosine, sine = rotary_tables(position_ids)

        def forward(values, *parameters):
            return layer(values, parameters, segment_ids, cosine, sine)
        result, pull = jax.vjp(forward, token_values, *weights)
        gradient = pull(upstream)
        totals = tuple((total + part for total, part in zip(totals, gradient[1:])))
        return (totals, (result.astype(jnp.bfloat16), gradient[0]))
    initial = tuple((jnp.zeros(w.shape, jnp.float32) for w in weights))
    totals, (results, token_grads) = lax.scan(step, initial, (token_seqs, segment_seqs, position_seqs, upstream_seqs))
    return (results.reshape(TOKENS, D), token_grads.reshape(TOKENS, D), totals[0], totals[1], totals[2], totals[3], totals[4], totals[5], totals[6], totals[7], totals[8], totals[9], totals[10], totals[11])
```

```python
import functools
import math

import jax
import jax.numpy as jnp
from jax import lax
from jax.experimental import pallas as pl
from jax.experimental.pallas import tpu as pltpu
from jax.sharding import PartitionSpec as P

HEADS = 40
NOPE = 64
ROPE = 32
VDIM = 64
KVR = 256
LANES = 128
BLOCK = 256


EPSILON = 1e-05
RESIDUAL = 1.4 / math.sqrt(62.0)
NEGATIVE = -1e30
APART = -(2.0**96)
SCALE = 1.0 / math.sqrt(NOPE + ROPE)
LOG2E = math.log2(math.e)
ROOM = 56 * 1024 * 1024
BRIEF = pl.CostEstimate(flops=1, bytes_accessed=1, transcendentals=0)


def lasting(microseconds):
    return pl.CostEstimate(flops=1, bytes_accessed=microseconds * 3 * 10**6, transcendentals=0)


def normalize(values, gain):
    inverse = lax.rsqrt(jnp.mean(values * values, axis=-1, keepdims=True) + EPSILON)
    return (values * inverse * gain, inverse)


def normalize_back(values, inverse, gain, upstream):
    scaled = upstream * gain
    inner = jnp.mean(scaled * values, axis=-1, keepdims=True)
    return inverse * scaled - values * (inverse * inverse * inverse) * inner


def product(left, right):
    return jnp.dot(left, right, preferred_element_type=jnp.float32)


def product_left(left, right):
    return lax.dot_general(
        left, right, (((0,), (0,)), ((), ())), preferred_element_type=jnp.float32
    )


def product_right(left, right):
    return lax.dot_general(
        left, right, (((1,), (1,)), ((), ())), preferred_element_type=jnp.float32
    )


def rotary_lanes(positions):
    lane = jnp.arange(LANES, dtype=jnp.int32)
    steps = ((lane - NOPE) % (ROPE // 2)).astype(jnp.float32)
    frequency = jnp.exp(steps * (-2.0 * math.log(10000.0) / ROPE))
    angles = positions.astype(jnp.float32)[:, None] * frequency[None, :]
    first = ((lane >= NOPE) & (lane < NOPE + ROPE // 2))[None, :]
    second = ((lane >= NOPE + ROPE // 2) & (lane < NOPE + ROPE))[None, :]
    cosine = jnp.cos(angles)
    sine = jnp.sin(angles)
    here = jnp.where((lane < NOPE)[None, :], 1.0, jnp.where(first | second, cosine, 0.0))
    return (here, jnp.where(first, -sine, 0.0), jnp.where(second, sine, 0.0))


def segment_lanes(segment_ids):
    lane = jnp.arange(LANES, dtype=jnp.int32) - (NOPE + ROPE)
    same = lane[None, :] == segment_ids[:, None]
    used = ((lane >= 0) & (lane < 4))[None, :]
    query = jnp.where(used & same, 1.0, 0.0)
    key = jnp.where(used & ~same, APART, 0.0)
    return (query, key)


def roll_lanes(values, amount):
    return pltpu.roll(values, amount % LANES, 1)


def forward_kernel(
    xq_ref, lat_ref, wq_ref, wkv_ref, rope_ref, feat_ref, here_ref, low_ref, high_ref,
    out_ref, q_ref, kv_ref, lse_ref, k_ref,
):
    length = xq_ref.shape[0]
    lane = lax.broadcasted_iota(jnp.int32, (BLOCK, LANES), 1)
    causal = lax.broadcasted_iota(jnp.int32, (BLOCK, BLOCK), 1) <= lax.broadcasted_iota(
        jnp.int32, (BLOCK, BLOCK), 0
    )
    blocks = [slice(start, start + BLOCK) for start in range(0, length, BLOCK)]
    for rows in blocks:
        q_raw = product(xq_ref[rows, :], wq_ref[...])
        kv_ref[rows, :] = product(lat_ref[rows, :], wkv_ref[...]).astype(jnp.bfloat16)
        for head in range(2):
            part = slice(head * LANES, (head + 1) * LANES)
            raw = q_raw[:, part]
            turned = (
                raw * here_ref[rows, :]
                + roll_lanes(raw, -ROPE // 2) * low_ref[rows, :]
                + roll_lanes(raw, ROPE // 2) * high_ref[rows, :]
                + feat_ref[rows, :]
            )
            q_ref[rows, part] = turned.astype(jnp.bfloat16)
            k_ref[head, rows, :] = jnp.where(lane < NOPE, kv_ref[rows, part], rope_ref[rows, :])
    for rows in blocks:
        results = []
        for head in range(2):
            part = slice(head * LANES, (head + 1) * LANES)
            query = q_ref[rows, part]
            near = product_right(query, k_ref[head, rows, :])
            near = jnp.where(causal, near, NEGATIVE)
            top = jnp.max(near, axis=1, keepdims=True)
            if rows.start:
                far = product_right(query, k_ref[head, : rows.start, :])
                top = jnp.maximum(top, jnp.max(far, axis=1, keepdims=True))
            weights = jnp.exp2((near - top) * (SCALE * LOG2E))
            total = jnp.sum(weights, axis=1, keepdims=True)
            result = product(weights.astype(jnp.bfloat16), kv_ref[rows, part])
            if rows.start:
                weights = jnp.exp2((far - top) * (SCALE * LOG2E))
                total = total + jnp.sum(weights, axis=1, keepdims=True)
                result = result + product(
                    weights.astype(jnp.bfloat16), kv_ref[: rows.start, part]
                )
            results.append(result / total)
            log_total = top * (SCALE * LOG2E) + jnp.log2(total)
            lse_ref[0, head : head + 1, rows] = jnp.transpose(
                jnp.broadcast_to(log_total, (BLOCK, LANES))
            )[0:1, :]
        out_ref[rows, :] = jnp.where(
            lane < VDIM, roll_lanes(results[0], VDIM), results[1]
        ).astype(jnp.bfloat16)


def attention_forward(latents, wq, wkv, rope, feat, tables, pairs):
    length = latents.shape[0]
    rank = wq.shape[0]
    whole = lambda width, at=0: pl.BlockSpec((length, width), lambda j: (0, at))
    mine = lambda width: pl.BlockSpec((length, width), lambda j: (0, j))
    tall = lambda rows: pl.BlockSpec((rows, 2 * LANES), lambda j: (0, j))
    low = jnp.bfloat16
    return pl.pallas_call(
        forward_kernel,
        grid=(pairs,),
        in_specs=[
            whole(rank), whole(KVR, rank // KVR), tall(rank), tall(KVR),
            whole(LANES), whole(LANES), whole(LANES), whole(LANES), whole(LANES),
        ],
        out_specs=[
            mine(LANES), mine(2 * LANES), mine(2 * LANES),
            pl.BlockSpec((1, 2, length), lambda j: (j, 0, 0)),
        ],
        out_shape=[
            jax.ShapeDtypeStruct((length, pairs * LANES), low),
            jax.ShapeDtypeStruct((length, pairs * 2 * LANES), low),
            jax.ShapeDtypeStruct((length, pairs * 2 * LANES), low),
            jax.ShapeDtypeStruct((pairs, 2, length), jnp.float32),
        ],
        scratch_shapes=[pltpu.VMEM((2, length, LANES), low)],
        compiler_params=pltpu.CompilerParams(vmem_limit_bytes=ROOM),
        cost_estimate=BRIEF,
        name="attention_forward",
    )(latents, latents, wq, wkv, rope, feat, *tables)


def backward_kernel(
    q_ref, kv_ref, grad_ref, lse_ref, rope_ref, here_ref, low_ref, high_ref,
    dq_ref, dkv_ref, drope_ref, k_ref, do_ref, dk_ref, dv_ref,
):
    length = q_ref.shape[0]
    lane = lax.broadcasted_iota(jnp.int32, (BLOCK, LANES), 1)
    causal = lax.broadcasted_iota(jnp.int32, (BLOCK, BLOCK), 0) <= lax.broadcasted_iota(
        jnp.int32, (BLOCK, BLOCK), 1
    )
    blocks = [slice(start, start + BLOCK) for start in range(0, length, BLOCK)]

    @pl.when(pl.program_id(0) == 0)
    def _():
        drope_ref[...] = jnp.zeros_like(drope_ref)

    for rows in blocks:
        for head in range(2):
            part = slice(head * LANES, (head + 1) * LANES)
            k_ref[head, rows, :] = jnp.where(lane < NOPE, kv_ref[rows, part], rope_ref[rows, :])
            upstream = grad_ref[rows, :].astype(jnp.float32)
            if head == 0:
                upstream = roll_lanes(upstream, VDIM)
            do_ref[head, rows, :] = jnp.where(lane < NOPE, 0.0, upstream).astype(jnp.bfloat16)
    for head in range(2):
        part = slice(head * LANES, (head + 1) * LANES)
        for rows in reversed(blocks):
            last = rows.stop == length
            query = q_ref[rows, part]
            upstream = do_ref[head, rows, :]
            log_total = lse_ref[0, head : head + 1, rows]
            pieces = [rows] + ([slice(0, rows.start)] if rows.start else [])
            held = []
            delta = None
            for piece in pieces:
                scores = product_right(k_ref[head, piece, :], query)
                probability = jnp.exp2(scores * (SCALE * LOG2E) - log_total)
                if piece is rows:
                    probability = jnp.where(causal, probability, 0.0)
                slope = product_right(kv_ref[piece, part], upstream)
                inner = jnp.sum(probability * slope, axis=0, keepdims=True)
                delta = inner if delta is None else delta + inner
                held.append((piece, probability, slope))
            query_grad = None
            for piece, probability, slope in held:
                score_grad = (probability * (slope - delta)).astype(jnp.bfloat16)
                key_grad = product(score_grad, query)
                value_grad = product(probability.astype(jnp.bfloat16), upstream)
                if last:
                    dk_ref[piece, :] = key_grad
                    dv_ref[piece, :] = value_grad
                else:
                    dk_ref[piece, :] += key_grad
                    dv_ref[piece, :] += value_grad
                term = product_left(score_grad, k_ref[head, piece, :])
                query_grad = term if query_grad is None else query_grad + term
            query_grad = query_grad * SCALE
            dq_ref[rows, part] = (
                query_grad * here_ref[rows, :]
                - roll_lanes(query_grad, -ROPE // 2) * low_ref[rows, :]
                - roll_lanes(query_grad, ROPE // 2) * high_ref[rows, :]
            ).astype(jnp.bfloat16)
        for rows in blocks:
            key_grad = dk_ref[rows, :] * SCALE
            dkv_ref[rows, part] = jnp.where(lane < NOPE, key_grad, dv_ref[rows, :]).astype(
                jnp.bfloat16
            )
            drope_ref[rows, :] += jnp.where(
                (lane >= NOPE) & (lane < NOPE + ROPE), key_grad, 0.0
            )


def attention_backward(query, key_value, grad, lse, rope, tables):
    length = query.shape[0]
    pairs = grad.shape[1] // LANES
    whole = lambda width: pl.BlockSpec((length, width), lambda j: (0, 0))
    mine = lambda width: pl.BlockSpec((length, width), lambda j: (0, j))
    low = jnp.bfloat16
    return pl.pallas_call(
        backward_kernel,
        grid=(pairs,),
        in_specs=[
            mine(2 * LANES), mine(2 * LANES), mine(LANES),
            pl.BlockSpec((1, 2, length), lambda j: (j, 0, 0)),
            whole(LANES), whole(LANES), whole(LANES), whole(LANES),
        ],
        out_specs=[mine(2 * LANES), mine(2 * LANES), whole(LANES)],
        out_shape=[
            jax.ShapeDtypeStruct((length, pairs * 2 * LANES), low),
            jax.ShapeDtypeStruct((length, pairs * 2 * LANES), low),
            jax.ShapeDtypeStruct((length, LANES), jnp.float32),
        ],
        scratch_shapes=[
            pltpu.VMEM((2, length, LANES), low),
            pltpu.VMEM((2, length, LANES), low),
            pltpu.VMEM((length, LANES), jnp.float32),
            pltpu.VMEM((length, LANES), jnp.float32),
        ],
        compiler_params=pltpu.CompilerParams(vmem_limit_bytes=ROOM),
        cost_estimate=BRIEF,
        name="attention_backward",
    )(query, key_value, grad, lse, rope, *tables)


def vector(width):
    return pl.BlockSpec((1, width), lambda *_: (0, 0))


def full(array):
    return pl.BlockSpec(array.shape, lambda *_: (0,) * array.ndim)


ANYWHERE = pl.BlockSpec(memory_space=pl.ANY)
SCALARS = pl.BlockSpec(memory_space=pltpu.SMEM)


def assemble_kernel(copies, count, *refs):
    spots_ref, pieces, outs, sems = refs[0], refs[1 : count + 1], refs[count + 1 : -1], refs[-1]
    started = []
    for number, (piece, row, rows, column, width, out, place) in enumerate(copies):
        start = place if isinstance(place, int) else spots_ref[place[0]] * place[1]
        start = pl.multiple_of(start, 16)
        copy = pltpu.make_async_copy(
            pieces[piece].at[pl.ds(row, rows), pl.ds(column, width)],
            outs[out].at[pl.ds(start, rows), :],
            sems.at[number],
        )
        copy.start()
        started.append(copy)
    for copy in started:
        copy.wait()


def assemble(spots, pieces, copies, shapes):
    return pl.pallas_call(
        functools.partial(assemble_kernel, copies, len(pieces)),
        in_specs=[SCALARS] + [ANYWHERE] * len(pieces),
        out_specs=[pl.BlockSpec(shape, lambda: (0, 0)) for shape in shapes],
        out_shape=[jax.ShapeDtypeStruct(shape, jnp.bfloat16) for shape in shapes],
        scratch_shapes=[pltpu.SemaphoreType.DMA((len(copies),))],
        compiler_params=pltpu.CompilerParams(vmem_limit_bytes=ROOM),
        cost_estimate=BRIEF,
        name="assemble",
    )(spots, *pieces)


def collect_kernel(copies, count, team_ref, *refs):
    pieces, (out_ref, sems) = refs[:count], refs[count:]
    width = out_ref.shape[1]
    started = []
    for number, (piece, row, block, team) in enumerate(copies):
        start = pl.multiple_of((block + team_ref[team]) * 16, 16)
        copy = pltpu.make_async_copy(
            pieces[piece].at[pl.ds(row, 16), pl.ds(pieces[piece].shape[1] - width, width)],
            out_ref.at[pl.ds(start, 16), :],
            sems.at[number],
        )
        copy.start()
        started.append(copy)
    for copy in started:
        copy.wait()


def collect_rows(teams, pieces, copies):
    return pl.pallas_call(
        functools.partial(collect_kernel, copies, len(pieces)),
        in_specs=[SCALARS] + [ANYWHERE] * len(pieces),
        out_specs=pl.BlockSpec((16 * len(copies), LANES), lambda: (0, 0)),
        out_shape=jax.ShapeDtypeStruct((16 * len(copies), LANES), jnp.bfloat16),
        scratch_shapes=[pltpu.SemaphoreType.DMA((len(copies),))],
        cost_estimate=BRIEF,
        name="collect",
    )(teams, *pieces)


def project_kernel(copies, count, rank, *refs):
    (team_ref, tokens_ref, gain_ref, gain_query_ref, gain_latent_ref, here_ref, low_ref, high_ref) = refs[:8]
    pieces = refs[8 : 8 + count]
    send_ref, raw_ref, input_ref, weights_ref, sems = refs[8 + count :]
    started = []
    for number, (piece, row, rows, block, team) in enumerate(copies):
        start = block if team is None else (block + team_ref[team]) * rows
        copy = pltpu.make_async_copy(
            pieces[piece].at[pl.ds(row, rows), :],
            weights_ref.at[pl.ds(pl.multiple_of(start, 16), rows), :],
            sems.at[number],
        )
        copy.start()
        started.append(copy)
    values = tokens_ref[...].astype(jnp.float32)
    input_ref[...] = normalize(values, gain_ref[...])[0].astype(jnp.bfloat16)
    for copy in started:
        copy.wait()
    raw = product(input_ref[...], weights_ref[...])
    raw_ref[...] = raw
    send_ref[:, :rank] = normalize(raw[:, :rank], gain_query_ref[...])[0].astype(jnp.bfloat16)
    send_ref[:, rank : rank + KVR] = normalize(
        raw[:, rank : rank + KVR], gain_latent_ref[...]
    )[0].astype(jnp.bfloat16)
    key = raw[:, rank + KVR :]
    send_ref[:, rank + KVR :] = (
        key * here_ref[...]
        + roll_lanes(key, -ROPE // 2) * low_ref[...]
        + roll_lanes(key, ROPE // 2) * high_ref[...]
    ).astype(jnp.bfloat16)


def project(teams, tokens, gains, tables, pieces, copies, rank):
    rows, width = tokens.shape
    out = rank + KVR + LANES
    low = jnp.bfloat16
    shapes = [((rows, out), low), ((rows, out), jnp.float32), ((rows, width), low), ((width, out), low)]
    return pl.pallas_call(
        functools.partial(project_kernel, copies, len(pieces), rank),
        in_specs=[SCALARS, full(tokens)]
        + [full(gain) for gain in gains]
        + [full(table) for table in tables]
        + [ANYWHERE] * len(pieces),
        out_specs=[pl.BlockSpec(shape, lambda: (0, 0)) for shape, _ in shapes],
        out_shape=[jax.ShapeDtypeStruct(*shape) for shape in shapes],
        scratch_shapes=[pltpu.SemaphoreType.DMA((len(copies),))],
        compiler_params=pltpu.CompilerParams(vmem_limit_bytes=ROOM),
        cost_estimate=BRIEF,
        name="project",
    )(teams, tokens, *gains, *tables, *pieces)


def joined(refs):
    if len(refs) == 1:
        return refs[0][...]
    return jnp.concatenate([ref[...] for ref in refs], axis=0)


def single_kernel(left_ref, *refs):
    refs[-1][...] = product(left_ref[...], joined(refs[:-1]))


def gate_kernel(count, last, left_ref, *refs):
    weights = joined(refs[:count])
    slope_ref, activated_ref, grads_ref = refs[count:]
    rows = left_ref.shape[0] // 2

    def work(width):
        for start in (0, rows):
            part = slice(start, start + rows)
            both = product(left_ref[part, :], weights[:, : 2 * width])
            gate, up = both[:, :width], both[:, width:]
            sigmoid = jax.nn.sigmoid(gate)
            swish = gate * sigmoid
            activated_ref[part, :width] = (swish * up).astype(jnp.bfloat16)
            upstream = slope_ref[part, :width]
            slope = sigmoid * (1.0 + gate * (1.0 - sigmoid))
            grads_ref[part, :width] = (upstream * up * slope).astype(jnp.bfloat16)
            grads_ref[part, width : 2 * width] = (upstream * swish).astype(jnp.bfloat16)
            rest = -width % LANES
            if rest:
                activated_ref[part, width : width + rest] = jnp.zeros((rows, rest), jnp.bfloat16)

    step, final = pl.program_id(0), pl.num_programs(0) - 1

    @pl.when(step < final)
    def _():
        work(TILE)

    @pl.when(step == final)
    def _():
        work(last)


TILE = 256


def piece_specs(pieces, width):
    return [pl.BlockSpec((piece.shape[0], width), lambda j: (0, j)) for piece in pieces]


def pair_columns(width):
    full_width = width
    if 2 * (width % TILE) % LANES:
        full_width = -(-width // LANES) * LANES
    return [
        (start, 2 * start, min(TILE, full_width - start), min(TILE, width - start))
        for start in range(0, full_width, TILE)
    ]


def paired_kernel(gate_ref, up_ref, out_ref):
    for start, place, size, real in pair_columns(gate_ref.shape[1]):
        for side, ref in enumerate((gate_ref, up_ref)):
            tile = ref[:, start : start + real]
            if real < size:
                rest = jnp.zeros((tile.shape[0], size - real), tile.dtype)
                tile = jnp.concatenate([tile, rest], axis=1)
            out_ref[:, place + side * size : place + (side + 1) * size] = tile


def paired(gate, up):
    width = sum(2 * size for _, _, size, _ in pair_columns(gate.shape[1]))
    shape = (gate.shape[0], width)
    return pl.pallas_call(
        paired_kernel,
        in_specs=[full(gate), full(up)],
        out_specs=pl.BlockSpec(shape, lambda: (0, 0)),
        out_shape=jax.ShapeDtypeStruct(shape, gate.dtype),
        compiler_params=pltpu.CompilerParams(vmem_limit_bytes=ROOM),
        cost_estimate=lasting(4),
        name="paired",
    )(gate, up)


def unpaired_kernel(own_ref, low_ref, high_ref, weights_ref, gate_ref, up_ref, sums_ref):
    sums = None
    for start, place, size, real in pair_columns(gate_ref.shape[1]):
        for side, out_ref in enumerate((gate_ref, up_ref)):
            part = slice(place + side * size, place + (side + 1) * size)
            total = own_ref[:, part].astype(jnp.float32) + low_ref[:, part].astype(jnp.float32)
            total = total + high_ref[:, part].astype(jnp.float32)
            out_ref[:, start : start + real] = total[:, :real]
            term = jnp.sum(total * weights_ref[:, part].astype(jnp.float32), axis=1, keepdims=True)
            sums = term if sums is None else sums + term
    sums_ref[...] = jnp.broadcast_to(sums, sums_ref.shape)


def unpaired(own, low, high, weights, width):
    rows = weights.shape[0]
    shapes = [(rows, width), (rows, width), (rows, LANES)]
    return pl.pallas_call(
        unpaired_kernel,
        grid=(1,),
        in_specs=[pl.BlockSpec(weights.shape, lambda _: (0, 0))] * 4,
        out_specs=[pl.BlockSpec(shape, lambda _: (0, 0)) for shape in shapes],
        out_shape=[jax.ShapeDtypeStruct(shape, jnp.float32) for shape in shapes],
        compiler_params=pltpu.CompilerParams(vmem_limit_bytes=ROOM),
        cost_estimate=lasting(5),
        name="unpaired",
    )(own, low, high, weights)


def feed_product(left, pieces):
    rows, width = left.shape[0], pieces[0].shape[1]
    return pl.pallas_call(
        single_kernel,
        grid=(pl.cdiv(width, TILE),),
        in_specs=[full(left)] + piece_specs(pieces, TILE),
        out_specs=pl.BlockSpec((rows, TILE), lambda j: (0, j)),
        out_shape=jax.ShapeDtypeStruct((rows, width), jnp.float32),
        compiler_params=pltpu.CompilerParams(vmem_limit_bytes=ROOM),
        cost_estimate=lasting(15),
        name="feed_product",
    )(left, *pieces)


def feed_gate(left, pieces, upstream):
    rows, width = upstream.shape
    pair_width = pieces[0].shape[1]
    column = lambda size: pl.BlockSpec((rows, size), lambda j: (0, j))
    return pl.pallas_call(
        functools.partial(gate_kernel, len(pieces), pair_width // 2 % TILE or TILE),
        grid=(pl.cdiv(width, TILE),),
        in_specs=[full(left)] + piece_specs(pieces, 2 * TILE) + [column(TILE)],
        out_specs=[column(TILE), column(2 * TILE)],
        out_shape=[
            jax.ShapeDtypeStruct((rows, width), jnp.bfloat16),
            jax.ShapeDtypeStruct((rows, pair_width), jnp.bfloat16),
        ],
        compiler_params=pltpu.CompilerParams(vmem_limit_bytes=ROOM),
        cost_estimate=BRIEF,
        name="feed_gate",
    )(left, *pieces, upstream)


def terms_kernel(count, *refs):
    arrays, out_ref = refs[: count + 1], refs[-4]
    left_ref, right_ref, sems = refs[-3:]
    rows = right_ref.shape[0] // count
    places = [left_ref]
    places += [right_ref.at[pl.ds(number * rows, rows), :] for number in range(count)]
    copies = [
        pltpu.make_async_copy(array, place, sems.at[number])
        for number, (array, place) in enumerate(zip(arrays, places))
    ]
    for copy in copies:
        copy.start()
    copies[0].wait()
    ready = 0
    for start in range(0, right_ref.shape[0], TILE):
        while ready * rows < min(start + TILE, right_ref.shape[0]):
            copies[ready + 1].wait()
            ready += 1
        part = slice(start, start + TILE)
        out_ref[:, part] = product_right(left_ref[...], right_ref[part, :]).astype(jnp.bfloat16)


def feed_terms(left, pieces, total, block, earlier=None, cost=lasting(18)):
    arrays = [left, *pieces]
    rows, width = left.shape
    columns = sum(piece.shape[0] for piece in pieces)
    low = jnp.bfloat16
    return pl.pallas_call(
        functools.partial(terms_kernel, len(pieces)),
        grid=(1,),
        in_specs=[ANYWHERE] * (len(arrays) + (earlier is not None)),
        out_specs=pl.BlockSpec((rows, columns), lambda _: (0, block)),
        out_shape=jax.ShapeDtypeStruct((rows, total), low),
        scratch_shapes=[
            pltpu.VMEM((rows, width), low),
            pltpu.VMEM((columns, width), low),
            pltpu.SemaphoreType.DMA((len(arrays),)),
        ],
        input_output_aliases={} if earlier is None else {len(arrays): 0},
        compiler_params=pltpu.CompilerParams(vmem_limit_bytes=ROOM),
        cost_estimate=cost,
        name="feed_terms",
    )(*arrays, *([] if earlier is None else [earlier]))


def latent_back_kernel(
    copies, rank, team_ref, back_ref, raw_ref, input_ref, gain_query_ref, gain_latent_ref,
    here_ref, low_ref, high_ref, *refs,
):
    outs, (grad_ref, held_ref, sems) = refs[:-3], refs[-3:]
    cuts = [(slice(0, rank), gain_query_ref), (slice(rank, rank + KVR), gain_latent_ref)]
    for part, gain_ref in cuts:
        values = raw_ref[:, part]
        inverse = normalize(values, gain_ref[...])[1]
        grad = normalize_back(
            values, inverse, gain_ref[...], back_ref[:, part].astype(jnp.float32)
        )
        grad_ref[:, part] = grad.astype(jnp.bfloat16)
    key = back_ref[:, rank + KVR :].astype(jnp.float32)
    grad_ref[:, rank + KVR :] = (
        key * here_ref[...]
        - roll_lanes(key, -ROPE // 2) * low_ref[...]
        - roll_lanes(key, ROPE // 2) * high_ref[...]
    ).astype(jnp.bfloat16)
    held_ref[...] = product_left(input_ref[...], grad_ref[...]).astype(jnp.bfloat16)
    started = []
    for number, (out, row, rows, block, team) in enumerate(copies):
        start = block if team is None else (block + team_ref[team]) * rows
        copy = pltpu.make_async_copy(
            held_ref.at[pl.ds(pl.multiple_of(start, 16), rows), :],
            outs[out].at[pl.ds(row, rows), :],
            sems.at[number],
        )
        copy.start()
        started.append(copy)
    for copy in started:
        copy.wait()


def latent_back(teams, back, raw, inputs, gains, tables, copies, heights, rank):
    rows, width = inputs.shape
    out = back.shape[1]
    low = jnp.bfloat16
    shapes = [((rows, out), low)]
    arrays = [back, raw, inputs, *gains, *tables]
    results = pl.pallas_call(
        functools.partial(latent_back_kernel, copies, rank),
        in_specs=[SCALARS] + [full(array) for array in arrays],
        out_specs=[ANYWHERE] * len(heights)
        + [pl.BlockSpec(shape, lambda: (0, 0)) for shape, _ in shapes],
        out_shape=[jax.ShapeDtypeStruct((height, out), low) for height in heights]
        + [jax.ShapeDtypeStruct(*shape) for shape in shapes],
        scratch_shapes=[pltpu.VMEM((width, out), low), pltpu.SemaphoreType.DMA((len(copies),))],
        compiler_params=pltpu.CompilerParams(vmem_limit_bytes=ROOM),
        cost_estimate=BRIEF,
        name="latent_back",
    )(teams, *arrays)
    return results[:-1], results[-1]


def head_sums_kernel(
    copies, rank, spots_ref, latents_ref, query_ref, key_value_ref, upstream_ref, heads_ref,
    out_ref, q_ref, kv_ref, o_ref, sems,
):
    q_ref[...] = product_left(latents_ref[:, :rank], query_ref[...]).astype(jnp.bfloat16)
    kv_ref[...] = product_left(latents_ref[:, rank : rank + KVR], key_value_ref[...]).astype(
        jnp.bfloat16
    )
    started = []

    def send(wanted):
        for number, (side, row, rows, place, column) in enumerate(copies):
            if side not in wanted:
                continue
            start = row if isinstance(row, int) else spots_ref[row[0]] * rows
            held = (q_ref, kv_ref, o_ref)[side]
            copy = pltpu.make_async_copy(
                held.at[pl.ds(pl.multiple_of(start, 16), rows), :],
                out_ref.at[pl.ds(place, rows), pl.ds(column, held.shape[1])],
                sems.at[number],
            )
            copy.start()
            started.append(copy)

    send((0, 1))
    o_ref[...] = product_left(upstream_ref[...], heads_ref[...]).astype(jnp.bfloat16)
    send((2,))
    for copy in started:
        copy.wait()


def head_sums(spots, latents, query, key_value, upstream, heads, rank, query_rows, latent_rows, out_rows):
    width, out_width = query.shape[1], heads.shape[1]
    count = spots.shape[0]
    rows = query_rows + latent_rows + out_rows // 2
    copies = []
    for spot in range(count):
        start = spot * rows
        copies.append((0, (spot,), query_rows, start, 0))
        copies.append((1, (spot,), latent_rows, start + query_rows, 0))
        for side in (0, 1):
            copies.append(
                (2, spot * out_rows + side * (out_rows // 2), out_rows // 2,
                 start + query_rows + latent_rows, side * out_width)
            )
    low = jnp.bfloat16
    arrays = [latents, query, key_value, upstream, heads]
    return pl.pallas_call(
        functools.partial(head_sums_kernel, copies, rank),
        in_specs=[SCALARS] + [full(array) for array in arrays],
        out_specs=pl.BlockSpec((count * rows, width), lambda: (0, 0)),
        out_shape=jax.ShapeDtypeStruct((count * rows, width), low),
        scratch_shapes=[
            pltpu.VMEM((rank, width), low),
            pltpu.VMEM((KVR, width), low),
            pltpu.VMEM((upstream.shape[1], out_width), low),
            pltpu.SemaphoreType.DMA((len(copies),)),
        ],
        compiler_params=pltpu.CompilerParams(vmem_limit_bytes=ROOM),
        cost_estimate=lasting(20),
        name="head_sums",
    )(spots, *arrays)


def token_back_kernel(grad_ref, weights_ref, tokens_ref, hidden_ref, gain_ref, out_ref):
    upstream = product_right(grad_ref[...], weights_ref[...])
    values = tokens_ref[...].astype(jnp.float32)
    inverse = normalize(values, gain_ref[...])[1]
    out_ref[...] = hidden_ref[...] + normalize_back(values, inverse, gain_ref[...], upstream)


def token_back(grad, weights, tokens, hidden_grad, gain):
    arrays = [grad, weights, tokens, hidden_grad, gain]
    return pl.pallas_call(
        token_back_kernel,
        in_specs=[full(array) for array in arrays],
        out_specs=full(hidden_grad),
        out_shape=jax.ShapeDtypeStruct(hidden_grad.shape, jnp.float32),
        compiler_params=pltpu.CompilerParams(vmem_limit_bytes=ROOM),
        cost_estimate=lasting(8),
        name="token_back",
    )(*arrays)


def reorder_kernel(spots_ref, in_ref, out_ref):
    width = in_ref.shape[1]
    count = spots_ref.shape[0]
    size = width // count
    window = min(-(-(size + LANES - 1) // LANES) * LANES, width)
    for place in range(count):
        start = spots_ref[place] * size
        base = jnp.minimum(start // LANES * LANES, width - window)
        held = in_ref[:, pl.ds(pl.multiple_of(base, LANES), window)].astype(jnp.float32)
        held = pltpu.roll(held, lax.rem(window - (start - base), window), 1)
        out_ref[:, place * size : (place + 1) * size] = held[:, :size].astype(out_ref.dtype)


def reorder(values, spots):
    return pl.pallas_call(
        reorder_kernel,
        in_specs=[SCALARS, full(values)],
        out_specs=full(values),
        out_shape=jax.ShapeDtypeStruct(values.shape, values.dtype),
        compiler_params=pltpu.CompilerParams(vmem_limit_bytes=ROOM),
        cost_estimate=lasting(4),
        name="reorder",
    )(spots, values)


class Ring:
    def __init__(self, axis):
        self.axis = axis
        self.count = lax.axis_size(axis)
        self.half = self.count // 2
        order = list(range(0, self.count, 2)) + list(range(self.count - 1, 0, -2))
        self.me = lax.axis_index(axis)
        self.spot = self.place(self.me)
        indices = jnp.arange(self.count, dtype=jnp.int32)
        self.ahead = self.owner(indices)
        self.behind = lax.rem(self.place(indices) - self.spot + self.count, self.count)
        self.up = [(order[i], order[(i + 1) % self.count]) for i in range(self.count)]
        self.down = [(b, a) for a, b in self.up]

    def place(self, index):
        return jnp.where(index % 2 == 0, index // 2, self.count - (index + 1) // 2)

    def owner(self, step):
        spot = lax.rem(self.spot + step + self.count, self.count)
        return jnp.where(spot < self.half, 2 * spot, 2 * self.count - 1 - 2 * spot)

    def send_up(self, block):
        return lax.ppermute(block, self.axis, self.up)

    def send_down(self, block):
        return lax.ppermute(block, self.axis, self.down)


class Gather:
    def __init__(self, ring, shard):
        self.ring = ring
        self.rows = shard.shape[0]
        self.low = self.high = shard
        self.blocks = {0: shard}
        self.step = 0

    def advance(self):
        ring = self.ring
        if self.done:
            return
        self.step += 1
        if self.step < ring.half:
            self.low = ring.send_up(self.low)
            self.high = ring.send_down(self.high)
            self.blocks[self.step] = self.high
            self.blocks[ring.count - self.step] = self.low
        else:
            cut = self.rows // 2
            self.low = ring.send_up(self.low[:cut])
            self.high = ring.send_down(self.high[cut:])
            self.blocks[ring.half] = None

    @property
    def done(self):
        return self.step >= self.ring.half

    def finish(self):
        while not self.done:
            self.advance()
        self.blocks[self.ring.half] = jnp.concatenate([self.low, self.high], axis=0)
        return [self.blocks[spot] for spot in range(self.ring.count)]


class Scatter:
    def __init__(self, ring, take, rows):
        self.ring = ring
        self.take = lambda step, start, size: take(step % ring.count, start, size)
        self.rows = rows
        self.step = 0
        self.low = self.high = None

    def add(self, a, b):
        return (a.astype(jnp.float32) + b.astype(jnp.float32)).astype(b.dtype)

    def advance(self):
        ring, rows, cut = self.ring, self.rows, self.rows // 2
        if self.done:
            return
        ahead = ring.half - self.step
        if self.step:
            self.low, self.high = lax.optimization_barrier((self.low, self.high))
        self.step += 1
        if ahead == ring.half:
            low = self.take(ahead, 0, cut)
            high = self.take(ahead, cut, rows - cut)
        elif ahead == ring.half - 1:
            low = self.take(ahead, 0, rows)
            high = self.take(-ahead, 0, rows)
            low = jnp.concatenate([self.add(self.low, low[:cut]), low[cut:]], axis=0)
            high = jnp.concatenate([high[:cut], self.add(self.high, high[cut:])], axis=0)
        else:
            low = self.add(self.low, self.take(ahead, 0, rows))
            high = self.add(self.high, self.take(-ahead, 0, rows))
        self.sent = (low, high)
        self.low = ring.send_up(low)
        self.high = ring.send_down(high)

    @property
    def done(self):
        return self.step >= self.ring.half

    def finish(self):
        while not self.done:
            self.advance()
        own = self.take(0, 0, self.rows).astype(jnp.float32)
        return own + self.low.astype(jnp.float32) + self.high.astype(jnp.float32)


def stacked(ring, grads):
    rows = grads.shape[0] // ring.count

    def take(spot, start, size):
        return lax.slice_in_dim(grads, spot * rows + start, spot * rows + start + size, axis=0)

    return Scatter(ring, take, rows)


def staged(ring, left, right):
    size = left.shape[1] // ring.count
    low, high = ring.count // 4, ring.count // 4 + ring.half
    parts = {}
    held = [right]

    def take(spot, start, rows):
        name = 1 if low <= spot < high else 0 if spot < low else 2
        first = (0, low, high)[name]
        if name not in parts:
            last = (low, high, ring.count)[name]
            columns = lax.slice_in_dim(left, first * size, last * size, axis=1)
            parts[name] = product_left(columns, held[0]).astype(jnp.bfloat16)
        begin = (spot - first) * size + start
        return lax.slice_in_dim(parts[name], begin, begin + rows, axis=0)

    scatter = Scatter(ring, take, size)
    scatter.held = held
    scatter.parts = parts
    return scatter


def delay(scatter, *others):
    scatter.held[0] = follow(scatter.held[0], *others)


def follow(values, *others):
    return lax.optimization_barrier((values, others))[0]


def ends(*streams):
    return [(stream.low, stream.high) for stream in streams]


def hold(stream, *others):
    stream.low, stream.high = follow((stream.low, stream.high), *others)


def swap(values, bit):
    count = lax.axis_size("tensor")
    return lax.ppermute(values, "tensor", [(i, i ^ bit) for i in range(count)])


def pad_heads(weights, heads):
    rows = weights.shape[0]
    width = weights.shape[1] // heads
    padded = jnp.pad(weights.reshape(rows, heads, width), ((0, 0), (0, 0), (0, LANES - width)))
    return padded.reshape(rows, heads * LANES)


def on_device(
    tokens,
    segments,
    positions,
    norm_input,
    norm_query,
    norm_latent,
    norm_hidden,
    query_down,
    latent_down,
    query_up,
    latent_up,
    attention_out,
    gate_weight,
    up_weight,
    down_weight,
    cotangent,
):
    low = jnp.bfloat16
    local_rows = tokens.shape[0]
    shard = lax.axis_index("tensor")
    offset = shard * local_rows
    length = segments.shape[0]
    local_heads = HEADS // lax.axis_size("tensor")
    pairs = local_heads // 2
    rank = query_down.shape[1]
    ring = Ring("fsdp")
    everyone = lax.axis_size("fsdp") * lax.axis_size("tensor")
    teams = lax.axis_size("tensor")
    gains_own = jnp.concatenate([norm_input, norm_hidden, norm_query, norm_latent])
    gain_sizes = [norm_input.shape[0], norm_hidden.shape[0], norm_query.shape[0], norm_latent.shape[0]]
    gain_width = -(-gains_own.shape[0] // LANES) * LANES
    spare = LANES - NOPE - ROPE
    gain_rows = -(-gains_own.shape[0] // spare)
    down_rows = query_down.shape[0]
    down_width = rank + KVR + LANES
    gain_part = jnp.pad(gains_own, (0, gain_rows * spare - gains_own.shape[0]))
    gain_part = jnp.pad(gain_part.reshape(gain_rows, spare), ((0, down_rows - gain_rows), (0, 0)))
    packed = jnp.concatenate(
        [
            query_down,
            latent_down[:, :KVR],
            jnp.zeros((down_rows, NOPE), low),
            latent_down[:, KVR:],
            gain_part,
        ],
        axis=1,
    )
    feed_width = gate_weight.shape[1]
    feed_rows = gate_weight.shape[0]
    feed_pad = -feed_width % LANES
    widen = lambda weights: jnp.pad(weights, ((0, 0), (0, feed_pad)))
    head_width = 2 * pairs * LANES
    query_rows, latent_rows, out_rows = query_up.shape[0], latent_up.shape[0], attention_out.shape[1]
    out_width = attention_out.shape[0]
    out_t = attention_out.T
    mixed = jnp.concatenate(
        [
            pad_heads(query_up, local_heads),
            latent_up,
            jnp.concatenate([out_t[: out_rows // 2], out_t[out_rows // 2 :]], axis=1),
        ],
        axis=0,
    )
    mixed_up = Gather(ring, mixed)
    down_up = Gather(ring, widen(down_weight.T))
    pair_own = paired(gate_weight, up_weight)
    pair_up = Gather(ring, pair_own)

    tokens_ring = reorder(tokens, ring.ahead)
    upstream = reorder(cotangent, ring.ahead)
    here, turn_low, turn_high = rotary_lanes(positions)
    tables = (here, turn_low, turn_high)
    local_tables = [lax.dynamic_slice_in_dim(table, offset, local_rows) for table in tables]
    query_feat, key_feat = segment_lanes(segments)
    key_feat = key_feat.astype(low)
    ahead, behind = ring.ahead, ring.behind
    team_ids = shard ^ jnp.asarray([0, 2, 1, 3], jnp.int32)

    small_up = Gather(ring, jnp.concatenate([packed, swap(packed, 2)], axis=0))
    pieces, copies = [], []

    def collect(block, spot, team):
        for first, piece in ((team, block), (team + 2, swap(block, 1))):
            for part in range(block.shape[0] // down_rows):
                copies.append(
                    (len(pieces), part * down_rows, down_rows, spot * teams, first + part)
                )
            pieces.append(piece)

    collect(small_up.low, 0, 0)
    mixed_up.advance()
    while not small_up.done:
        swapped = pieces[1::2]
        small_up.advance()
        mixed_up.advance()
        if not small_up.done:
            collect(small_up.high, small_up.step, 0)
            collect(small_up.low, ring.count - small_up.step, 0)
            hold(small_up, ends(mixed_up), swapped)
            hold(mixed_up, ends(small_up))
    collect(small_up.low, ring.half, 0)
    collect(small_up.high, ring.half, 1)
    hold(down_up, ends(mixed_up, small_up))
    down_up.advance()
    if down_rows % 16:
        table = [[None] * teams for _ in range(ring.count)]
        for piece, row, _, block, team in copies:
            table[block // teams][team] = pieces[piece][row : row + gain_rows, down_width - spare :]
        table = jnp.stack([part for group in zip(*table) for part in group])
        table = table.reshape(teams, ring.count, gain_rows * spare)
        places = shard ^ jnp.arange(teams, dtype=jnp.int32)
        places = jnp.where(places == 1, 2, jnp.where(places == 2, 1, places))
        table = jnp.take(table, places, axis=0)
    else:
        table = collect_rows(
            team_ids, pieces, [(piece, row, block, team) for piece, row, _, block, team in copies]
        )
        table = table.reshape(ring.count, teams, 16, LANES)[:, :, :gain_rows, LANES - spare :]
        table = jnp.transpose(table, (1, 0, 2, 3)).reshape(teams, ring.count, gain_rows * spare)
    table = table.astype(jnp.float32)
    gain_parts = []
    start = 0
    for number, size in enumerate(gain_sizes):
        part = jnp.transpose(table[:, :, start : start + size], (1, 0, 2))
        if number >= 2:
            part = jnp.take(part, behind, axis=0)
        gain_parts.append(part.reshape(1, -1))
        start += size
    gain_in, gain_hidden, gain_query, gain_latent = gain_parts
    if down_rows % 16:
        whole = jnp.zeros((everyone * down_rows, down_width), low)
        for piece, row, rows, block, team in copies:
            whole = lax.dynamic_update_slice(
                whole, pieces[piece][row : row + rows], ((block + team_ids[team]) * rows, 0)
            )
        pieces, copies = [whole], [(0, 0, whole.shape[0], 0, None)]
    latent_send, latent_raw, attention_input, down_projections = project(
        team_ids, tokens_ring, (gain_in, gain_query, gain_latent), local_tables, pieces, copies, rank
    )
    latent_send = follow(latent_send, ends(down_up))
    latents = lax.all_gather(latent_send, "tensor", axis=0, tiled=True)
    hold(down_up, latent_send)
    down_up.advance()
    latents = follow(latents, ends(down_up))
    hold(pair_up, ends(down_up))
    mixed_blocks = mixed_up.finish()
    if query_rows % 16 or latent_rows % 16 or out_rows % 32:
        mixed_all = jnp.stack([mixed_blocks[0]] * ring.count)
        for spot, block in enumerate(mixed_blocks):
            mixed_all = lax.dynamic_update_slice(mixed_all, block[None], (ring.owner(spot), 0, 0))
        wq = mixed_all[:, :query_rows].reshape(-1, head_width)
        wkv = mixed_all[:, query_rows : query_rows + latent_rows].reshape(-1, head_width)
        outs = [block[query_rows + latent_rows :] for block in mixed_blocks]
        attention_out_t = jnp.concatenate(
            [block[:, side * out_width : (side + 1) * out_width] for block in outs for side in (0, 1)],
            axis=0,
        )
    else:
        copies = []
        for spot in range(ring.count):
            copies.append((spot, 0, query_rows, 0, head_width, 0, (spot, query_rows)))
            copies.append((spot, query_rows, latent_rows, 0, head_width, 1, (spot, latent_rows)))
            for side in (0, 1):
                copies.append(
                    (spot, query_rows + latent_rows, out_rows // 2, side * out_width, out_width, 2,
                     spot * out_rows + side * (out_rows // 2))
                )
        wq, wkv, attention_out_t = assemble(
            ahead,
            mixed_blocks,
            copies,
            [(ring.count * query_rows, head_width), (ring.count * latent_rows, head_width),
             (ring.count * out_rows, out_width)],
        )
    down_up.advance()
    pair_up.advance()
    feed_upstream = follow(RESIDUAL * upstream.astype(jnp.float32), latents).astype(low)
    feed_upstream = lax.all_gather(feed_upstream, "tensor", axis=0, tiled=True)
    rope = latents[:, rank + KVR :] + key_feat
    heads, query_heads, key_value, log_totals = attention_forward(
        latents, wq, wkv, rope, query_feat, tables, pairs
    )
    branch_terms = product_right(heads, attention_out_t).astype(low)
    branch_terms = follow(branch_terms, feed_upstream, ends(pair_up))
    attention_branch = lax.psum_scatter(branch_terms, "tensor", scatter_dimension=0, tiled=True)
    attention_branch = follow(attention_branch, ends(down_up))
    downs = down_up.finish()
    if ring.count > 8:
        downs = [jnp.concatenate(downs, axis=0)]
    activated_grad = feed_product(feed_upstream, downs)
    hidden = tokens_ring.astype(jnp.float32) + RESIDUAL * attention_branch.astype(jnp.float32)
    feed_normed, inverse_hidden = normalize(hidden, gain_hidden)
    pair_up.advance()
    feed_normed = follow(feed_normed.astype(low), ends(pair_up))
    feed_seq = lax.all_gather(feed_normed, "tensor", axis=0, tiled=True)
    hold(pair_up, ends(down_up))
    pair_up.advance()
    hold(pair_up, activated_grad)
    weights = pair_up.finish()
    if ring.count > 8:
        weights = [jnp.concatenate(weights, axis=0)]
    activated, pair_grad = feed_gate(feed_seq, weights, activated_grad)

    grad_down = staged(ring, feed_upstream, activated)
    grad_down.advance()
    grad_pair = staged(ring, feed_seq, follow(pair_grad, grad_down.sent))
    grad_pair.advance()
    hold(grad_down, grad_pair.sent)
    grad_down.advance()
    half = max(len(weights) // 2, 1)
    width = feed_seq.shape[1]
    pair_grad = follow(pair_grad, grad_down.sent)
    terms = feed_terms(pair_grad, weights[:half], width, 0)
    hold(grad_pair, terms)
    grad_pair.advance()
    if len(weights) > half:
        terms = follow(terms, grad_pair.sent)
        terms = feed_terms(pair_grad, weights[half:], width, 1, terms)
    terms = follow(terms, ends(grad_down))
    feed_back = lax.psum_scatter(terms, "tensor", scatter_dimension=0, tiled=True)
    delay(grad_down, terms)
    hold(grad_down, terms)
    grad_down.advance()
    feed_back = follow(feed_back, grad_down.sent)
    delay(grad_pair, grad_down.sent)
    grad_pair.advance()
    grad_pair.take(0, 0, 1), grad_down.take(0, 0, 1)
    feed_back = follow(feed_back, grad_pair.parts[0], grad_down.parts[0])
    hidden_back = normalize_back(
        hidden, inverse_hidden, gain_hidden, feed_back.astype(jnp.float32)
    )
    hidden_grad = upstream.astype(jnp.float32) + hidden_back
    upstream_send = follow((RESIDUAL * hidden_grad).astype(low), grad_pair.sent, ends(grad_down))
    attention_upstream = lax.all_gather(upstream_send, "tensor", axis=0, tiled=True)
    activated = follow(activated, upstream_send)
    feed_branch = feed_terms(activated, downs[:half], width, 0, None, BRIEF)
    if len(downs) > half:
        feed_branch = feed_terms(activated, downs[half:], width, 1, feed_branch, BRIEF)
    attention_upstream = follow(attention_upstream, feed_branch, ends(grad_pair))
    feed_branch = lax.psum_scatter(feed_branch, "tensor", scatter_dimension=0, tiled=True)
    heads_grad = product(attention_upstream, attention_out_t).astype(low)
    grad_pair.advance()
    heads_grad = follow(heads_grad, grad_pair.sent)
    query_raw_grad, key_value_grad, key_rope_grad = attention_backward(
        query_heads, key_value, heads_grad, log_totals, rope, tables
    )
    query_raw_grad, key_value_grad = follow((query_raw_grad, key_value_grad), ends(grad_pair))
    hold(grad_down, query_raw_grad)
    grad_down.advance()
    latent_terms = jnp.concatenate(
        [
            product_right(query_raw_grad, wq),
            product_right(key_value_grad, wkv),
            key_rope_grad,
        ],
        axis=1,
    ).astype(low)
    latent_terms = follow(latent_terms, feed_branch)
    output = hidden + RESIDUAL * feed_branch.astype(jnp.float32)
    latent_grad = lax.psum_scatter(latent_terms, "tensor", scatter_dimension=0, tiled=True)
    upstream_late, query_raw_grad, key_value_grad = follow(
        (attention_upstream, query_raw_grad, key_value_grad), latent_terms, grad_down.sent
    )
    if query_rows % 16 or latent_rows % 16 or out_rows % 32:
        sums = [
            jnp.take(product_left(left, right).astype(low).reshape(ring.count, -1, head_width), ahead, axis=0)
            for left, right in (
                (latents[:, :rank], query_raw_grad),
                (latents[:, rank : rank + KVR], key_value_grad),
            )
        ]
        out_sums = product_left(upstream_late, heads).astype(low)
        out_sums = out_sums.reshape(ring.count, 2, out_rows // 2, out_width)
        sums.append(jnp.concatenate([out_sums[:, 0], out_sums[:, 1]], axis=2))
        mixed_sums = jnp.concatenate(sums, axis=1).reshape(-1, head_width)
    else:
        mixed_sums = head_sums(
            ahead, latents, query_raw_grad, key_value_grad, upstream_late, heads,
            rank, query_rows, latent_rows, out_rows,
        )
    grad_mixed = stacked(ring, mixed_sums)
    grad_mixed.advance()
    latent_grad = follow(latent_grad, grad_mixed.sent, ends(grad_down))
    pair = 2 * down_rows
    height = ring.count * pair
    heights = [height, height]
    copies = [
        (team // 2, spot * pair + (team % 2) * down_rows, down_rows, spot * teams, team)
        for spot in range(ring.count)
        for team in range(teams)
    ]
    aligned = down_rows % 16 == 0
    if not aligned:
        copies, heights = [(0, 0, 2 * height, 0, None)], [2 * height]
    sent, latent_low = latent_back(
        team_ids, latent_grad, latent_raw, attention_input, (gain_query, gain_latent),
        local_tables, copies, heights, rank,
    )
    if not aligned:
        blocks = jnp.take(
            sent[0].reshape(ring.count, teams, down_rows, down_width), team_ids, axis=1
        )
        sent = [blocks[:, :2].reshape(height, -1), blocks[:, 2:].reshape(height, -1)]

    def add_low(a, b):
        return (a.astype(jnp.float32) + b.astype(jnp.float32)).astype(low)

    other_sums = swap(sent[1], 1)
    token_grad = token_back(
        latent_low, down_projections, tokens_ring, hidden_grad, gain_in
    )
    hold(grad_mixed, latent_low)
    grad_mixed.advance()
    other_sums = follow(other_sums, token_grad, grad_mixed.sent)
    grad_small = stacked(ring, add_low(sent[0], other_sums))
    grad_small.advance()
    token_grad = reorder(follow(token_grad, grad_small.take(0, 0, 1)), ring.behind)
    hold(grad_down, ends(grad_small))
    hold(grad_mixed, grad_small.sent)
    grad_mixed.advance()
    hold(grad_small, token_grad)
    grad_small.advance()
    hold(grad_mixed, grad_small.sent)
    hold(grad_pair, ends(grad_small))
    grad_small.advance()
    output = reorder(follow(output.astype(low), grad_small.sent), ring.behind)
    grad_mixed.advance()
    small_own = grad_small.finish()
    small_other = follow(small_own[down_rows:].astype(low), ends(grad_mixed))
    packed_own = small_own[:down_rows] + swap(small_other, 2).astype(jnp.float32)
    rope_from = rank + KVR + NOPE
    lanes = jnp.arange(down_width) < rope_from + ROPE
    grad_gain_input = jnp.sum(
        jnp.where(lanes, packed.astype(jnp.float32) * packed_own, 0.0), axis=1
    ) / norm_input.astype(jnp.float32)
    grad_mixed_own = grad_mixed.finish()
    while not grad_pair.done:
        grad_pair.advance()
    grad_query_own = grad_mixed_own[:query_rows].reshape(query_rows, local_heads, LANES)
    grad_out_own = grad_mixed_own[query_rows + latent_rows :]
    grad_out_own = jnp.concatenate(
        [grad_out_own[:, :out_width], grad_out_own[:, out_width:]], axis=0
    )
    grad_gate_own, grad_up_own, pair_sums = unpaired(
        grad_pair.take(0, 0, feed_rows), grad_pair.low, grad_pair.high, pair_own, feed_width
    )
    row_sums = lambda weights, grads: jnp.sum(weights.astype(jnp.float32) * grads, axis=1)
    head_rows = query_rows + latent_rows
    gain_sums = jnp.concatenate(
        [pair_sums[:, 0], row_sums(mixed[:head_rows], grad_mixed_own[:head_rows])]
    )
    gain_sums = jnp.pad(gain_sums, (0, -gain_sums.shape[0] % LANES))[None]
    gain_sums = gain_sums + swap(gain_sums, 1)
    gain_sums = (gain_sums + swap(gain_sums, 2))[0]
    gain_grads = []
    start = 0
    for gain in (norm_hidden, norm_query, norm_latent):
        size = gain.shape[0]
        own = lax.dynamic_slice_in_dim(gain_sums, start + shard * size, size)
        gain_grads.append(own / gain.astype(jnp.float32))
        start += size * teams
    return (
        output,
        token_grad,
        grad_gain_input,
        gain_grads[1],
        gain_grads[2],
        gain_grads[0],
        packed_own[:, :rank],
        jnp.concatenate(
            [packed_own[:, rank : rank + KVR], packed_own[:, rope_from : rope_from + ROPE]],
            axis=1,
        ),
        grad_query_own[:, :, : NOPE + ROPE].reshape(query_rows, -1),
        grad_mixed_own[query_rows : query_rows + latent_rows],
        grad_out_own.T,
        grad_gate_own,
        grad_up_own,
        grad_down.finish()[:, :feed_width].T,
    )


def solution(mesh):
    return jax.shard_map(
        on_device,
        mesh=mesh,
        in_specs=(
            P(("fsdp", "tensor"), None),
            P("fsdp"),
            P("fsdp"),
            P(("fsdp", "tensor")),
            P(("fsdp", "tensor")),
            P(("fsdp", "tensor")),
            P(("fsdp", "tensor")),
            P(("fsdp", "tensor"), None),
            P(("fsdp", "tensor"), None),
            P("fsdp", "tensor"),
            P("fsdp", "tensor"),
            P("tensor", "fsdp"),
            P("fsdp", "tensor"),
            P("fsdp", "tensor"),
            P("tensor", "fsdp"),
            P(("fsdp", "tensor"), None),
        ),
        out_specs=(
            P(("fsdp", "tensor"), None),
            P(("fsdp", "tensor"), None),
            P(("fsdp", "tensor")),
            P(("fsdp", "tensor")),
            P(("fsdp", "tensor")),
            P(("fsdp", "tensor")),
            P(("fsdp", "tensor"), None),
            P(("fsdp", "tensor"), None),
            P("fsdp", "tensor"),
            P("fsdp", "tensor"),
            P("tensor", "fsdp"),
            P("fsdp", "tensor"),
            P("fsdp", "tensor"),
            P("tensor", "fsdp"),
        ),
        check_vma=False,
    )
```

```python
import functools
import math

import jax
import jax.numpy as jnp
from jax import lax
from jax.experimental import pallas as pl
from jax.experimental.pallas import tpu as pltpu
from jax.sharding import PartitionSpec as P

HEADS = 40
NOPE = 64
ROPE = 32
VDIM = 64
KVR = 256
LANES = 128
BLOCK = 256


EPSILON = 1e-05
RESIDUAL = 1.4 / math.sqrt(62.0)
NEGATIVE = -1e30
APART = -(2.0**96)
SCALE = 1.0 / math.sqrt(NOPE + ROPE)
LOG2E = math.log2(math.e)
ROOM = 56 * 1024 * 1024
BRIEF = pl.CostEstimate(flops=1, bytes_accessed=1, transcendentals=0)


def lasting(microseconds):
    return pl.CostEstimate(flops=1, bytes_accessed=microseconds * 3 * 10**6, transcendentals=0)


def normalize(values, gain):
    inverse = lax.rsqrt(jnp.mean(values * values, axis=-1, keepdims=True) + EPSILON)
    return (values * inverse * gain, inverse)


def normalize_back(values, inverse, gain, upstream):
    scaled = upstream * gain
    inner = jnp.mean(scaled * values, axis=-1, keepdims=True)
    return inverse * scaled - values * (inverse * inverse * inverse) * inner


def product(left, right):
    return jnp.dot(left, right, preferred_element_type=jnp.float32)


def product_left(left, right):
    return lax.dot_general(
        left, right, (((0,), (0,)), ((), ())), preferred_element_type=jnp.float32
    )


def product_right(left, right):
    return lax.dot_general(
        left, right, (((1,), (1,)), ((), ())), preferred_element_type=jnp.float32
    )


def rotary_lanes(positions):
    lane = jnp.arange(LANES, dtype=jnp.int32)
    steps = ((lane - NOPE) % (ROPE // 2)).astype(jnp.float32)
    frequency = jnp.exp(steps * (-2.0 * math.log(10000.0) / ROPE))
    angles = positions.astype(jnp.float32)[:, None] * frequency[None, :]
    first = ((lane >= NOPE) & (lane < NOPE + ROPE // 2))[None, :]
    second = ((lane >= NOPE + ROPE // 2) & (lane < NOPE + ROPE))[None, :]
    cosine = jnp.cos(angles)
    sine = jnp.sin(angles)
    here = jnp.where((lane < NOPE)[None, :], 1.0, jnp.where(first | second, cosine, 0.0))
    return (here, jnp.where(first, -sine, 0.0), jnp.where(second, sine, 0.0))


def segment_lanes(segment_ids):
    lane = jnp.arange(LANES, dtype=jnp.int32) - (NOPE + ROPE)
    same = lane[None, :] == segment_ids[:, None]
    used = ((lane >= 0) & (lane < 4))[None, :]
    query = jnp.where(used & same, 1.0, 0.0)
    key = jnp.where(used & ~same, APART, 0.0)
    return (query, key)


def roll_lanes(values, amount):
    return pltpu.roll(values, amount % LANES, 1)


def forward_kernel(
    xq_ref, lat_ref, wq_ref, wkv_ref, rope_ref, feat_ref, here_ref, low_ref, high_ref,
    out_ref, q_ref, kv_ref, lse_ref, k_ref,
):
    length = xq_ref.shape[0]
    lane = lax.broadcasted_iota(jnp.int32, (BLOCK, LANES), 1)
    causal = lax.broadcasted_iota(jnp.int32, (BLOCK, BLOCK), 1) <= lax.broadcasted_iota(
        jnp.int32, (BLOCK, BLOCK), 0
    )
    blocks = [slice(start, start + BLOCK) for start in range(0, length, BLOCK)]
    for rows in blocks:
        q_raw = product(xq_ref[rows, :], wq_ref[...])
        kv_ref[rows, :] = product(lat_ref[rows, :], wkv_ref[...]).astype(jnp.bfloat16)
        for head in range(2):
            part = slice(head * LANES, (head + 1) * LANES)
            raw = q_raw[:, part]
            turned = (
                raw * here_ref[rows, :]
                + roll_lanes(raw, -ROPE // 2) * low_ref[rows, :]
                + roll_lanes(raw, ROPE // 2) * high_ref[rows, :]
                + feat_ref[rows, :]
            )
            q_ref[rows, part] = turned.astype(jnp.bfloat16)
            k_ref[head, rows, :] = jnp.where(lane < NOPE, kv_ref[rows, part], rope_ref[rows, :])
    for rows in blocks:
        results = []
        for head in range(2):
            part = slice(head * LANES, (head + 1) * LANES)
            query = q_ref[rows, part]
            near = product_right(query, k_ref[head, rows, :])
            near = jnp.where(causal, near, NEGATIVE)
            top = jnp.max(near, axis=1, keepdims=True)
            if rows.start:
                far = product_right(query, k_ref[head, : rows.start, :])
                top = jnp.maximum(top, jnp.max(far, axis=1, keepdims=True))
            weights = jnp.exp2((near - top) * (SCALE * LOG2E))
            total = jnp.sum(weights, axis=1, keepdims=True)
            result = product(weights.astype(jnp.bfloat16), kv_ref[rows, part])
            if rows.start:
                weights = jnp.exp2((far - top) * (SCALE * LOG2E))
                total = total + jnp.sum(weights, axis=1, keepdims=True)
                result = result + product(
                    weights.astype(jnp.bfloat16), kv_ref[: rows.start, part]
                )
            results.append(result / total)
            log_total = top * (SCALE * LOG2E) + jnp.log2(total)
            lse_ref[0, head : head + 1, rows] = jnp.transpose(
                jnp.broadcast_to(log_total, (BLOCK, LANES))
            )[0:1, :]
        out_ref[rows, :] = jnp.where(
            lane < VDIM, roll_lanes(results[0], VDIM), results[1]
        ).astype(jnp.bfloat16)


def attention_forward(latents, wq, wkv, rope, feat, tables, pairs):
    length = latents.shape[0]
    rank = wq.shape[0]
    whole = lambda width, at=0: pl.BlockSpec((length, width), lambda j: (0, at))
    mine = lambda width: pl.BlockSpec((length, width), lambda j: (0, j))
    tall = lambda rows: pl.BlockSpec((rows, 2 * LANES), lambda j: (0, j))
    low = jnp.bfloat16
    return pl.pallas_call(
        forward_kernel,
        grid=(pairs,),
        in_specs=[
            whole(rank), whole(KVR, rank // KVR), tall(rank), tall(KVR),
            whole(LANES), whole(LANES), whole(LANES), whole(LANES), whole(LANES),
        ],
        out_specs=[
            mine(LANES), mine(2 * LANES), mine(2 * LANES),
            pl.BlockSpec((1, 2, length), lambda j: (j, 0, 0)),
        ],
        out_shape=[
            jax.ShapeDtypeStruct((length, pairs * LANES), low),
            jax.ShapeDtypeStruct((length, pairs * 2 * LANES), low),
            jax.ShapeDtypeStruct((length, pairs * 2 * LANES), low),
            jax.ShapeDtypeStruct((pairs, 2, length), jnp.float32),
        ],
        scratch_shapes=[pltpu.VMEM((2, length, LANES), low)],
        compiler_params=pltpu.CompilerParams(vmem_limit_bytes=ROOM),
        cost_estimate=lasting(23),
        name="attention_forward",
    )(latents, latents, wq, wkv, rope, feat, *tables)


def backward_kernel(
    q_ref, kv_ref, grad_ref, lse_ref, rope_ref, here_ref, low_ref, high_ref,
    dq_ref, dkv_ref, drope_ref, k_ref, do_ref, dk_ref, dv_ref,
):
    length = q_ref.shape[0]
    lane = lax.broadcasted_iota(jnp.int32, (BLOCK, LANES), 1)
    causal = lax.broadcasted_iota(jnp.int32, (BLOCK, BLOCK), 0) <= lax.broadcasted_iota(
        jnp.int32, (BLOCK, BLOCK), 1
    )
    blocks = [slice(start, start + BLOCK) for start in range(0, length, BLOCK)]

    @pl.when(pl.program_id(0) == 0)
    def _():
        drope_ref[...] = jnp.zeros_like(drope_ref)

    for rows in blocks:
        for head in range(2):
            part = slice(head * LANES, (head + 1) * LANES)
            k_ref[head, rows, :] = jnp.where(lane < NOPE, kv_ref[rows, part], rope_ref[rows, :])
            upstream = grad_ref[rows, :].astype(jnp.float32)
            if head == 0:
                upstream = roll_lanes(upstream, VDIM)
            do_ref[head, rows, :] = jnp.where(lane < NOPE, 0.0, upstream).astype(jnp.bfloat16)
    for head in range(2):
        part = slice(head * LANES, (head + 1) * LANES)
        for rows in reversed(blocks):
            last = rows.stop == length
            query = q_ref[rows, part]
            upstream = do_ref[head, rows, :]
            log_total = lse_ref[0, head : head + 1, rows]
            pieces = [rows] + ([slice(0, rows.start)] if rows.start else [])
            held = []
            delta = None
            for piece in pieces:
                scores = product_right(k_ref[head, piece, :], query)
                probability = jnp.exp2(scores * (SCALE * LOG2E) - log_total)
                if piece is rows:
                    probability = jnp.where(causal, probability, 0.0)
                slope = product_right(kv_ref[piece, part], upstream)
                inner = jnp.sum(probability * slope, axis=0, keepdims=True)
                delta = inner if delta is None else delta + inner
                held.append((piece, probability, slope))
            query_grad = None
            for piece, probability, slope in held:
                score_grad = (probability * (slope - delta)).astype(jnp.bfloat16)
                key_grad = product(score_grad, query)
                value_grad = product(probability.astype(jnp.bfloat16), upstream)
                if last:
                    dk_ref[piece, :] = key_grad
                    dv_ref[piece, :] = value_grad
                else:
                    dk_ref[piece, :] += key_grad
                    dv_ref[piece, :] += value_grad
                term = product_left(score_grad, k_ref[head, piece, :])
                query_grad = term if query_grad is None else query_grad + term
            query_grad = query_grad * SCALE
            dq_ref[rows, part] = (
                query_grad * here_ref[rows, :]
                - roll_lanes(query_grad, -ROPE // 2) * low_ref[rows, :]
                - roll_lanes(query_grad, ROPE // 2) * high_ref[rows, :]
            ).astype(jnp.bfloat16)
        for rows in blocks:
            key_grad = dk_ref[rows, :] * SCALE
            dkv_ref[rows, part] = jnp.where(lane < NOPE, key_grad, dv_ref[rows, :]).astype(
                jnp.bfloat16
            )
            drope_ref[rows, :] += jnp.where(
                (lane >= NOPE) & (lane < NOPE + ROPE), key_grad, 0.0
            )


def attention_backward(query, key_value, grad, lse, rope, tables):
    length = query.shape[0]
    pairs = grad.shape[1] // LANES
    whole = lambda width: pl.BlockSpec((length, width), lambda j: (0, 0))
    mine = lambda width: pl.BlockSpec((length, width), lambda j: (0, j))
    low = jnp.bfloat16
    return pl.pallas_call(
        backward_kernel,
        grid=(pairs,),
        in_specs=[
            mine(2 * LANES), mine(2 * LANES), mine(LANES),
            pl.BlockSpec((1, 2, length), lambda j: (j, 0, 0)),
            whole(LANES), whole(LANES), whole(LANES), whole(LANES),
        ],
        out_specs=[mine(2 * LANES), mine(2 * LANES), whole(LANES)],
        out_shape=[
            jax.ShapeDtypeStruct((length, pairs * 2 * LANES), low),
            jax.ShapeDtypeStruct((length, pairs * 2 * LANES), low),
            jax.ShapeDtypeStruct((length, LANES), jnp.float32),
        ],
        scratch_shapes=[
            pltpu.VMEM((2, length, LANES), low),
            pltpu.VMEM((2, length, LANES), low),
            pltpu.VMEM((length, LANES), jnp.float32),
            pltpu.VMEM((length, LANES), jnp.float32),
        ],
        compiler_params=pltpu.CompilerParams(vmem_limit_bytes=ROOM),
        cost_estimate=lasting(31),
        name="attention_backward",
    )(query, key_value, grad, lse, rope, *tables)


def vector(width):
    return pl.BlockSpec((1, width), lambda *_: (0, 0))


def full(array):
    return pl.BlockSpec(array.shape, lambda *_: (0,) * array.ndim)


ANYWHERE = pl.BlockSpec(memory_space=pl.ANY)
SCALARS = pl.BlockSpec(memory_space=pltpu.SMEM)


def assemble_kernel(copies, count, *refs):
    spots_ref, pieces, outs, sems = refs[0], refs[1 : count + 1], refs[count + 1 : -1], refs[-1]
    started = []
    for number, (piece, row, rows, column, width, out, place) in enumerate(copies):
        start = place if isinstance(place, int) else spots_ref[place[0]] * place[1]
        start = pl.multiple_of(start, 16)
        copy = pltpu.make_async_copy(
            pieces[piece].at[pl.ds(row, rows), pl.ds(column, width)],
            outs[out].at[pl.ds(start, rows), :],
            sems.at[number],
        )
        copy.start()
        started.append(copy)
    for copy in started:
        copy.wait()


def assemble(spots, pieces, copies, shapes):
    return pl.pallas_call(
        functools.partial(assemble_kernel, copies, len(pieces)),
        in_specs=[SCALARS] + [ANYWHERE] * len(pieces),
        out_specs=[pl.BlockSpec(shape, lambda: (0, 0)) for shape in shapes],
        out_shape=[jax.ShapeDtypeStruct(shape, jnp.bfloat16) for shape in shapes],
        scratch_shapes=[pltpu.SemaphoreType.DMA((len(copies),))],
        compiler_params=pltpu.CompilerParams(vmem_limit_bytes=ROOM),
        cost_estimate=lasting(6),
        name="assemble",
    )(spots, *pieces)


def collect_kernel(copies, count, team_ref, *refs):
    pieces, (out_ref, sems) = refs[:count], refs[count:]
    width = out_ref.shape[1]
    started = []
    for number, (piece, row, block, team) in enumerate(copies):
        start = pl.multiple_of((block + team_ref[team]) * 16, 16)
        copy = pltpu.make_async_copy(
            pieces[piece].at[pl.ds(row, 16), pl.ds(pieces[piece].shape[1] - width, width)],
            out_ref.at[pl.ds(start, 16), :],
            sems.at[number],
        )
        copy.start()
        started.append(copy)
    for copy in started:
        copy.wait()


def collect_rows(teams, pieces, copies):
    return pl.pallas_call(
        functools.partial(collect_kernel, copies, len(pieces)),
        in_specs=[SCALARS] + [ANYWHERE] * len(pieces),
        out_specs=pl.BlockSpec((16 * len(copies), LANES), lambda: (0, 0)),
        out_shape=jax.ShapeDtypeStruct((16 * len(copies), LANES), jnp.bfloat16),
        scratch_shapes=[pltpu.SemaphoreType.DMA((len(copies),))],
        cost_estimate=lasting(3),
        name="collect",
    )(teams, *pieces)


def project_kernel(copies, count, rank, *refs):
    (team_ref, tokens_ref, gain_ref, gain_query_ref, gain_latent_ref, here_ref, low_ref, high_ref) = refs[:8]
    pieces = refs[8 : 8 + count]
    send_ref, raw_ref, input_ref, weights_ref, sems = refs[8 + count :]
    started = []
    for number, (piece, row, rows, block, team) in enumerate(copies):
        start = block if team is None else (block + team_ref[team]) * rows
        copy = pltpu.make_async_copy(
            pieces[piece].at[pl.ds(row, rows), :],
            weights_ref.at[pl.ds(pl.multiple_of(start, 16), rows), :],
            sems.at[number],
        )
        copy.start()
        started.append(copy)
    values = tokens_ref[...].astype(jnp.float32)
    input_ref[...] = normalize(values, gain_ref[...])[0].astype(jnp.bfloat16)
    for copy in started:
        copy.wait()
    raw = product(input_ref[...], weights_ref[...])
    raw_ref[...] = raw
    send_ref[:, :rank] = normalize(raw[:, :rank], gain_query_ref[...])[0].astype(jnp.bfloat16)
    send_ref[:, rank : rank + KVR] = normalize(
        raw[:, rank : rank + KVR], gain_latent_ref[...]
    )[0].astype(jnp.bfloat16)
    key = raw[:, rank + KVR :]
    send_ref[:, rank + KVR :] = (
        key * here_ref[...]
        + roll_lanes(key, -ROPE // 2) * low_ref[...]
        + roll_lanes(key, ROPE // 2) * high_ref[...]
    ).astype(jnp.bfloat16)


def project(teams, tokens, gains, tables, pieces, copies, rank):
    rows, width = tokens.shape
    out = rank + KVR + LANES
    low = jnp.bfloat16
    shapes = [((rows, out), low), ((rows, out), jnp.float32), ((rows, width), low), ((width, out), low)]
    return pl.pallas_call(
        functools.partial(project_kernel, copies, len(pieces), rank),
        in_specs=[SCALARS, full(tokens)]
        + [full(gain) for gain in gains]
        + [full(table) for table in tables]
        + [ANYWHERE] * len(pieces),
        out_specs=[pl.BlockSpec(shape, lambda: (0, 0)) for shape, _ in shapes],
        out_shape=[jax.ShapeDtypeStruct(*shape) for shape in shapes],
        scratch_shapes=[pltpu.SemaphoreType.DMA((len(copies),))],
        compiler_params=pltpu.CompilerParams(vmem_limit_bytes=ROOM),
        cost_estimate=lasting(10),
        name="project",
    )(teams, tokens, *gains, *tables, *pieces)


def joined(refs):
    if len(refs) == 1:
        return refs[0][...]
    return jnp.concatenate([ref[...] for ref in refs], axis=0)


def single_kernel(left_ref, *refs):
    refs[-1][...] = product(left_ref[...], joined(refs[:-1]))


def gate_kernel(count, last, left_ref, *refs):
    weights = joined(refs[:count])
    slope_ref, activated_ref, grads_ref = refs[count:]
    rows = left_ref.shape[0] // 2

    def work(width):
        for start in (0, rows):
            part = slice(start, start + rows)
            both = product(left_ref[part, :], weights[:, : 2 * width])
            gate, up = both[:, :width], both[:, width:]
            sigmoid = jax.nn.sigmoid(gate)
            swish = gate * sigmoid
            activated_ref[part, :width] = (swish * up).astype(jnp.bfloat16)
            upstream = slope_ref[part, :width]
            slope = sigmoid * (1.0 + gate * (1.0 - sigmoid))
            grads_ref[part, :width] = (upstream * up * slope).astype(jnp.bfloat16)
            grads_ref[part, width : 2 * width] = (upstream * swish).astype(jnp.bfloat16)
            rest = -width % LANES
            if rest:
                activated_ref[part, width : width + rest] = jnp.zeros((rows, rest), jnp.bfloat16)

    step, final = pl.program_id(0), pl.num_programs(0) - 1

    @pl.when(step < final)
    def _():
        work(TILE)

    @pl.when(step == final)
    def _():
        work(last)


TILE = 256


def piece_specs(pieces, width):
    return [pl.BlockSpec((piece.shape[0], width), lambda j: (0, j)) for piece in pieces]


def pair_columns(width):
    full_width = width
    if 2 * (width % TILE) % LANES:
        full_width = -(-width // LANES) * LANES
    return [
        (start, 2 * start, min(TILE, full_width - start), min(TILE, width - start))
        for start in range(0, full_width, TILE)
    ]


def paired_kernel(gate_ref, up_ref, out_ref):
    for start, place, size, real in pair_columns(gate_ref.shape[1]):
        for side, ref in enumerate((gate_ref, up_ref)):
            tile = ref[:, start : start + real]
            if real < size:
                rest = jnp.zeros((tile.shape[0], size - real), tile.dtype)
                tile = jnp.concatenate([tile, rest], axis=1)
            out_ref[:, place + side * size : place + (side + 1) * size] = tile


def paired(gate, up):
    width = sum(2 * size for _, _, size, _ in pair_columns(gate.shape[1]))
    shape = (gate.shape[0], width)
    return pl.pallas_call(
        paired_kernel,
        in_specs=[full(gate), full(up)],
        out_specs=pl.BlockSpec(shape, lambda: (0, 0)),
        out_shape=jax.ShapeDtypeStruct(shape, gate.dtype),
        compiler_params=pltpu.CompilerParams(vmem_limit_bytes=ROOM),
        cost_estimate=lasting(4),
        name="paired",
    )(gate, up)


def unpaired_kernel(own_ref, low_ref, high_ref, weights_ref, gate_ref, up_ref, sums_ref):
    sums = None
    for start, place, size, real in pair_columns(gate_ref.shape[1]):
        for side, out_ref in enumerate((gate_ref, up_ref)):
            part = slice(place + side * size, place + (side + 1) * size)
            total = own_ref[:, part].astype(jnp.float32) + low_ref[:, part].astype(jnp.float32)
            total = total + high_ref[:, part].astype(jnp.float32)
            out_ref[:, start : start + real] = total[:, :real]
            term = jnp.sum(total * weights_ref[:, part].astype(jnp.float32), axis=1, keepdims=True)
            sums = term if sums is None else sums + term
    sums_ref[...] = jnp.broadcast_to(sums, sums_ref.shape)


def unpaired(own, low, high, weights, width):
    rows = weights.shape[0]
    shapes = [(rows, width), (rows, width), (rows, LANES)]
    return pl.pallas_call(
        unpaired_kernel,
        grid=(1,),
        in_specs=[pl.BlockSpec(weights.shape, lambda _: (0, 0))] * 4,
        out_specs=[pl.BlockSpec(shape, lambda _: (0, 0)) for shape in shapes],
        out_shape=[jax.ShapeDtypeStruct(shape, jnp.float32) for shape in shapes],
        compiler_params=pltpu.CompilerParams(vmem_limit_bytes=ROOM),
        cost_estimate=lasting(5),
        name="unpaired",
    )(own, low, high, weights)


def feed_product(left, pieces):
    rows, width = left.shape[0], pieces[0].shape[1]
    return pl.pallas_call(
        single_kernel,
        grid=(pl.cdiv(width, TILE),),
        in_specs=[full(left)] + piece_specs(pieces, TILE),
        out_specs=pl.BlockSpec((rows, TILE), lambda j: (0, j)),
        out_shape=jax.ShapeDtypeStruct((rows, width), jnp.float32),
        compiler_params=pltpu.CompilerParams(vmem_limit_bytes=ROOM),
        cost_estimate=lasting(15),
        name="feed_product",
    )(left, *pieces)


def feed_gate(left, pieces, upstream):
    rows, width = upstream.shape
    pair_width = pieces[0].shape[1]
    column = lambda size: pl.BlockSpec((rows, size), lambda j: (0, j))
    return pl.pallas_call(
        functools.partial(gate_kernel, len(pieces), pair_width // 2 % TILE or TILE),
        grid=(pl.cdiv(width, TILE),),
        in_specs=[full(left)] + piece_specs(pieces, 2 * TILE) + [column(TILE)],
        out_specs=[column(TILE), column(2 * TILE)],
        out_shape=[
            jax.ShapeDtypeStruct((rows, width), jnp.bfloat16),
            jax.ShapeDtypeStruct((rows, pair_width), jnp.bfloat16),
        ],
        compiler_params=pltpu.CompilerParams(vmem_limit_bytes=ROOM),
        cost_estimate=lasting(26),
        name="feed_gate",
    )(left, *pieces, upstream)


def terms_kernel(count, *refs):
    arrays, out_ref = refs[: count + 1], refs[-4]
    left_ref, right_ref, sems = refs[-3:]
    rows = right_ref.shape[0] // count
    places = [left_ref]
    places += [right_ref.at[pl.ds(number * rows, rows), :] for number in range(count)]
    copies = [
        pltpu.make_async_copy(array, place, sems.at[number])
        for number, (array, place) in enumerate(zip(arrays, places))
    ]
    for copy in copies:
        copy.start()
    copies[0].wait()
    ready = 0
    for start in range(0, right_ref.shape[0], TILE):
        while ready * rows < min(start + TILE, right_ref.shape[0]):
            copies[ready + 1].wait()
            ready += 1
        part = slice(start, start + TILE)
        out_ref[:, part] = product_right(left_ref[...], right_ref[part, :]).astype(jnp.bfloat16)


def feed_terms(left, pieces, total, block, earlier=None, cost=lasting(18)):
    arrays = [left, *pieces]
    rows, width = left.shape
    columns = sum(piece.shape[0] for piece in pieces)
    low = jnp.bfloat16
    return pl.pallas_call(
        functools.partial(terms_kernel, len(pieces)),
        grid=(1,),
        in_specs=[ANYWHERE] * (len(arrays) + (earlier is not None)),
        out_specs=pl.BlockSpec((rows, columns), lambda _: (0, block)),
        out_shape=jax.ShapeDtypeStruct((rows, total), low),
        scratch_shapes=[
            pltpu.VMEM((rows, width), low),
            pltpu.VMEM((columns, width), low),
            pltpu.SemaphoreType.DMA((len(arrays),)),
        ],
        input_output_aliases={} if earlier is None else {len(arrays): 0},
        compiler_params=pltpu.CompilerParams(vmem_limit_bytes=ROOM),
        cost_estimate=cost,
        name="feed_terms",
    )(*arrays, *([] if earlier is None else [earlier]))


def latent_back_kernel(
    copies, rank, team_ref, back_ref, raw_ref, input_ref, gain_query_ref, gain_latent_ref,
    here_ref, low_ref, high_ref, *refs,
):
    outs, (grad_ref, held_ref, sems) = refs[:-3], refs[-3:]
    cuts = [(slice(0, rank), gain_query_ref), (slice(rank, rank + KVR), gain_latent_ref)]
    for part, gain_ref in cuts:
        values = raw_ref[:, part]
        inverse = normalize(values, gain_ref[...])[1]
        grad = normalize_back(
            values, inverse, gain_ref[...], back_ref[:, part].astype(jnp.float32)
        )
        grad_ref[:, part] = grad.astype(jnp.bfloat16)
    key = back_ref[:, rank + KVR :].astype(jnp.float32)
    grad_ref[:, rank + KVR :] = (
        key * here_ref[...]
        - roll_lanes(key, -ROPE // 2) * low_ref[...]
        - roll_lanes(key, ROPE // 2) * high_ref[...]
    ).astype(jnp.bfloat16)
    held_ref[...] = product_left(input_ref[...], grad_ref[...]).astype(jnp.bfloat16)
    started = []
    for number, (out, row, rows, block, team) in enumerate(copies):
        start = block if team is None else (block + team_ref[team]) * rows
        copy = pltpu.make_async_copy(
            held_ref.at[pl.ds(pl.multiple_of(start, 16), rows), :],
            outs[out].at[pl.ds(row, rows), :],
            sems.at[number],
        )
        copy.start()
        started.append(copy)
    for copy in started:
        copy.wait()


def latent_back(teams, back, raw, inputs, gains, tables, copies, heights, rank):
    rows, width = inputs.shape
    out = back.shape[1]
    low = jnp.bfloat16
    shapes = [((rows, out), low)]
    arrays = [back, raw, inputs, *gains, *tables]
    results = pl.pallas_call(
        functools.partial(latent_back_kernel, copies, rank),
        in_specs=[SCALARS] + [full(array) for array in arrays],
        out_specs=[ANYWHERE] * len(heights)
        + [pl.BlockSpec(shape, lambda: (0, 0)) for shape, _ in shapes],
        out_shape=[jax.ShapeDtypeStruct((height, out), low) for height in heights]
        + [jax.ShapeDtypeStruct(*shape) for shape in shapes],
        scratch_shapes=[pltpu.VMEM((width, out), low), pltpu.SemaphoreType.DMA((len(copies),))],
        compiler_params=pltpu.CompilerParams(vmem_limit_bytes=ROOM),
        cost_estimate=lasting(8),
        name="latent_back",
    )(teams, *arrays)
    return results[:-1], results[-1]


def head_sums_kernel(
    copies, rank, spots_ref, latents_ref, query_ref, key_value_ref, upstream_ref, heads_ref,
    out_ref, q_ref, kv_ref, o_ref, sems,
):
    q_ref[...] = product_left(latents_ref[:, :rank], query_ref[...]).astype(jnp.bfloat16)
    kv_ref[...] = product_left(latents_ref[:, rank : rank + KVR], key_value_ref[...]).astype(
        jnp.bfloat16
    )
    started = []

    def send(wanted):
        for number, (side, row, rows, place, column) in enumerate(copies):
            if side not in wanted:
                continue
            start = row if isinstance(row, int) else spots_ref[row[0]] * rows
            held = (q_ref, kv_ref, o_ref)[side]
            copy = pltpu.make_async_copy(
                held.at[pl.ds(pl.multiple_of(start, 16), rows), :],
                out_ref.at[pl.ds(place, rows), pl.ds(column, held.shape[1])],
                sems.at[number],
            )
            copy.start()
            started.append(copy)

    send((0, 1))
    o_ref[...] = product_left(upstream_ref[...], heads_ref[...]).astype(jnp.bfloat16)
    send((2,))
    for copy in started:
        copy.wait()


def head_sums(spots, latents, query, key_value, upstream, heads, rank, query_rows, latent_rows, out_rows):
    width, out_width = query.shape[1], heads.shape[1]
    count = spots.shape[0]
    rows = query_rows + latent_rows + out_rows // 2
    copies = []
    for spot in range(count):
        start = spot * rows
        copies.append((0, (spot,), query_rows, start, 0))
        copies.append((1, (spot,), latent_rows, start + query_rows, 0))
        for side in (0, 1):
            copies.append(
                (2, spot * out_rows + side * (out_rows // 2), out_rows // 2,
                 start + query_rows + latent_rows, side * out_width)
            )
    low = jnp.bfloat16
    arrays = [latents, query, key_value, upstream, heads]
    return pl.pallas_call(
        functools.partial(head_sums_kernel, copies, rank),
        in_specs=[SCALARS] + [full(array) for array in arrays],
        out_specs=pl.BlockSpec((count * rows, width), lambda: (0, 0)),
        out_shape=jax.ShapeDtypeStruct((count * rows, width), low),
        scratch_shapes=[
            pltpu.VMEM((rank, width), low),
            pltpu.VMEM((KVR, width), low),
            pltpu.VMEM((upstream.shape[1], out_width), low),
            pltpu.SemaphoreType.DMA((len(copies),)),
        ],
        compiler_params=pltpu.CompilerParams(vmem_limit_bytes=ROOM),
        cost_estimate=lasting(20),
        name="head_sums",
    )(spots, *arrays)


def token_back_kernel(grad_ref, weights_ref, tokens_ref, hidden_ref, gain_ref, out_ref):
    upstream = product_right(grad_ref[...], weights_ref[...])
    values = tokens_ref[...].astype(jnp.float32)
    inverse = normalize(values, gain_ref[...])[1]
    out_ref[...] = hidden_ref[...] + normalize_back(values, inverse, gain_ref[...], upstream)


def token_back(grad, weights, tokens, hidden_grad, gain):
    arrays = [grad, weights, tokens, hidden_grad, gain]
    return pl.pallas_call(
        token_back_kernel,
        in_specs=[full(array) for array in arrays],
        out_specs=full(hidden_grad),
        out_shape=jax.ShapeDtypeStruct(hidden_grad.shape, jnp.float32),
        compiler_params=pltpu.CompilerParams(vmem_limit_bytes=ROOM),
        cost_estimate=lasting(8),
        name="token_back",
    )(*arrays)


def reorder_kernel(spots_ref, in_ref, out_ref):
    width = in_ref.shape[1]
    count = spots_ref.shape[0]
    size = width // count
    window = min(-(-(size + LANES - 1) // LANES) * LANES, width)
    for place in range(count):
        start = spots_ref[place] * size
        base = jnp.minimum(start // LANES * LANES, width - window)
        held = in_ref[:, pl.ds(pl.multiple_of(base, LANES), window)].astype(jnp.float32)
        held = pltpu.roll(held, lax.rem(window - (start - base), window), 1)
        out_ref[:, place * size : (place + 1) * size] = held[:, :size].astype(out_ref.dtype)


def reorder(values, spots):
    return pl.pallas_call(
        reorder_kernel,
        in_specs=[SCALARS, full(values)],
        out_specs=full(values),
        out_shape=jax.ShapeDtypeStruct(values.shape, values.dtype),
        compiler_params=pltpu.CompilerParams(vmem_limit_bytes=ROOM),
        cost_estimate=lasting(4),
        name="reorder",
    )(spots, values)


class Ring:
    def __init__(self, axis):
        self.axis = axis
        self.count = lax.axis_size(axis)
        self.half = self.count // 2
        order = list(range(0, self.count, 2)) + list(range(self.count - 1, 0, -2))
        self.me = lax.axis_index(axis)
        self.spot = self.place(self.me)
        indices = jnp.arange(self.count, dtype=jnp.int32)
        self.ahead = self.owner(indices)
        self.behind = lax.rem(self.place(indices) - self.spot + self.count, self.count)
        self.up = [(order[i], order[(i + 1) % self.count]) for i in range(self.count)]
        self.down = [(b, a) for a, b in self.up]

    def place(self, index):
        return jnp.where(index % 2 == 0, index // 2, self.count - (index + 1) // 2)

    def owner(self, step):
        spot = lax.rem(self.spot + step + self.count, self.count)
        return jnp.where(spot < self.half, 2 * spot, 2 * self.count - 1 - 2 * spot)

    def send_up(self, block):
        return lax.ppermute(block, self.axis, self.up)

    def send_down(self, block):
        return lax.ppermute(block, self.axis, self.down)


class Gather:
    def __init__(self, ring, shard):
        self.ring = ring
        self.rows = shard.shape[0]
        self.low = self.high = shard
        self.blocks = {0: shard}
        self.step = 0

    def advance(self):
        ring = self.ring
        if self.done:
            return
        self.step += 1
        if self.step < ring.half:
            self.low = ring.send_up(self.low)
            self.high = ring.send_down(self.high)
            self.blocks[self.step] = self.high
            self.blocks[ring.count - self.step] = self.low
        else:
            cut = self.rows // 2
            self.low = ring.send_up(self.low[:cut])
            self.high = ring.send_down(self.high[cut:])
            self.blocks[ring.half] = None

    @property
    def done(self):
        return self.step >= self.ring.half

    def finish(self):
        while not self.done:
            self.advance()
        self.blocks[self.ring.half] = jnp.concatenate([self.low, self.high], axis=0)
        return [self.blocks[spot] for spot in range(self.ring.count)]


class Scatter:
    def __init__(self, ring, take, rows):
        self.ring = ring
        self.take = lambda step, start, size: take(step % ring.count, start, size)
        self.rows = rows
        self.step = 0
        self.low = self.high = None

    def add(self, a, b):
        return (a.astype(jnp.float32) + b.astype(jnp.float32)).astype(b.dtype)

    def advance(self):
        ring, rows, cut = self.ring, self.rows, self.rows // 2
        if self.done:
            return
        ahead = ring.half - self.step
        if self.step:
            self.low, self.high = lax.optimization_barrier((self.low, self.high))
        self.step += 1
        if ahead == ring.half:
            low = self.take(ahead, 0, cut)
            high = self.take(ahead, cut, rows - cut)
        elif ahead == ring.half - 1:
            low = self.take(ahead, 0, rows)
            high = self.take(-ahead, 0, rows)
            low = jnp.concatenate([self.add(self.low, low[:cut]), low[cut:]], axis=0)
            high = jnp.concatenate([high[:cut], self.add(self.high, high[cut:])], axis=0)
        else:
            low = self.add(self.low, self.take(ahead, 0, rows))
            high = self.add(self.high, self.take(-ahead, 0, rows))
        self.sent = (low, high)
        self.low = ring.send_up(low)
        self.high = ring.send_down(high)

    @property
    def done(self):
        return self.step >= self.ring.half

    def finish(self):
        while not self.done:
            self.advance()
        own = self.take(0, 0, self.rows).astype(jnp.float32)
        return own + self.low.astype(jnp.float32) + self.high.astype(jnp.float32)


def stacked(ring, grads):
    rows = grads.shape[0] // ring.count

    def take(spot, start, size):
        return lax.slice_in_dim(grads, spot * rows + start, spot * rows + start + size, axis=0)

    return Scatter(ring, take, rows)


def staged(ring, left, right):
    size = left.shape[1] // ring.count
    low, high = ring.count // 4, ring.count // 4 + ring.half
    parts = {}
    held = [right]

    def take(spot, start, rows):
        name = 1 if low <= spot < high else 0 if spot < low else 2
        first = (0, low, high)[name]
        if name not in parts:
            last = (low, high, ring.count)[name]
            columns = lax.slice_in_dim(left, first * size, last * size, axis=1)
            parts[name] = product_left(columns, held[0]).astype(jnp.bfloat16)
        begin = (spot - first) * size + start
        return lax.slice_in_dim(parts[name], begin, begin + rows, axis=0)

    scatter = Scatter(ring, take, size)
    scatter.held = held
    scatter.parts = parts
    return scatter


def delay(scatter, *others):
    scatter.held[0] = follow(scatter.held[0], *others)


def follow(values, *others):
    return lax.optimization_barrier((values, others))[0]


def ends(*streams):
    return [(stream.low, stream.high) for stream in streams]


def hold(stream, *others):
    stream.low, stream.high = follow((stream.low, stream.high), *others)


def swap(values, bit):
    count = lax.axis_size("tensor")
    return lax.ppermute(values, "tensor", [(i, i ^ bit) for i in range(count)])


def pad_heads(weights, heads):
    rows = weights.shape[0]
    width = weights.shape[1] // heads
    padded = jnp.pad(weights.reshape(rows, heads, width), ((0, 0), (0, 0), (0, LANES - width)))
    return padded.reshape(rows, heads * LANES)


def on_device(
    tokens,
    segments,
    positions,
    norm_input,
    norm_query,
    norm_latent,
    norm_hidden,
    query_down,
    latent_down,
    query_up,
    latent_up,
    attention_out,
    gate_weight,
    up_weight,
    down_weight,
    cotangent,
):
    low = jnp.bfloat16
    local_rows = tokens.shape[0]
    shard = lax.axis_index("tensor")
    offset = shard * local_rows
    length = segments.shape[0]
    local_heads = HEADS // lax.axis_size("tensor")
    pairs = local_heads // 2
    rank = query_down.shape[1]
    ring = Ring("fsdp")
    everyone = lax.axis_size("fsdp") * lax.axis_size("tensor")
    teams = lax.axis_size("tensor")
    gains_own = jnp.concatenate([norm_input, norm_hidden, norm_query, norm_latent])
    gain_sizes = [norm_input.shape[0], norm_hidden.shape[0], norm_query.shape[0], norm_latent.shape[0]]
    gain_width = -(-gains_own.shape[0] // LANES) * LANES
    spare = LANES - NOPE - ROPE
    gain_rows = -(-gains_own.shape[0] // spare)
    down_rows = query_down.shape[0]
    down_width = rank + KVR + LANES
    gain_part = jnp.pad(gains_own, (0, gain_rows * spare - gains_own.shape[0]))
    gain_part = jnp.pad(gain_part.reshape(gain_rows, spare), ((0, down_rows - gain_rows), (0, 0)))
    packed = jnp.concatenate(
        [
            query_down,
            latent_down[:, :KVR],
            jnp.zeros((down_rows, NOPE), low),
            latent_down[:, KVR:],
            gain_part,
        ],
        axis=1,
    )
    feed_width = gate_weight.shape[1]
    feed_rows = gate_weight.shape[0]
    feed_pad = -feed_width % LANES
    widen = lambda weights: jnp.pad(weights, ((0, 0), (0, feed_pad)))
    head_width = 2 * pairs * LANES
    query_rows, latent_rows, out_rows = query_up.shape[0], latent_up.shape[0], attention_out.shape[1]
    out_width = attention_out.shape[0]
    out_t = attention_out.T
    mixed = jnp.concatenate(
        [
            pad_heads(query_up, local_heads),
            latent_up,
            jnp.concatenate([out_t[: out_rows // 2], out_t[out_rows // 2 :]], axis=1),
        ],
        axis=0,
    )
    mixed_up = Gather(ring, mixed)
    down_up = Gather(ring, widen(down_weight.T))
    pair_own = paired(gate_weight, up_weight)
    pair_up = Gather(ring, pair_own)

    tokens_ring = reorder(tokens, ring.ahead)
    upstream = reorder(cotangent, ring.ahead)
    here, turn_low, turn_high = rotary_lanes(positions)
    tables = (here, turn_low, turn_high)
    local_tables = [lax.dynamic_slice_in_dim(table, offset, local_rows) for table in tables]
    query_feat, key_feat = segment_lanes(segments)
    key_feat = key_feat.astype(low)
    ahead, behind = ring.ahead, ring.behind
    team_ids = shard ^ jnp.asarray([0, 2, 1, 3], jnp.int32)

    small_up = Gather(ring, jnp.concatenate([packed, swap(packed, 2)], axis=0))
    pieces, copies = [], []

    def collect(block, spot, team):
        for first, piece in ((team, block), (team + 2, swap(block, 1))):
            for part in range(block.shape[0] // down_rows):
                copies.append(
                    (len(pieces), part * down_rows, down_rows, spot * teams, first + part)
                )
            pieces.append(piece)

    collect(small_up.low, 0, 0)
    mixed_up.advance()
    down_up.advance()
    while not small_up.done:
        swapped = pieces[1::2]
        small_up.advance()
        mixed_up.advance()
        if not small_up.done:
            collect(small_up.high, small_up.step, 0)
            collect(small_up.low, ring.count - small_up.step, 0)
            hold(small_up, ends(mixed_up, down_up), swapped)
            hold(mixed_up, ends(small_up))
    collect(small_up.low, ring.half, 0)
    collect(small_up.high, ring.half, 1)
    hold(down_up, ends(mixed_up, small_up))
    down_up.advance()
    if down_rows % 16:
        table = [[None] * teams for _ in range(ring.count)]
        for piece, row, _, block, team in copies:
            table[block // teams][team] = pieces[piece][row : row + gain_rows, down_width - spare :]
        table = jnp.stack([part for group in zip(*table) for part in group])
        table = table.reshape(teams, ring.count, gain_rows * spare)
        places = shard ^ jnp.arange(teams, dtype=jnp.int32)
        places = jnp.where(places == 1, 2, jnp.where(places == 2, 1, places))
        table = jnp.take(table, places, axis=0)
    else:
        table = collect_rows(
            team_ids, pieces, [(piece, row, block, team) for piece, row, _, block, team in copies]
        )
        table = table.reshape(ring.count, teams, 16, LANES)[:, :, :gain_rows, LANES - spare :]
        table = jnp.transpose(table, (1, 0, 2, 3)).reshape(teams, ring.count, gain_rows * spare)
    table = table.astype(jnp.float32)
    gain_parts = []
    start = 0
    for number, size in enumerate(gain_sizes):
        part = jnp.transpose(table[:, :, start : start + size], (1, 0, 2))
        if number >= 2:
            part = jnp.take(part, behind, axis=0)
        gain_parts.append(part.reshape(1, -1))
        start += size
    gain_in, gain_hidden, gain_query, gain_latent = gain_parts
    if down_rows % 16:
        whole = jnp.zeros((everyone * down_rows, down_width), low)
        for piece, row, rows, block, team in copies:
            whole = lax.dynamic_update_slice(
                whole, pieces[piece][row : row + rows], ((block + team_ids[team]) * rows, 0)
            )
        pieces, copies = [whole], [(0, 0, whole.shape[0], 0, None)]
    latent_send, latent_raw, attention_input, down_projections = project(
        team_ids, tokens_ring, (gain_in, gain_query, gain_latent), local_tables, pieces, copies, rank
    )
    latent_send = follow(latent_send, ends(down_up))
    latents = lax.all_gather(latent_send, "tensor", axis=0, tiled=True)
    hold(down_up, latent_send)
    down_up.advance()
    latents = follow(latents, ends(down_up))
    hold(pair_up, ends(down_up))
    mixed_blocks = mixed_up.finish()
    if query_rows % 16 or latent_rows % 16 or out_rows % 32:
        mixed_all = jnp.stack([mixed_blocks[0]] * ring.count)
        for spot, block in enumerate(mixed_blocks):
            mixed_all = lax.dynamic_update_slice(mixed_all, block[None], (ring.owner(spot), 0, 0))
        wq = mixed_all[:, :query_rows].reshape(-1, head_width)
        wkv = mixed_all[:, query_rows : query_rows + latent_rows].reshape(-1, head_width)
        outs = [block[query_rows + latent_rows :] for block in mixed_blocks]
        attention_out_t = jnp.concatenate(
            [block[:, side * out_width : (side + 1) * out_width] for block in outs for side in (0, 1)],
            axis=0,
        )
    else:
        copies = []
        for spot in range(ring.count):
            copies.append((spot, 0, query_rows, 0, head_width, 0, (spot, query_rows)))
            copies.append((spot, query_rows, latent_rows, 0, head_width, 1, (spot, latent_rows)))
            for side in (0, 1):
                copies.append(
                    (spot, query_rows + latent_rows, out_rows // 2, side * out_width, out_width, 2,
                     spot * out_rows + side * (out_rows // 2))
                )
        wq, wkv, attention_out_t = assemble(
            ahead,
            mixed_blocks,
            copies,
            [(ring.count * query_rows, head_width), (ring.count * latent_rows, head_width),
             (ring.count * out_rows, out_width)],
        )
    down_up.advance()
    pair_up.advance()
    feed_upstream = follow(RESIDUAL * upstream.astype(jnp.float32), latents).astype(low)
    feed_upstream = lax.all_gather(feed_upstream, "tensor", axis=0, tiled=True)
    rope = latents[:, rank + KVR :] + key_feat
    heads, query_heads, key_value, log_totals = attention_forward(
        latents, wq, wkv, rope, query_feat, tables, pairs
    )
    branch_terms = product_right(heads, attention_out_t).astype(low)
    branch_terms = follow(branch_terms, feed_upstream, ends(pair_up))
    attention_branch = lax.psum_scatter(branch_terms, "tensor", scatter_dimension=0, tiled=True)
    downs = down_up.finish()
    if ring.count > 8:
        downs = [jnp.concatenate(downs, axis=0)]
    activated_grad = feed_product(feed_upstream, downs)
    attention_branch = follow(attention_branch, activated_grad)
    hidden = tokens_ring.astype(jnp.float32) + RESIDUAL * attention_branch.astype(jnp.float32)
    feed_normed, inverse_hidden = normalize(hidden, gain_hidden)
    pair_up.advance()
    feed_normed = follow(feed_normed.astype(low), ends(pair_up))
    feed_seq = lax.all_gather(feed_normed, "tensor", axis=0, tiled=True)
    weights = pair_up.finish()
    if ring.count > 8:
        weights = [jnp.concatenate(weights, axis=0)]
    activated, pair_grad = feed_gate(feed_seq, weights, activated_grad)

    grad_down = staged(ring, feed_upstream, activated)
    grad_down.advance()
    grad_pair = staged(ring, feed_seq, follow(pair_grad, grad_down.sent))
    grad_pair.advance()
    hold(grad_down, grad_pair.sent)
    grad_down.advance()
    half = max(len(weights) // 2, 1)
    width = feed_seq.shape[1]
    pair_grad = follow(pair_grad, grad_down.sent)
    terms = feed_terms(pair_grad, weights[:half], width, 0)
    hold(grad_pair, terms)
    grad_pair.advance()
    if len(weights) > half:
        terms = follow(terms, grad_pair.sent)
        terms = feed_terms(pair_grad, weights[half:], width, 1, terms)
    terms = follow(terms, ends(grad_down))
    feed_back = lax.psum_scatter(terms, "tensor", scatter_dimension=0, tiled=True)
    delay(grad_down, terms)
    hold(grad_down, terms)
    grad_down.advance()
    feed_back = follow(feed_back, grad_down.sent)
    delay(grad_pair, grad_down.sent)
    grad_pair.advance()
    grad_pair.take(0, 0, 1), grad_down.take(0, 0, 1)
    feed_back = follow(feed_back, grad_pair.parts[0], grad_down.parts[0])
    hidden_back = normalize_back(
        hidden, inverse_hidden, gain_hidden, feed_back.astype(jnp.float32)
    )
    hidden_grad = upstream.astype(jnp.float32) + hidden_back
    upstream_send = follow((RESIDUAL * hidden_grad).astype(low), grad_pair.sent, ends(grad_down))
    attention_upstream = lax.all_gather(upstream_send, "tensor", axis=0, tiled=True)
    grad_down.advance()
    activated = follow(activated, upstream_send)
    feed_branch = feed_terms(activated, downs[:half], width, 0, None, lasting(11))
    if len(downs) > half:
        feed_branch = feed_terms(activated, downs[half:], width, 1, feed_branch, lasting(11))
    attention_upstream = follow(
        attention_upstream, feed_branch, ends(grad_pair), grad_down.sent
    )
    feed_branch = lax.psum_scatter(feed_branch, "tensor", scatter_dimension=0, tiled=True)
    heads_grad = product(attention_upstream, attention_out_t).astype(low)
    grad_pair.advance()
    heads_grad = follow(heads_grad, grad_pair.sent)
    query_raw_grad, key_value_grad, key_rope_grad = attention_backward(
        query_heads, key_value, heads_grad, log_totals, rope, tables
    )
    query_raw_grad, key_value_grad = follow((query_raw_grad, key_value_grad), ends(grad_down))
    latent_terms = jnp.concatenate(
        [
            product_right(query_raw_grad, wq),
            product_right(key_value_grad, wkv),
            key_rope_grad,
        ],
        axis=1,
    ).astype(low)
    latent_terms = follow(latent_terms, feed_branch)
    output = hidden + RESIDUAL * feed_branch.astype(jnp.float32)
    latent_grad = lax.psum_scatter(latent_terms, "tensor", scatter_dimension=0, tiled=True)
    upstream_late, query_raw_grad, key_value_grad = follow(
        (attention_upstream, query_raw_grad, key_value_grad), latent_terms
    )
    if query_rows % 16 or latent_rows % 16 or out_rows % 32:
        sums = [
            jnp.take(product_left(left, right).astype(low).reshape(ring.count, -1, head_width), ahead, axis=0)
            for left, right in (
                (latents[:, :rank], query_raw_grad),
                (latents[:, rank : rank + KVR], key_value_grad),
            )
        ]
        out_sums = product_left(upstream_late, heads).astype(low)
        out_sums = out_sums.reshape(ring.count, 2, out_rows // 2, out_width)
        sums.append(jnp.concatenate([out_sums[:, 0], out_sums[:, 1]], axis=2))
        mixed_sums = jnp.concatenate(sums, axis=1).reshape(-1, head_width)
    else:
        mixed_sums = head_sums(
            ahead, latents, query_raw_grad, key_value_grad, upstream_late, heads,
            rank, query_rows, latent_rows, out_rows,
        )
    grad_mixed = stacked(ring, mixed_sums)
    grad_mixed.advance()
    grad_mixed.advance()
    latent_grad = follow(latent_grad, grad_mixed.sent, ends(grad_pair))
    pair = 2 * down_rows
    height = ring.count * pair
    heights = [height, height]
    copies = [
        (team // 2, spot * pair + (team % 2) * down_rows, down_rows, spot * teams, team)
        for spot in range(ring.count)
        for team in range(teams)
    ]
    aligned = down_rows % 16 == 0
    if not aligned:
        copies, heights = [(0, 0, 2 * height, 0, None)], [2 * height]
    sent, latent_low = latent_back(
        team_ids, latent_grad, latent_raw, attention_input, (gain_query, gain_latent),
        local_tables, copies, heights, rank,
    )
    if not aligned:
        blocks = jnp.take(
            sent[0].reshape(ring.count, teams, down_rows, down_width), team_ids, axis=1
        )
        sent = [blocks[:, :2].reshape(height, -1), blocks[:, 2:].reshape(height, -1)]

    def add_low(a, b):
        return (a.astype(jnp.float32) + b.astype(jnp.float32)).astype(low)

    other_sums = swap(sent[1], 1)
    token_grad = token_back(
        latent_low, down_projections, tokens_ring, hidden_grad, gain_in
    )
    other_sums = follow(other_sums, token_grad)
    grad_small = stacked(ring, add_low(sent[0], other_sums))
    grad_small.advance()
    token_grad = reorder(follow(token_grad, grad_small.sent), ring.behind)
    hold(grad_down, ends(grad_small))
    hold(grad_mixed, grad_small.sent)
    grad_mixed.advance()
    hold(grad_small, token_grad)
    grad_small.advance()
    hold(grad_mixed, grad_small.sent)
    hold(grad_pair, ends(grad_small))
    grad_small.advance()
    output = reorder(follow(output.astype(low), grad_small.sent), ring.behind)
    grad_mixed.advance()
    small_own = grad_small.finish()
    small_other = follow(small_own[down_rows:].astype(low), ends(grad_mixed))
    packed_own = small_own[:down_rows] + swap(small_other, 2).astype(jnp.float32)
    rope_from = rank + KVR + NOPE
    lanes = jnp.arange(down_width) < rope_from + ROPE
    grad_gain_input = jnp.sum(
        jnp.where(lanes, packed.astype(jnp.float32) * packed_own, 0.0), axis=1
    ) / norm_input.astype(jnp.float32)
    grad_mixed_own = grad_mixed.finish()
    while not grad_pair.done:
        grad_pair.advance()
    grad_query_own = grad_mixed_own[:query_rows].reshape(query_rows, local_heads, LANES)
    grad_out_own = grad_mixed_own[query_rows + latent_rows :]
    grad_out_own = jnp.concatenate(
        [grad_out_own[:, :out_width], grad_out_own[:, out_width:]], axis=0
    )
    grad_gate_own, grad_up_own, pair_sums = unpaired(
        grad_pair.parts[0], grad_pair.low, grad_pair.high, pair_own, feed_width
    )
    row_sums = lambda weights, grads: jnp.sum(weights.astype(jnp.float32) * grads, axis=1)
    head_rows = query_rows + latent_rows
    gain_sums = jnp.concatenate(
        [pair_sums[:, 0], row_sums(mixed[:head_rows], grad_mixed_own[:head_rows])]
    )
    gain_sums = jnp.pad(gain_sums, (0, -gain_sums.shape[0] % LANES))[None]
    gain_sums = gain_sums + swap(gain_sums, 1)
    gain_sums = (gain_sums + swap(gain_sums, 2))[0]
    gain_grads = []
    start = 0
    for gain in (norm_hidden, norm_query, norm_latent):
        size = gain.shape[0]
        own = lax.dynamic_slice_in_dim(gain_sums, start + shard * size, size)
        gain_grads.append(own / gain.astype(jnp.float32))
        start += size * teams
    return (
        output,
        token_grad,
        grad_gain_input,
        gain_grads[1],
        gain_grads[2],
        gain_grads[0],
        packed_own[:, :rank],
        jnp.concatenate(
            [packed_own[:, rank : rank + KVR], packed_own[:, rope_from : rope_from + ROPE]],
            axis=1,
        ),
        grad_query_own[:, :, : NOPE + ROPE].reshape(query_rows, -1),
        grad_mixed_own[query_rows : query_rows + latent_rows],
        grad_out_own.T,
        grad_gate_own,
        grad_up_own,
        grad_down.finish()[:, :feed_width].T,
    )


def solution(mesh):
    return jax.shard_map(
        on_device,
        mesh=mesh,
        in_specs=(
            P(("fsdp", "tensor"), None),
            P("fsdp"),
            P("fsdp"),
            P(("fsdp", "tensor")),
            P(("fsdp", "tensor")),
            P(("fsdp", "tensor")),
            P(("fsdp", "tensor")),
            P(("fsdp", "tensor"), None),
            P(("fsdp", "tensor"), None),
            P("fsdp", "tensor"),
            P("fsdp", "tensor"),
            P("tensor", "fsdp"),
            P("fsdp", "tensor"),
            P("fsdp", "tensor"),
            P("tensor", "fsdp"),
            P(("fsdp", "tensor"), None),
        ),
        out_specs=(
            P(("fsdp", "tensor"), None),
            P(("fsdp", "tensor"), None),
            P(("fsdp", "tensor")),
            P(("fsdp", "tensor")),
            P(("fsdp", "tensor")),
            P(("fsdp", "tensor")),
            P(("fsdp", "tensor"), None),
            P(("fsdp", "tensor"), None),
            P("fsdp", "tensor"),
            P("fsdp", "tensor"),
            P("tensor", "fsdp"),
            P("fsdp", "tensor"),
            P("fsdp", "tensor"),
            P("tensor", "fsdp"),
        ),
        check_vma=False,
    )
```

```python
import functools
import math

import jax
import jax.numpy as jnp
from jax import lax
from jax.experimental import pallas as pl
from jax.experimental.pallas import tpu as pltpu
from jax.sharding import PartitionSpec as P

HEADS = 40
NOPE = 64
ROPE = 32
VDIM = 64
KVR = 256
LANES = 128
BLOCK = 256


EPSILON = 1e-05
RESIDUAL = 1.4 / math.sqrt(62.0)
NEGATIVE = -1e30
APART = -(2.0**96)
SCALE = 1.0 / math.sqrt(NOPE + ROPE)
LOG2E = math.log2(math.e)
ROOM = 56 * 1024 * 1024
BRIEF = pl.CostEstimate(flops=1, bytes_accessed=1, transcendentals=0)


def lasting(microseconds):
    return pl.CostEstimate(flops=1, bytes_accessed=microseconds * 3 * 10**6, transcendentals=0)


def normalize(values, gain):
    inverse = lax.rsqrt(jnp.mean(values * values, axis=-1, keepdims=True) + EPSILON)
    return (values * inverse * gain, inverse)


def normalize_back(values, inverse, gain, upstream):
    scaled = upstream * gain
    inner = jnp.mean(scaled * values, axis=-1, keepdims=True)
    return inverse * scaled - values * (inverse * inverse * inverse) * inner


def product(left, right):
    return jnp.dot(left, right, preferred_element_type=jnp.float32)


def product_left(left, right):
    return lax.dot_general(
        left, right, (((0,), (0,)), ((), ())), preferred_element_type=jnp.float32
    )


def product_right(left, right):
    return lax.dot_general(
        left, right, (((1,), (1,)), ((), ())), preferred_element_type=jnp.float32
    )


def rotary_lanes(positions):
    lane = jnp.arange(LANES, dtype=jnp.int32)
    steps = ((lane - NOPE) % (ROPE // 2)).astype(jnp.float32)
    frequency = jnp.exp(steps * (-2.0 * math.log(10000.0) / ROPE))
    angles = positions.astype(jnp.float32)[:, None] * frequency[None, :]
    first = ((lane >= NOPE) & (lane < NOPE + ROPE // 2))[None, :]
    second = ((lane >= NOPE + ROPE // 2) & (lane < NOPE + ROPE))[None, :]
    cosine = jnp.cos(angles)
    sine = jnp.sin(angles)
    here = jnp.where((lane < NOPE)[None, :], 1.0, jnp.where(first | second, cosine, 0.0))
    return (here, jnp.where(first, -sine, 0.0), jnp.where(second, sine, 0.0))


def segment_lanes(segment_ids):
    lane = jnp.arange(LANES, dtype=jnp.int32) - (NOPE + ROPE)
    same = lane[None, :] == segment_ids[:, None]
    used = ((lane >= 0) & (lane < 4))[None, :]
    query = jnp.where(used & same, 1.0, 0.0)
    key = jnp.where(used & ~same, APART, 0.0)
    return (query, key)


def roll_lanes(values, amount):
    return pltpu.roll(values, amount % LANES, 1)


def forward_kernel(
    xq_ref, lat_ref, wq_ref, wkv_ref, rope_ref, feat_ref, here_ref, low_ref, high_ref,
    out_ref, q_ref, kv_ref, lse_ref, k_ref,
):
    length = xq_ref.shape[0]
    lane = lax.broadcasted_iota(jnp.int32, (BLOCK, LANES), 1)
    causal = lax.broadcasted_iota(jnp.int32, (BLOCK, BLOCK), 1) <= lax.broadcasted_iota(
        jnp.int32, (BLOCK, BLOCK), 0
    )
    blocks = [slice(start, start + BLOCK) for start in range(0, length, BLOCK)]
    for rows in blocks:
        q_raw = product(xq_ref[rows, :], wq_ref[...])
        kv_ref[rows, :] = product(lat_ref[rows, :], wkv_ref[...]).astype(jnp.bfloat16)
        for head in range(2):
            part = slice(head * LANES, (head + 1) * LANES)
            raw = q_raw[:, part]
            turned = (
                raw * here_ref[rows, :]
                + roll_lanes(raw, -ROPE // 2) * low_ref[rows, :]
                + roll_lanes(raw, ROPE // 2) * high_ref[rows, :]
                + feat_ref[rows, :]
            )
            q_ref[rows, part] = turned.astype(jnp.bfloat16)
            k_ref[head, rows, :] = jnp.where(lane < NOPE, kv_ref[rows, part], rope_ref[rows, :])
    for rows in blocks:
        results = []
        for head in range(2):
            part = slice(head * LANES, (head + 1) * LANES)
            query = q_ref[rows, part]
            near = product_right(query, k_ref[head, rows, :])
            near = jnp.where(causal, near, NEGATIVE)
            top = jnp.max(near, axis=1, keepdims=True)
            if rows.start:
                far = product_right(query, k_ref[head, : rows.start, :])
                top = jnp.maximum(top, jnp.max(far, axis=1, keepdims=True))
            weights = jnp.exp2((near - top) * (SCALE * LOG2E))
            total = jnp.sum(weights, axis=1, keepdims=True)
            result = product(weights.astype(jnp.bfloat16), kv_ref[rows, part])
            if rows.start:
                weights = jnp.exp2((far - top) * (SCALE * LOG2E))
                total = total + jnp.sum(weights, axis=1, keepdims=True)
                result = result + product(
                    weights.astype(jnp.bfloat16), kv_ref[: rows.start, part]
                )
            results.append(result / total)
            log_total = top * (SCALE * LOG2E) + jnp.log2(total)
            lse_ref[0, head : head + 1, rows] = jnp.transpose(
                jnp.broadcast_to(log_total, (BLOCK, LANES))
            )[0:1, :]
        out_ref[rows, :] = jnp.where(
            lane < VDIM, roll_lanes(results[0], VDIM), results[1]
        ).astype(jnp.bfloat16)


def attention_forward(latents, wq, wkv, rope, feat, tables, pairs):
    length = latents.shape[0]
    rank = wq.shape[0]
    whole = lambda width, at=0: pl.BlockSpec((length, width), lambda j: (0, at))
    mine = lambda width: pl.BlockSpec((length, width), lambda j: (0, j))
    tall = lambda rows: pl.BlockSpec((rows, 2 * LANES), lambda j: (0, j))
    low = jnp.bfloat16
    return pl.pallas_call(
        forward_kernel,
        grid=(pairs,),
        in_specs=[
            whole(rank), whole(KVR, rank // KVR), tall(rank), tall(KVR),
            whole(LANES), whole(LANES), whole(LANES), whole(LANES), whole(LANES),
        ],
        out_specs=[
            mine(LANES), mine(2 * LANES), mine(2 * LANES),
            pl.BlockSpec((1, 2, length), lambda j: (j, 0, 0)),
        ],
        out_shape=[
            jax.ShapeDtypeStruct((length, pairs * LANES), low),
            jax.ShapeDtypeStruct((length, pairs * 2 * LANES), low),
            jax.ShapeDtypeStruct((length, pairs * 2 * LANES), low),
            jax.ShapeDtypeStruct((pairs, 2, length), jnp.float32),
        ],
        scratch_shapes=[pltpu.VMEM((2, length, LANES), low)],
        compiler_params=pltpu.CompilerParams(vmem_limit_bytes=ROOM),
        cost_estimate=lasting(23),
        name="attention_forward",
    )(latents, latents, wq, wkv, rope, feat, *tables)


def backward_kernel(
    q_ref, kv_ref, grad_ref, lse_ref, rope_ref, here_ref, low_ref, high_ref,
    dq_ref, dkv_ref, drope_ref, k_ref, do_ref, dk_ref, dv_ref,
):
    length = q_ref.shape[0]
    lane = lax.broadcasted_iota(jnp.int32, (BLOCK, LANES), 1)
    causal = lax.broadcasted_iota(jnp.int32, (BLOCK, BLOCK), 0) <= lax.broadcasted_iota(
        jnp.int32, (BLOCK, BLOCK), 1
    )
    blocks = [slice(start, start + BLOCK) for start in range(0, length, BLOCK)]

    @pl.when(pl.program_id(0) == 0)
    def _():
        drope_ref[...] = jnp.zeros_like(drope_ref)

    for rows in blocks:
        for head in range(2):
            part = slice(head * LANES, (head + 1) * LANES)
            k_ref[head, rows, :] = jnp.where(lane < NOPE, kv_ref[rows, part], rope_ref[rows, :])
            upstream = grad_ref[rows, :].astype(jnp.float32)
            if head == 0:
                upstream = roll_lanes(upstream, VDIM)
            do_ref[head, rows, :] = jnp.where(lane < NOPE, 0.0, upstream).astype(jnp.bfloat16)
    for head in range(2):
        part = slice(head * LANES, (head + 1) * LANES)
        for rows in reversed(blocks):
            last = rows.stop == length
            query = q_ref[rows, part]
            upstream = do_ref[head, rows, :]
            log_total = lse_ref[0, head : head + 1, rows]
            pieces = [rows] + ([slice(0, rows.start)] if rows.start else [])
            held = []
            delta = None
            for piece in pieces:
                scores = product_right(k_ref[head, piece, :], query)
                probability = jnp.exp2(scores * (SCALE * LOG2E) - log_total)
                if piece is rows:
                    probability = jnp.where(causal, probability, 0.0)
                slope = product_right(kv_ref[piece, part], upstream)
                inner = jnp.sum(probability * slope, axis=0, keepdims=True)
                delta = inner if delta is None else delta + inner
                held.append((piece, probability, slope))
            query_grad = None
            for piece, probability, slope in held:
                score_grad = (probability * (slope - delta)).astype(jnp.bfloat16)
                key_grad = product(score_grad, query)
                value_grad = product(probability.astype(jnp.bfloat16), upstream)
                if last:
                    dk_ref[piece, :] = key_grad
                    dv_ref[piece, :] = value_grad
                else:
                    dk_ref[piece, :] += key_grad
                    dv_ref[piece, :] += value_grad
                term = product_left(score_grad, k_ref[head, piece, :])
                query_grad = term if query_grad is None else query_grad + term
            query_grad = query_grad * SCALE
            dq_ref[rows, part] = (
                query_grad * here_ref[rows, :]
                - roll_lanes(query_grad, -ROPE // 2) * low_ref[rows, :]
                - roll_lanes(query_grad, ROPE // 2) * high_ref[rows, :]
            ).astype(jnp.bfloat16)
        for rows in blocks:
            key_grad = dk_ref[rows, :] * SCALE
            dkv_ref[rows, part] = jnp.where(lane < NOPE, key_grad, dv_ref[rows, :]).astype(
                jnp.bfloat16
            )
            drope_ref[rows, :] += jnp.where(
                (lane >= NOPE) & (lane < NOPE + ROPE), key_grad, 0.0
            )


def attention_backward(query, key_value, grad, lse, rope, tables):
    length = query.shape[0]
    pairs = grad.shape[1] // LANES
    whole = lambda width: pl.BlockSpec((length, width), lambda j: (0, 0))
    mine = lambda width: pl.BlockSpec((length, width), lambda j: (0, j))
    low = jnp.bfloat16
    return pl.pallas_call(
        backward_kernel,
        grid=(pairs,),
        in_specs=[
            mine(2 * LANES), mine(2 * LANES), mine(LANES),
            pl.BlockSpec((1, 2, length), lambda j: (j, 0, 0)),
            whole(LANES), whole(LANES), whole(LANES), whole(LANES),
        ],
        out_specs=[mine(2 * LANES), mine(2 * LANES), whole(LANES)],
        out_shape=[
            jax.ShapeDtypeStruct((length, pairs * 2 * LANES), low),
            jax.ShapeDtypeStruct((length, pairs * 2 * LANES), low),
            jax.ShapeDtypeStruct((length, LANES), jnp.float32),
        ],
        scratch_shapes=[
            pltpu.VMEM((2, length, LANES), low),
            pltpu.VMEM((2, length, LANES), low),
            pltpu.VMEM((length, LANES), jnp.float32),
            pltpu.VMEM((length, LANES), jnp.float32),
        ],
        compiler_params=pltpu.CompilerParams(vmem_limit_bytes=ROOM),
        cost_estimate=lasting(31),
        name="attention_backward",
    )(query, key_value, grad, lse, rope, *tables)


def vector(width):
    return pl.BlockSpec((1, width), lambda *_: (0, 0))


def full(array):
    return pl.BlockSpec(array.shape, lambda *_: (0,) * array.ndim)


ANYWHERE = pl.BlockSpec(memory_space=pl.ANY)
SCALARS = pl.BlockSpec(memory_space=pltpu.SMEM)


def assemble_kernel(copies, count, *refs):
    spots_ref, pieces, outs, sems = refs[0], refs[1 : count + 1], refs[count + 1 : -1], refs[-1]
    started = []
    for number, (piece, row, rows, column, width, out, place) in enumerate(copies):
        start = place if isinstance(place, int) else spots_ref[place[0]] * place[1]
        start = pl.multiple_of(start, 16)
        copy = pltpu.make_async_copy(
            pieces[piece].at[pl.ds(row, rows), pl.ds(column, width)],
            outs[out].at[pl.ds(start, rows), :],
            sems.at[number],
        )
        copy.start()
        started.append(copy)
    for copy in started:
        copy.wait()


def assemble(spots, pieces, copies, shapes):
    return pl.pallas_call(
        functools.partial(assemble_kernel, copies, len(pieces)),
        in_specs=[SCALARS] + [ANYWHERE] * len(pieces),
        out_specs=[pl.BlockSpec(shape, lambda: (0, 0)) for shape in shapes],
        out_shape=[jax.ShapeDtypeStruct(shape, jnp.bfloat16) for shape in shapes],
        scratch_shapes=[pltpu.SemaphoreType.DMA((len(copies),))],
        compiler_params=pltpu.CompilerParams(vmem_limit_bytes=ROOM),
        cost_estimate=lasting(6),
        name="assemble",
    )(spots, *pieces)


def collect_kernel(copies, count, team_ref, *refs):
    pieces, (out_ref, sems) = refs[:count], refs[count:]
    width = out_ref.shape[1]
    started = []
    for number, (piece, row, block, team) in enumerate(copies):
        start = pl.multiple_of((block + team_ref[team]) * 16, 16)
        copy = pltpu.make_async_copy(
            pieces[piece].at[pl.ds(row, 16), pl.ds(pieces[piece].shape[1] - width, width)],
            out_ref.at[pl.ds(start, 16), :],
            sems.at[number],
        )
        copy.start()
        started.append(copy)
    for copy in started:
        copy.wait()


def collect_rows(teams, pieces, copies):
    return pl.pallas_call(
        functools.partial(collect_kernel, copies, len(pieces)),
        in_specs=[SCALARS] + [ANYWHERE] * len(pieces),
        out_specs=pl.BlockSpec((16 * len(copies), LANES), lambda: (0, 0)),
        out_shape=jax.ShapeDtypeStruct((16 * len(copies), LANES), jnp.bfloat16),
        scratch_shapes=[pltpu.SemaphoreType.DMA((len(copies),))],
        cost_estimate=lasting(3),
        name="collect",
    )(teams, *pieces)


def project_kernel(copies, count, rank, *refs):
    (team_ref, tokens_ref, gain_ref, gain_query_ref, gain_latent_ref, here_ref, low_ref, high_ref) = refs[:8]
    pieces = refs[8 : 8 + count]
    send_ref, raw_ref, input_ref, weights_ref, sems = refs[8 + count :]
    started = []
    for number, (piece, row, rows, block, team) in enumerate(copies):
        start = block if team is None else (block + team_ref[team]) * rows
        copy = pltpu.make_async_copy(
            pieces[piece].at[pl.ds(row, rows), :],
            weights_ref.at[pl.ds(pl.multiple_of(start, 16), rows), :],
            sems.at[number],
        )
        copy.start()
        started.append(copy)
    values = tokens_ref[...].astype(jnp.float32)
    input_ref[...] = normalize(values, gain_ref[...])[0].astype(jnp.bfloat16)
    for copy in started:
        copy.wait()
    raw = product(input_ref[...], weights_ref[...])
    raw_ref[...] = raw
    send_ref[:, :rank] = normalize(raw[:, :rank], gain_query_ref[...])[0].astype(jnp.bfloat16)
    send_ref[:, rank : rank + KVR] = normalize(
        raw[:, rank : rank + KVR], gain_latent_ref[...]
    )[0].astype(jnp.bfloat16)
    key = raw[:, rank + KVR :]
    send_ref[:, rank + KVR :] = (
        key * here_ref[...]
        + roll_lanes(key, -ROPE // 2) * low_ref[...]
        + roll_lanes(key, ROPE // 2) * high_ref[...]
    ).astype(jnp.bfloat16)


def project(teams, tokens, gains, tables, pieces, copies, rank):
    rows, width = tokens.shape
    out = rank + KVR + LANES
    low = jnp.bfloat16
    shapes = [((rows, out), low), ((rows, out), jnp.float32), ((rows, width), low), ((width, out), low)]
    return pl.pallas_call(
        functools.partial(project_kernel, copies, len(pieces), rank),
        in_specs=[SCALARS, full(tokens)]
        + [full(gain) for gain in gains]
        + [full(table) for table in tables]
        + [ANYWHERE] * len(pieces),
        out_specs=[pl.BlockSpec(shape, lambda: (0, 0)) for shape, _ in shapes],
        out_shape=[jax.ShapeDtypeStruct(*shape) for shape in shapes],
        scratch_shapes=[pltpu.SemaphoreType.DMA((len(copies),))],
        compiler_params=pltpu.CompilerParams(vmem_limit_bytes=ROOM),
        cost_estimate=lasting(10),
        name="project",
    )(teams, tokens, *gains, *tables, *pieces)


def joined(refs):
    if len(refs) == 1:
        return refs[0][...]
    return jnp.concatenate([ref[...] for ref in refs], axis=0)


def single_kernel(left_ref, *refs):
    refs[-1][...] = product(left_ref[...], joined(refs[:-1]))


def gate_kernel(count, last, left_ref, *refs):
    weights = joined(refs[:count])
    slope_ref, activated_ref, grads_ref = refs[count:]
    rows = left_ref.shape[0] // 2

    def work(width):
        for start in (0, rows):
            part = slice(start, start + rows)
            both = product(left_ref[part, :], weights[:, : 2 * width])
            gate, up = both[:, :width], both[:, width:]
            sigmoid = jax.nn.sigmoid(gate)
            swish = gate * sigmoid
            activated_ref[part, :width] = (swish * up).astype(jnp.bfloat16)
            upstream = slope_ref[part, :width]
            slope = sigmoid * (1.0 + gate * (1.0 - sigmoid))
            grads_ref[part, :width] = (upstream * up * slope).astype(jnp.bfloat16)
            grads_ref[part, width : 2 * width] = (upstream * swish).astype(jnp.bfloat16)
            rest = -width % LANES
            if rest:
                activated_ref[part, width : width + rest] = jnp.zeros((rows, rest), jnp.bfloat16)

    step, final = pl.program_id(0), pl.num_programs(0) - 1

    @pl.when(step < final)
    def _():
        work(TILE)

    @pl.when(step == final)
    def _():
        work(last)


TILE = 256


def piece_specs(pieces, width):
    return [pl.BlockSpec((piece.shape[0], width), lambda j: (0, j)) for piece in pieces]


def pair_columns(width):
    full_width = width
    if 2 * (width % TILE) % LANES:
        full_width = -(-width // LANES) * LANES
    return [
        (start, 2 * start, min(TILE, full_width - start), min(TILE, width - start))
        for start in range(0, full_width, TILE)
    ]


def paired_kernel(gate_ref, up_ref, out_ref):
    for start, place, size, real in pair_columns(gate_ref.shape[1]):
        for side, ref in enumerate((gate_ref, up_ref)):
            tile = ref[:, start : start + real]
            if real < size:
                rest = jnp.zeros((tile.shape[0], size - real), tile.dtype)
                tile = jnp.concatenate([tile, rest], axis=1)
            out_ref[:, place + side * size : place + (side + 1) * size] = tile


def paired(gate, up):
    width = sum(2 * size for _, _, size, _ in pair_columns(gate.shape[1]))
    shape = (gate.shape[0], width)
    return pl.pallas_call(
        paired_kernel,
        in_specs=[full(gate), full(up)],
        out_specs=pl.BlockSpec(shape, lambda: (0, 0)),
        out_shape=jax.ShapeDtypeStruct(shape, gate.dtype),
        compiler_params=pltpu.CompilerParams(vmem_limit_bytes=ROOM),
        cost_estimate=lasting(4),
        name="paired",
    )(gate, up)


def unpaired_kernel(own_ref, low_ref, high_ref, weights_ref, gate_ref, up_ref, sums_ref):
    sums = None
    for start, place, size, real in pair_columns(gate_ref.shape[1]):
        for side, out_ref in enumerate((gate_ref, up_ref)):
            part = slice(place + side * size, place + (side + 1) * size)
            total = own_ref[:, part].astype(jnp.float32) + low_ref[:, part].astype(jnp.float32)
            total = total + high_ref[:, part].astype(jnp.float32)
            out_ref[:, start : start + real] = total[:, :real]
            term = jnp.sum(total * weights_ref[:, part].astype(jnp.float32), axis=1, keepdims=True)
            sums = term if sums is None else sums + term
    sums_ref[...] = jnp.broadcast_to(sums, sums_ref.shape)


def unpaired(own, low, high, weights, width):
    rows = weights.shape[0]
    shapes = [(rows, width), (rows, width), (rows, LANES)]
    return pl.pallas_call(
        unpaired_kernel,
        grid=(1,),
        in_specs=[pl.BlockSpec(weights.shape, lambda _: (0, 0))] * 4,
        out_specs=[pl.BlockSpec(shape, lambda _: (0, 0)) for shape in shapes],
        out_shape=[jax.ShapeDtypeStruct(shape, jnp.float32) for shape in shapes],
        compiler_params=pltpu.CompilerParams(vmem_limit_bytes=ROOM),
        cost_estimate=lasting(5),
        name="unpaired",
    )(own, low, high, weights)


def feed_product(left, pieces):
    rows, width = left.shape[0], pieces[0].shape[1]
    return pl.pallas_call(
        single_kernel,
        grid=(pl.cdiv(width, TILE),),
        in_specs=[full(left)] + piece_specs(pieces, TILE),
        out_specs=pl.BlockSpec((rows, TILE), lambda j: (0, j)),
        out_shape=jax.ShapeDtypeStruct((rows, width), jnp.float32),
        compiler_params=pltpu.CompilerParams(vmem_limit_bytes=ROOM),
        cost_estimate=lasting(15),
        name="feed_product",
    )(left, *pieces)


def feed_gate(left, pieces, upstream):
    rows, width = upstream.shape
    pair_width = pieces[0].shape[1]
    column = lambda size: pl.BlockSpec((rows, size), lambda j: (0, j))
    return pl.pallas_call(
        functools.partial(gate_kernel, len(pieces), pair_width // 2 % TILE or TILE),
        grid=(pl.cdiv(width, TILE),),
        in_specs=[full(left)] + piece_specs(pieces, 2 * TILE) + [column(TILE)],
        out_specs=[column(TILE), column(2 * TILE)],
        out_shape=[
            jax.ShapeDtypeStruct((rows, width), jnp.bfloat16),
            jax.ShapeDtypeStruct((rows, pair_width), jnp.bfloat16),
        ],
        compiler_params=pltpu.CompilerParams(vmem_limit_bytes=ROOM),
        cost_estimate=lasting(26),
        name="feed_gate",
    )(left, *pieces, upstream)


def terms_kernel(count, *refs):
    arrays, out_ref = refs[: count + 1], refs[-4]
    left_ref, right_ref, sems = refs[-3:]
    rows = right_ref.shape[0] // count
    places = [left_ref]
    places += [right_ref.at[pl.ds(number * rows, rows), :] for number in range(count)]
    copies = [
        pltpu.make_async_copy(array, place, sems.at[number])
        for number, (array, place) in enumerate(zip(arrays, places))
    ]
    for copy in copies:
        copy.start()
    copies[0].wait()
    ready = 0
    for start in range(0, right_ref.shape[0], TILE):
        while ready * rows < min(start + TILE, right_ref.shape[0]):
            copies[ready + 1].wait()
            ready += 1
        part = slice(start, start + TILE)
        out_ref[:, part] = product_right(left_ref[...], right_ref[part, :]).astype(jnp.bfloat16)


def feed_terms(left, pieces, total, block, earlier=None, cost=lasting(18)):
    arrays = [left, *pieces]
    rows, width = left.shape
    columns = sum(piece.shape[0] for piece in pieces)
    low = jnp.bfloat16
    return pl.pallas_call(
        functools.partial(terms_kernel, len(pieces)),
        grid=(1,),
        in_specs=[ANYWHERE] * (len(arrays) + (earlier is not None)),
        out_specs=pl.BlockSpec((rows, columns), lambda _: (0, block)),
        out_shape=jax.ShapeDtypeStruct((rows, total), low),
        scratch_shapes=[
            pltpu.VMEM((rows, width), low),
            pltpu.VMEM((columns, width), low),
            pltpu.SemaphoreType.DMA((len(arrays),)),
        ],
        input_output_aliases={} if earlier is None else {len(arrays): 0},
        compiler_params=pltpu.CompilerParams(vmem_limit_bytes=ROOM),
        cost_estimate=cost,
        name="feed_terms",
    )(*arrays, *([] if earlier is None else [earlier]))


def latent_back_kernel(
    copies, rank, team_ref, back_ref, raw_ref, input_ref, gain_query_ref, gain_latent_ref,
    here_ref, low_ref, high_ref, *refs,
):
    outs, (grad_ref, held_ref, sems) = refs[:-3], refs[-3:]
    cuts = [(slice(0, rank), gain_query_ref), (slice(rank, rank + KVR), gain_latent_ref)]
    for part, gain_ref in cuts:
        values = raw_ref[:, part]
        inverse = normalize(values, gain_ref[...])[1]
        grad = normalize_back(
            values, inverse, gain_ref[...], back_ref[:, part].astype(jnp.float32)
        )
        grad_ref[:, part] = grad.astype(jnp.bfloat16)
    key = back_ref[:, rank + KVR :].astype(jnp.float32)
    grad_ref[:, rank + KVR :] = (
        key * here_ref[...]
        - roll_lanes(key, -ROPE // 2) * low_ref[...]
        - roll_lanes(key, ROPE // 2) * high_ref[...]
    ).astype(jnp.bfloat16)
    held_ref[...] = product_left(input_ref[...], grad_ref[...]).astype(jnp.bfloat16)
    started = []
    for number, (out, row, rows, block, team) in enumerate(copies):
        start = block if team is None else (block + team_ref[team]) * rows
        copy = pltpu.make_async_copy(
            held_ref.at[pl.ds(pl.multiple_of(start, 16), rows), :],
            outs[out].at[pl.ds(row, rows), :],
            sems.at[number],
        )
        copy.start()
        started.append(copy)
    for copy in started:
        copy.wait()


def latent_back(teams, back, raw, inputs, gains, tables, copies, heights, rank):
    rows, width = inputs.shape
    out = back.shape[1]
    low = jnp.bfloat16
    shapes = [((rows, out), low)]
    arrays = [back, raw, inputs, *gains, *tables]
    results = pl.pallas_call(
        functools.partial(latent_back_kernel, copies, rank),
        in_specs=[SCALARS] + [full(array) for array in arrays],
        out_specs=[ANYWHERE] * len(heights)
        + [pl.BlockSpec(shape, lambda: (0, 0)) for shape, _ in shapes],
        out_shape=[jax.ShapeDtypeStruct((height, out), low) for height in heights]
        + [jax.ShapeDtypeStruct(*shape) for shape in shapes],
        scratch_shapes=[pltpu.VMEM((width, out), low), pltpu.SemaphoreType.DMA((len(copies),))],
        compiler_params=pltpu.CompilerParams(vmem_limit_bytes=ROOM),
        cost_estimate=lasting(8),
        name="latent_back",
    )(teams, *arrays)
    return results[:-1], results[-1]


def head_sums_kernel(
    copies, rank, spots_ref, latents_ref, query_ref, key_value_ref, upstream_ref, heads_ref,
    out_ref, q_ref, kv_ref, o_ref, sems,
):
    q_ref[...] = product_left(latents_ref[:, :rank], query_ref[...]).astype(jnp.bfloat16)
    kv_ref[...] = product_left(latents_ref[:, rank : rank + KVR], key_value_ref[...]).astype(
        jnp.bfloat16
    )
    started = []

    def send(wanted):
        for number, (side, row, rows, place, column) in enumerate(copies):
            if side not in wanted:
                continue
            start = row if isinstance(row, int) else spots_ref[row[0]] * rows
            held = (q_ref, kv_ref, o_ref)[side]
            copy = pltpu.make_async_copy(
                held.at[pl.ds(pl.multiple_of(start, 16), rows), :],
                out_ref.at[pl.ds(place, rows), pl.ds(column, held.shape[1])],
                sems.at[number],
            )
            copy.start()
            started.append(copy)

    send((0, 1))
    o_ref[...] = product_left(upstream_ref[...], heads_ref[...]).astype(jnp.bfloat16)
    send((2,))
    for copy in started:
        copy.wait()


def head_sums(spots, latents, query, key_value, upstream, heads, rank, query_rows, latent_rows, out_rows):
    width, out_width = query.shape[1], heads.shape[1]
    count = spots.shape[0]
    rows = query_rows + latent_rows + out_rows // 2
    copies = []
    for spot in range(count):
        start = spot * rows
        copies.append((0, (spot,), query_rows, start, 0))
        copies.append((1, (spot,), latent_rows, start + query_rows, 0))
        for side in (0, 1):
            copies.append(
                (2, spot * out_rows + side * (out_rows // 2), out_rows // 2,
                 start + query_rows + latent_rows, side * out_width)
            )
    low = jnp.bfloat16
    arrays = [latents, query, key_value, upstream, heads]
    return pl.pallas_call(
        functools.partial(head_sums_kernel, copies, rank),
        in_specs=[SCALARS] + [full(array) for array in arrays],
        out_specs=pl.BlockSpec((count * rows, width), lambda: (0, 0)),
        out_shape=jax.ShapeDtypeStruct((count * rows, width), low),
        scratch_shapes=[
            pltpu.VMEM((rank, width), low),
            pltpu.VMEM((KVR, width), low),
            pltpu.VMEM((upstream.shape[1], out_width), low),
            pltpu.SemaphoreType.DMA((len(copies),)),
        ],
        compiler_params=pltpu.CompilerParams(vmem_limit_bytes=ROOM),
        cost_estimate=lasting(20),
        name="head_sums",
    )(spots, *arrays)


def token_back_kernel(grad_ref, weights_ref, tokens_ref, hidden_ref, gain_ref, out_ref):
    upstream = product_right(grad_ref[...], weights_ref[...])
    values = tokens_ref[...].astype(jnp.float32)
    inverse = normalize(values, gain_ref[...])[1]
    out_ref[...] = hidden_ref[...] + normalize_back(values, inverse, gain_ref[...], upstream)


def token_back(grad, weights, tokens, hidden_grad, gain):
    arrays = [grad, weights, tokens, hidden_grad, gain]
    return pl.pallas_call(
        token_back_kernel,
        in_specs=[full(array) for array in arrays],
        out_specs=full(hidden_grad),
        out_shape=jax.ShapeDtypeStruct(hidden_grad.shape, jnp.float32),
        compiler_params=pltpu.CompilerParams(vmem_limit_bytes=ROOM),
        cost_estimate=lasting(8),
        name="token_back",
    )(*arrays)


def reorder_kernel(spots_ref, in_ref, out_ref):
    width = in_ref.shape[1]
    count = spots_ref.shape[0]
    size = width // count
    window = min(-(-(size + LANES - 1) // LANES) * LANES, width)
    for place in range(count):
        start = spots_ref[place] * size
        base = jnp.minimum(start // LANES * LANES, width - window)
        held = in_ref[:, pl.ds(pl.multiple_of(base, LANES), window)].astype(jnp.float32)
        held = pltpu.roll(held, lax.rem(window - (start - base), window), 1)
        out_ref[:, place * size : (place + 1) * size] = held[:, :size].astype(out_ref.dtype)


def reorder(values, spots):
    return pl.pallas_call(
        reorder_kernel,
        in_specs=[SCALARS, full(values)],
        out_specs=full(values),
        out_shape=jax.ShapeDtypeStruct(values.shape, values.dtype),
        compiler_params=pltpu.CompilerParams(vmem_limit_bytes=ROOM),
        cost_estimate=lasting(4),
        name="reorder",
    )(spots, values)


class Ring:
    def __init__(self, axis):
        self.axis = axis
        self.count = lax.axis_size(axis)
        self.half = self.count // 2
        order = list(range(0, self.count, 2)) + list(range(self.count - 1, 0, -2))
        self.me = lax.axis_index(axis)
        self.spot = self.place(self.me)
        indices = jnp.arange(self.count, dtype=jnp.int32)
        self.ahead = self.owner(indices)
        self.behind = lax.rem(self.place(indices) - self.spot + self.count, self.count)
        self.up = [(order[i], order[(i + 1) % self.count]) for i in range(self.count)]
        self.down = [(b, a) for a, b in self.up]

    def place(self, index):
        return jnp.where(index % 2 == 0, index // 2, self.count - (index + 1) // 2)

    def owner(self, step):
        spot = lax.rem(self.spot + step + self.count, self.count)
        return jnp.where(spot < self.half, 2 * spot, 2 * self.count - 1 - 2 * spot)

    def send_up(self, block):
        return lax.ppermute(block, self.axis, self.up)

    def send_down(self, block):
        return lax.ppermute(block, self.axis, self.down)


class Gather:
    def __init__(self, ring, shard):
        self.ring = ring
        self.rows = shard.shape[0]
        self.low = self.high = shard
        self.blocks = {0: shard}
        self.step = 0

    def advance(self):
        ring = self.ring
        if self.done:
            return
        self.step += 1
        if self.step < ring.half:
            self.low = ring.send_up(self.low)
            self.high = ring.send_down(self.high)
            self.blocks[self.step] = self.high
            self.blocks[ring.count - self.step] = self.low
        else:
            cut = self.rows // 2
            self.low = ring.send_up(self.low[:cut])
            self.high = ring.send_down(self.high[cut:])
            self.blocks[ring.half] = None

    @property
    def done(self):
        return self.step >= self.ring.half

    def finish(self):
        while not self.done:
            self.advance()
        self.blocks[self.ring.half] = jnp.concatenate([self.low, self.high], axis=0)
        return [self.blocks[spot] for spot in range(self.ring.count)]


class Scatter:
    def __init__(self, ring, take, rows):
        self.ring = ring
        self.take = lambda step, start, size: take(step % ring.count, start, size)
        self.rows = rows
        self.step = 0
        self.low = self.high = None

    def add(self, a, b):
        return (a.astype(jnp.float32) + b.astype(jnp.float32)).astype(b.dtype)

    def advance(self):
        ring, rows, cut = self.ring, self.rows, self.rows // 2
        if self.done:
            return
        ahead = ring.half - self.step
        if self.step:
            self.low, self.high = lax.optimization_barrier((self.low, self.high))
        self.step += 1
        if ahead == ring.half:
            low = self.take(ahead, 0, cut)
            high = self.take(ahead, cut, rows - cut)
        elif ahead == ring.half - 1:
            low = self.take(ahead, 0, rows)
            high = self.take(-ahead, 0, rows)
            low = jnp.concatenate([self.add(self.low, low[:cut]), low[cut:]], axis=0)
            high = jnp.concatenate([high[:cut], self.add(self.high, high[cut:])], axis=0)
        else:
            low = self.add(self.low, self.take(ahead, 0, rows))
            high = self.add(self.high, self.take(-ahead, 0, rows))
        self.sent = (low, high)
        self.low = ring.send_up(low)
        self.high = ring.send_down(high)

    @property
    def done(self):
        return self.step >= self.ring.half

    def finish(self):
        while not self.done:
            self.advance()
        own = self.take(0, 0, self.rows).astype(jnp.float32)
        return own + self.low.astype(jnp.float32) + self.high.astype(jnp.float32)


def stacked(ring, grads):
    rows = grads.shape[0] // ring.count

    def take(spot, start, size):
        return lax.slice_in_dim(grads, spot * rows + start, spot * rows + start + size, axis=0)

    return Scatter(ring, take, rows)


def staged(ring, left, right):
    size = left.shape[1] // ring.count
    low, high = ring.count // 4, ring.count // 4 + ring.half
    parts = {}
    held = [right]

    def take(spot, start, rows):
        name = 1 if low <= spot < high else 0 if spot < low else 2
        first = (0, low, high)[name]
        if name not in parts:
            last = (low, high, ring.count)[name]
            columns = lax.slice_in_dim(left, first * size, last * size, axis=1)
            parts[name] = product_left(columns, held[0]).astype(jnp.bfloat16)
        begin = (spot - first) * size + start
        return lax.slice_in_dim(parts[name], begin, begin + rows, axis=0)

    scatter = Scatter(ring, take, size)
    scatter.held = held
    scatter.parts = parts
    return scatter


def delay(scatter, *others):
    scatter.held[0] = follow(scatter.held[0], *others)


def follow(values, *others):
    return lax.optimization_barrier((values, others))[0]


def ends(*streams):
    return [(stream.low, stream.high) for stream in streams]


def hold(stream, *others):
    stream.low, stream.high = follow((stream.low, stream.high), *others)


def swap(values, bit):
    count = lax.axis_size("tensor")
    return lax.ppermute(values, "tensor", [(i, i ^ bit) for i in range(count)])


def pad_heads(weights, heads):
    rows = weights.shape[0]
    width = weights.shape[1] // heads
    padded = jnp.pad(weights.reshape(rows, heads, width), ((0, 0), (0, 0), (0, LANES - width)))
    return padded.reshape(rows, heads * LANES)


def on_device(
    tokens,
    segments,
    positions,
    norm_input,
    norm_query,
    norm_latent,
    norm_hidden,
    query_down,
    latent_down,
    query_up,
    latent_up,
    attention_out,
    gate_weight,
    up_weight,
    down_weight,
    cotangent,
):
    low = jnp.bfloat16
    local_rows = tokens.shape[0]
    shard = lax.axis_index("tensor")
    offset = shard * local_rows
    length = segments.shape[0]
    local_heads = HEADS // lax.axis_size("tensor")
    pairs = local_heads // 2
    rank = query_down.shape[1]
    ring = Ring("fsdp")
    everyone = lax.axis_size("fsdp") * lax.axis_size("tensor")
    teams = lax.axis_size("tensor")
    gains_own = jnp.concatenate([norm_input, norm_hidden, norm_query, norm_latent])
    gain_sizes = [norm_input.shape[0], norm_hidden.shape[0], norm_query.shape[0], norm_latent.shape[0]]
    gain_width = -(-gains_own.shape[0] // LANES) * LANES
    spare = LANES - NOPE - ROPE
    gain_rows = -(-gains_own.shape[0] // spare)
    down_rows = query_down.shape[0]
    down_width = rank + KVR + LANES
    gain_part = jnp.pad(gains_own, (0, gain_rows * spare - gains_own.shape[0]))
    gain_part = jnp.pad(gain_part.reshape(gain_rows, spare), ((0, down_rows - gain_rows), (0, 0)))
    packed = jnp.concatenate(
        [
            query_down,
            latent_down[:, :KVR],
            jnp.zeros((down_rows, NOPE), low),
            latent_down[:, KVR:],
            gain_part,
        ],
        axis=1,
    )
    feed_width = gate_weight.shape[1]
    feed_rows = gate_weight.shape[0]
    feed_pad = -feed_width % LANES
    widen = lambda weights: jnp.pad(weights, ((0, 0), (0, feed_pad)))
    head_width = 2 * pairs * LANES
    query_rows, latent_rows, out_rows = query_up.shape[0], latent_up.shape[0], attention_out.shape[1]
    out_width = attention_out.shape[0]
    out_t = attention_out.T
    mixed = jnp.concatenate(
        [
            pad_heads(query_up, local_heads),
            latent_up,
            jnp.concatenate([out_t[: out_rows // 2], out_t[out_rows // 2 :]], axis=1),
        ],
        axis=0,
    )
    mixed_up = Gather(ring, mixed)
    down_up = Gather(ring, widen(down_weight.T))
    pair_own = paired(gate_weight, up_weight)
    pair_up = Gather(ring, pair_own)

    tokens_ring = reorder(tokens, ring.ahead)
    upstream = reorder(cotangent, ring.ahead)
    here, turn_low, turn_high = rotary_lanes(positions)
    tables = (here, turn_low, turn_high)
    local_tables = [lax.dynamic_slice_in_dim(table, offset, local_rows) for table in tables]
    query_feat, key_feat = segment_lanes(segments)
    key_feat = key_feat.astype(low)
    ahead, behind = ring.ahead, ring.behind
    team_ids = shard ^ jnp.asarray([0, 2, 1, 3], jnp.int32)

    small_up = Gather(ring, jnp.concatenate([packed, swap(packed, 2)], axis=0))
    pieces, copies = [], []

    def collect(block, spot, team):
        for first, piece in ((team, block), (team + 2, swap(block, 1))):
            for part in range(block.shape[0] // down_rows):
                copies.append(
                    (len(pieces), part * down_rows, down_rows, spot * teams, first + part)
                )
            pieces.append(piece)

    collect(small_up.low, 0, 0)
    mixed_up.advance()
    while not small_up.done:
        swapped = pieces[1::2]
        small_up.advance()
        mixed_up.advance()
        if not small_up.done:
            collect(small_up.high, small_up.step, 0)
            collect(small_up.low, ring.count - small_up.step, 0)
            hold(small_up, ends(mixed_up), swapped)
            hold(mixed_up, ends(small_up))
    collect(small_up.low, ring.half, 0)
    collect(small_up.high, ring.half, 1)
    hold(down_up, ends(mixed_up, small_up))
    down_up.advance()
    if down_rows % 16:
        table = [[None] * teams for _ in range(ring.count)]
        for piece, row, _, block, team in copies:
            table[block // teams][team] = pieces[piece][row : row + gain_rows, down_width - spare :]
        table = jnp.stack([part for group in zip(*table) for part in group])
        table = table.reshape(teams, ring.count, gain_rows * spare)
        places = shard ^ jnp.arange(teams, dtype=jnp.int32)
        places = jnp.where(places == 1, 2, jnp.where(places == 2, 1, places))
        table = jnp.take(table, places, axis=0)
    else:
        table = collect_rows(
            team_ids, pieces, [(piece, row, block, team) for piece, row, _, block, team in copies]
        )
        table = table.reshape(ring.count, teams, 16, LANES)[:, :, :gain_rows, LANES - spare :]
        table = jnp.transpose(table, (1, 0, 2, 3)).reshape(teams, ring.count, gain_rows * spare)
    table = table.astype(jnp.float32)
    gain_parts = []
    start = 0
    for number, size in enumerate(gain_sizes):
        part = jnp.transpose(table[:, :, start : start + size], (1, 0, 2))
        if number >= 2:
            part = jnp.take(part, behind, axis=0)
        gain_parts.append(part.reshape(1, -1))
        start += size
    gain_in, gain_hidden, gain_query, gain_latent = gain_parts
    if down_rows % 16:
        whole = jnp.zeros((everyone * down_rows, down_width), low)
        for piece, row, rows, block, team in copies:
            whole = lax.dynamic_update_slice(
                whole, pieces[piece][row : row + rows], ((block + team_ids[team]) * rows, 0)
            )
        pieces, copies = [whole], [(0, 0, whole.shape[0], 0, None)]
    latent_send, latent_raw, attention_input, down_projections = project(
        team_ids, tokens_ring, (gain_in, gain_query, gain_latent), local_tables, pieces, copies, rank
    )
    latent_send = follow(latent_send, ends(down_up))
    latents = lax.all_gather(latent_send, "tensor", axis=0, tiled=True)
    hold(down_up, latent_send)
    down_up.advance()
    latents = follow(latents, ends(down_up))
    hold(pair_up, ends(down_up))
    mixed_blocks = mixed_up.finish()
    if query_rows % 16 or latent_rows % 16 or out_rows % 32:
        mixed_all = jnp.stack([mixed_blocks[0]] * ring.count)
        for spot, block in enumerate(mixed_blocks):
            mixed_all = lax.dynamic_update_slice(mixed_all, block[None], (ring.owner(spot), 0, 0))
        wq = mixed_all[:, :query_rows].reshape(-1, head_width)
        wkv = mixed_all[:, query_rows : query_rows + latent_rows].reshape(-1, head_width)
        outs = [block[query_rows + latent_rows :] for block in mixed_blocks]
        attention_out_t = jnp.concatenate(
            [block[:, side * out_width : (side + 1) * out_width] for block in outs for side in (0, 1)],
            axis=0,
        )
    else:
        copies = []
        for spot in range(ring.count):
            copies.append((spot, 0, query_rows, 0, head_width, 0, (spot, query_rows)))
            copies.append((spot, query_rows, latent_rows, 0, head_width, 1, (spot, latent_rows)))
            for side in (0, 1):
                copies.append(
                    (spot, query_rows + latent_rows, out_rows // 2, side * out_width, out_width, 2,
                     spot * out_rows + side * (out_rows // 2))
                )
        wq, wkv, attention_out_t = assemble(
            ahead,
            mixed_blocks,
            copies,
            [(ring.count * query_rows, head_width), (ring.count * latent_rows, head_width),
             (ring.count * out_rows, out_width)],
        )
    down_up.advance()
    pair_up.advance()
    feed_upstream = follow(RESIDUAL * upstream.astype(jnp.float32), latents).astype(low)
    feed_upstream = lax.all_gather(feed_upstream, "tensor", axis=0, tiled=True)
    rope = latents[:, rank + KVR :] + key_feat
    heads, query_heads, key_value, log_totals = attention_forward(
        latents, wq, wkv, rope, query_feat, tables, pairs
    )
    branch_terms = product_right(heads, attention_out_t).astype(low)
    branch_terms = follow(branch_terms, feed_upstream, ends(pair_up))
    attention_branch = lax.psum_scatter(branch_terms, "tensor", scatter_dimension=0, tiled=True)
    attention_branch = follow(attention_branch, ends(down_up))
    downs = down_up.finish()
    if ring.count > 8:
        downs = [jnp.concatenate(downs, axis=0)]
    activated_grad = feed_product(feed_upstream, downs)
    hidden = tokens_ring.astype(jnp.float32) + RESIDUAL * attention_branch.astype(jnp.float32)
    feed_normed, inverse_hidden = normalize(hidden, gain_hidden)
    pair_up.advance()
    feed_normed = follow(feed_normed.astype(low), ends(pair_up))
    feed_seq = lax.all_gather(feed_normed, "tensor", axis=0, tiled=True)
    hold(pair_up, ends(down_up))
    pair_up.advance()
    hold(pair_up, activated_grad)
    weights = pair_up.finish()
    if ring.count > 8:
        weights = [jnp.concatenate(weights, axis=0)]
    activated, pair_grad = feed_gate(feed_seq, weights, activated_grad)

    grad_down = staged(ring, feed_upstream, activated)
    grad_down.advance()
    grad_pair = staged(ring, feed_seq, follow(pair_grad, grad_down.sent))
    grad_pair.advance()
    hold(grad_down, grad_pair.sent)
    grad_down.advance()
    half = max(len(weights) // 2, 1)
    width = feed_seq.shape[1]
    pair_grad = follow(pair_grad, grad_down.sent)
    terms = feed_terms(pair_grad, weights[:half], width, 0)
    hold(grad_pair, terms)
    grad_pair.advance()
    if len(weights) > half:
        terms = follow(terms, grad_pair.sent)
        terms = feed_terms(pair_grad, weights[half:], width, 1, terms)
    terms = follow(terms, ends(grad_down))
    feed_back = lax.psum_scatter(terms, "tensor", scatter_dimension=0, tiled=True)
    activated = follow(activated, terms)
    feed_branch = feed_terms(activated, downs[:half], width, 0, None, lasting(11))
    delay(grad_down, terms)
    hold(grad_down, terms)
    grad_down.advance()
    feed_back = follow(feed_back, grad_down.sent)
    delay(grad_pair, grad_down.sent)
    grad_pair.advance()
    grad_pair.take(0, 0, 1), grad_down.take(0, 0, 1)
    feed_back = follow(feed_back, grad_pair.parts[0], grad_down.parts[0], feed_branch)
    hidden_back = normalize_back(
        hidden, inverse_hidden, gain_hidden, feed_back.astype(jnp.float32)
    )
    hidden_grad = upstream.astype(jnp.float32) + hidden_back
    upstream_send = follow((RESIDUAL * hidden_grad).astype(low), grad_pair.sent, ends(grad_down))
    attention_upstream = lax.all_gather(upstream_send, "tensor", axis=0, tiled=True)
    attention_upstream = follow(attention_upstream, ends(grad_pair))
    heads_grad = product(attention_upstream, attention_out_t).astype(low)
    grad_pair.advance()
    heads_grad = follow(heads_grad, grad_pair.sent)
    query_raw_grad, key_value_grad, key_rope_grad = attention_backward(
        query_heads, key_value, heads_grad, log_totals, rope, tables
    )
    query_raw_grad, key_value_grad = follow((query_raw_grad, key_value_grad), ends(grad_pair))
    hold(grad_down, query_raw_grad)
    grad_down.advance()
    latent_terms = jnp.concatenate(
        [
            product_right(query_raw_grad, wq),
            product_right(key_value_grad, wkv),
            key_rope_grad,
        ],
        axis=1,
    ).astype(low)
    latent_grad = lax.psum_scatter(latent_terms, "tensor", scatter_dimension=0, tiled=True)
    upstream_late, query_raw_grad, key_value_grad = follow(
        (attention_upstream, query_raw_grad, key_value_grad), latent_terms, grad_down.sent
    )
    if query_rows % 16 or latent_rows % 16 or out_rows % 32:
        sums = [
            jnp.take(product_left(left, right).astype(low).reshape(ring.count, -1, head_width), ahead, axis=0)
            for left, right in (
                (latents[:, :rank], query_raw_grad),
                (latents[:, rank : rank + KVR], key_value_grad),
            )
        ]
        out_sums = product_left(upstream_late, heads).astype(low)
        out_sums = out_sums.reshape(ring.count, 2, out_rows // 2, out_width)
        sums.append(jnp.concatenate([out_sums[:, 0], out_sums[:, 1]], axis=2))
        mixed_sums = jnp.concatenate(sums, axis=1).reshape(-1, head_width)
    else:
        mixed_sums = head_sums(
            ahead, latents, query_raw_grad, key_value_grad, upstream_late, heads,
            rank, query_rows, latent_rows, out_rows,
        )
    grad_mixed = stacked(ring, follow(mixed_sums, ends(grad_down)))
    grad_mixed.advance()
    if len(downs) > half:
        activated = follow(activated, grad_mixed.sent)
        feed_branch = feed_terms(activated, downs[half:], width, 1, feed_branch, lasting(11))
    latent_grad = follow(latent_grad, ends(grad_mixed), feed_branch)
    feed_branch = lax.psum_scatter(feed_branch, "tensor", scatter_dimension=0, tiled=True)
    pair = 2 * down_rows
    height = ring.count * pair
    heights = [height, height]
    copies = [
        (team // 2, spot * pair + (team % 2) * down_rows, down_rows, spot * teams, team)
        for spot in range(ring.count)
        for team in range(teams)
    ]
    aligned = down_rows % 16 == 0
    if not aligned:
        copies, heights = [(0, 0, 2 * height, 0, None)], [2 * height]
    sent, latent_low = latent_back(
        team_ids, latent_grad, latent_raw, attention_input, (gain_query, gain_latent),
        local_tables, copies, heights, rank,
    )
    if not aligned:
        blocks = jnp.take(
            sent[0].reshape(ring.count, teams, down_rows, down_width), team_ids, axis=1
        )
        sent = [blocks[:, :2].reshape(height, -1), blocks[:, 2:].reshape(height, -1)]

    def add_low(a, b):
        return (a.astype(jnp.float32) + b.astype(jnp.float32)).astype(low)

    other_sums = swap(sent[1], 1)
    hold(grad_mixed, latent_low)
    grad_mixed.advance()
    token_grad = token_back(
        latent_low, down_projections, tokens_ring, hidden_grad, gain_in
    )
    other_sums = follow(other_sums, token_grad)
    grad_small = stacked(ring, add_low(sent[0], other_sums))
    grad_small.advance()
    hold(grad_mixed, grad_small.sent)
    grad_mixed.advance()
    grad_small.advance()
    token_grad = reorder(follow(token_grad, grad_small.sent), ring.behind)
    hold(grad_mixed, grad_small.sent)
    hold(grad_down, ends(grad_small))
    hold(grad_small, token_grad)
    grad_small.advance()
    hold(grad_pair, grad_small.sent)
    grad_mixed.advance()
    grad_small.advance()
    feed_branch = follow(feed_branch, grad_small.sent)
    output = hidden + RESIDUAL * feed_branch.astype(jnp.float32)
    output = reorder(output.astype(low), ring.behind)
    small_own = grad_small.finish()
    small_other = follow(small_own[down_rows:].astype(low), ends(grad_mixed), output)
    packed_own = small_own[:down_rows] + swap(small_other, 2).astype(jnp.float32)
    rope_from = rank + KVR + NOPE
    lanes = jnp.arange(down_width) < rope_from + ROPE
    grad_gain_input = jnp.sum(
        jnp.where(lanes, packed.astype(jnp.float32) * packed_own, 0.0), axis=1
    ) / norm_input.astype(jnp.float32)
    grad_mixed_own = grad_mixed.finish()
    while not grad_pair.done:
        grad_pair.advance()
    grad_query_own = grad_mixed_own[:query_rows].reshape(query_rows, local_heads, LANES)
    grad_out_own = grad_mixed_own[query_rows + latent_rows :]
    grad_out_own = jnp.concatenate(
        [grad_out_own[:, :out_width], grad_out_own[:, out_width:]], axis=0
    )
    grad_gate_own, grad_up_own, pair_sums = unpaired(
        grad_pair.parts[0], grad_pair.low, grad_pair.high, pair_own, feed_width
    )
    row_sums = lambda weights, grads: jnp.sum(weights.astype(jnp.float32) * grads, axis=1)
    head_rows = query_rows + latent_rows
    gain_sums = jnp.concatenate(
        [pair_sums[:, 0], row_sums(mixed[:head_rows], grad_mixed_own[:head_rows])]
    )
    gain_sums = jnp.pad(gain_sums, (0, -gain_sums.shape[0] % LANES))[None]
    gain_sums = follow(gain_sums, small_other)
    gain_sums = gain_sums + swap(gain_sums, 1)
    gain_sums = (gain_sums + swap(gain_sums, 2))[0]
    gain_grads = []
    start = 0
    for gain in (norm_hidden, norm_query, norm_latent):
        size = gain.shape[0]
        own = lax.dynamic_slice_in_dim(gain_sums, start + shard * size, size)
        gain_grads.append(own / gain.astype(jnp.float32))
        start += size * teams
    return (
        output,
        token_grad,
        grad_gain_input,
        gain_grads[1],
        gain_grads[2],
        gain_grads[0],
        packed_own[:, :rank],
        jnp.concatenate(
            [packed_own[:, rank : rank + KVR], packed_own[:, rope_from : rope_from + ROPE]],
            axis=1,
        ),
        grad_query_own[:, :, : NOPE + ROPE].reshape(query_rows, -1),
        grad_mixed_own[query_rows : query_rows + latent_rows],
        grad_out_own.T,
        grad_gate_own,
        grad_up_own,
        grad_down.finish()[:, :feed_width].T,
    )


def solution(mesh):
    return jax.shard_map(
        on_device,
        mesh=mesh,
        in_specs=(
            P(("fsdp", "tensor"), None),
            P("fsdp"),
            P("fsdp"),
            P(("fsdp", "tensor")),
            P(("fsdp", "tensor")),
            P(("fsdp", "tensor")),
            P(("fsdp", "tensor")),
            P(("fsdp", "tensor"), None),
            P(("fsdp", "tensor"), None),
            P("fsdp", "tensor"),
            P("fsdp", "tensor"),
            P("tensor", "fsdp"),
            P("fsdp", "tensor"),
            P("fsdp", "tensor"),
            P("tensor", "fsdp"),
            P(("fsdp", "tensor"), None),
        ),
        out_specs=(
            P(("fsdp", "tensor"), None),
            P(("fsdp", "tensor"), None),
            P(("fsdp", "tensor")),
            P(("fsdp", "tensor")),
            P(("fsdp", "tensor")),
            P(("fsdp", "tensor")),
            P(("fsdp", "tensor"), None),
            P(("fsdp", "tensor"), None),
            P("fsdp", "tensor"),
            P("fsdp", "tensor"),
            P("tensor", "fsdp"),
            P("fsdp", "tensor"),
            P("fsdp", "tensor"),
            P("tensor", "fsdp"),
        ),
        check_vma=False,
    )
```

```python
import functools
import math

import jax
import jax.numpy as jnp
from jax import lax
from jax.experimental import pallas as pl
from jax.experimental.pallas import tpu as pltpu
from jax.sharding import PartitionSpec as P

HEADS = 40
NOPE = 64
ROPE = 32
VDIM = 64
KVR = 256
LANES = 128
BLOCK = 256


EPSILON = 1e-05
RESIDUAL = 1.4 / math.sqrt(62.0)
NEGATIVE = -1e30
APART = -(2.0**96)
SCALE = 1.0 / math.sqrt(NOPE + ROPE)
LOG2E = math.log2(math.e)
ROOM = 56 * 1024 * 1024
BRIEF = pl.CostEstimate(flops=1, bytes_accessed=1, transcendentals=0)


def lasting(microseconds):
    return pl.CostEstimate(flops=1, bytes_accessed=microseconds * 3 * 10**6, transcendentals=0)


def normalize(values, gain):
    inverse = lax.rsqrt(jnp.mean(values * values, axis=-1, keepdims=True) + EPSILON)
    return (values * inverse * gain, inverse)


def normalize_back(values, inverse, gain, upstream):
    scaled = upstream * gain
    inner = jnp.mean(scaled * values, axis=-1, keepdims=True)
    return inverse * scaled - values * (inverse * inverse * inverse) * inner


def product(left, right):
    return jnp.dot(left, right, preferred_element_type=jnp.float32)


def product_left(left, right):
    return lax.dot_general(
        left, right, (((0,), (0,)), ((), ())), preferred_element_type=jnp.float32
    )


def product_right(left, right):
    return lax.dot_general(
        left, right, (((1,), (1,)), ((), ())), preferred_element_type=jnp.float32
    )


def rotary_lanes(positions):
    lane = jnp.arange(LANES, dtype=jnp.int32)
    steps = ((lane - NOPE) % (ROPE // 2)).astype(jnp.float32)
    frequency = jnp.exp(steps * (-2.0 * math.log(10000.0) / ROPE))
    angles = positions.astype(jnp.float32)[:, None] * frequency[None, :]
    first = ((lane >= NOPE) & (lane < NOPE + ROPE // 2))[None, :]
    second = ((lane >= NOPE + ROPE // 2) & (lane < NOPE + ROPE))[None, :]
    cosine = jnp.cos(angles)
    sine = jnp.sin(angles)
    here = jnp.where((lane < NOPE)[None, :], 1.0, jnp.where(first | second, cosine, 0.0))
    return (here, jnp.where(first, -sine, 0.0), jnp.where(second, sine, 0.0))


def segment_lanes(segment_ids):
    lane = jnp.arange(LANES, dtype=jnp.int32) - (NOPE + ROPE)
    same = lane[None, :] == segment_ids[:, None]
    used = ((lane >= 0) & (lane < 4))[None, :]
    query = jnp.where(used & same, 1.0, 0.0)
    key = jnp.where(used & ~same, APART, 0.0)
    return (query, key)


def roll_lanes(values, amount):
    return pltpu.roll(values, amount % LANES, 1)


def forward_kernel(
    xq_ref, lat_ref, wq_ref, wkv_ref, rope_ref, feat_ref, here_ref, low_ref, high_ref,
    out_ref, q_ref, kv_ref, lse_ref, k_ref,
):
    length = xq_ref.shape[0]
    lane = lax.broadcasted_iota(jnp.int32, (BLOCK, LANES), 1)
    causal = lax.broadcasted_iota(jnp.int32, (BLOCK, BLOCK), 1) <= lax.broadcasted_iota(
        jnp.int32, (BLOCK, BLOCK), 0
    )
    blocks = [slice(start, start + BLOCK) for start in range(0, length, BLOCK)]
    for rows in blocks:
        q_raw = product(xq_ref[rows, :], wq_ref[...])
        kv_ref[rows, :] = product(lat_ref[rows, :], wkv_ref[...]).astype(jnp.bfloat16)
        for head in range(2):
            part = slice(head * LANES, (head + 1) * LANES)
            raw = q_raw[:, part]
            turned = (
                raw * here_ref[rows, :]
                + roll_lanes(raw, -ROPE // 2) * low_ref[rows, :]
                + roll_lanes(raw, ROPE // 2) * high_ref[rows, :]
                + feat_ref[rows, :]
            )
            q_ref[rows, part] = turned.astype(jnp.bfloat16)
            k_ref[head, rows, :] = jnp.where(lane < NOPE, kv_ref[rows, part], rope_ref[rows, :])
    for rows in blocks:
        results = []
        for head in range(2):
            part = slice(head * LANES, (head + 1) * LANES)
            query = q_ref[rows, part]
            near = product_right(query, k_ref[head, rows, :])
            near = jnp.where(causal, near, NEGATIVE)
            top = jnp.max(near, axis=1, keepdims=True)
            if rows.start:
                far = product_right(query, k_ref[head, : rows.start, :])
                top = jnp.maximum(top, jnp.max(far, axis=1, keepdims=True))
            weights = jnp.exp2((near - top) * (SCALE * LOG2E))
            total = jnp.sum(weights, axis=1, keepdims=True)
            result = product(weights.astype(jnp.bfloat16), kv_ref[rows, part])
            if rows.start:
                weights = jnp.exp2((far - top) * (SCALE * LOG2E))
                total = total + jnp.sum(weights, axis=1, keepdims=True)
                result = result + product(
                    weights.astype(jnp.bfloat16), kv_ref[: rows.start, part]
                )
            results.append(result / total)
            log_total = top * (SCALE * LOG2E) + jnp.log2(total)
            lse_ref[0, head : head + 1, rows] = jnp.transpose(
                jnp.broadcast_to(log_total, (BLOCK, LANES))
            )[0:1, :]
        out_ref[rows, :] = jnp.where(
            lane < VDIM, roll_lanes(results[0], VDIM), results[1]
        ).astype(jnp.bfloat16)


def attention_forward(latents, wq, wkv, rope, feat, tables, pairs):
    length = latents.shape[0]
    rank = wq.shape[0]
    whole = lambda width, at=0: pl.BlockSpec((length, width), lambda j: (0, at))
    mine = lambda width: pl.BlockSpec((length, width), lambda j: (0, j))
    tall = lambda rows: pl.BlockSpec((rows, 2 * LANES), lambda j: (0, j))
    low = jnp.bfloat16
    return pl.pallas_call(
        forward_kernel,
        grid=(pairs,),
        in_specs=[
            whole(rank), whole(KVR, rank // KVR), tall(rank), tall(KVR),
            whole(LANES), whole(LANES), whole(LANES), whole(LANES), whole(LANES),
        ],
        out_specs=[
            mine(LANES), mine(2 * LANES), mine(2 * LANES),
            pl.BlockSpec((1, 2, length), lambda j: (j, 0, 0)),
        ],
        out_shape=[
            jax.ShapeDtypeStruct((length, pairs * LANES), low),
            jax.ShapeDtypeStruct((length, pairs * 2 * LANES), low),
            jax.ShapeDtypeStruct((length, pairs * 2 * LANES), low),
            jax.ShapeDtypeStruct((pairs, 2, length), jnp.float32),
        ],
        scratch_shapes=[pltpu.VMEM((2, length, LANES), low)],
        compiler_params=pltpu.CompilerParams(vmem_limit_bytes=ROOM),
        cost_estimate=lasting(23),
        name="attention_forward",
    )(latents, latents, wq, wkv, rope, feat, *tables)


def backward_kernel(
    q_ref, kv_ref, grad_ref, lse_ref, rope_ref, here_ref, low_ref, high_ref,
    dq_ref, dkv_ref, drope_ref, k_ref, do_ref, dk_ref, dv_ref,
):
    length = q_ref.shape[0]
    lane = lax.broadcasted_iota(jnp.int32, (BLOCK, LANES), 1)
    causal = lax.broadcasted_iota(jnp.int32, (BLOCK, BLOCK), 0) <= lax.broadcasted_iota(
        jnp.int32, (BLOCK, BLOCK), 1
    )
    blocks = [slice(start, start + BLOCK) for start in range(0, length, BLOCK)]

    @pl.when(pl.program_id(0) == 0)
    def _():
        drope_ref[...] = jnp.zeros_like(drope_ref)

    for rows in blocks:
        for head in range(2):
            part = slice(head * LANES, (head + 1) * LANES)
            k_ref[head, rows, :] = jnp.where(lane < NOPE, kv_ref[rows, part], rope_ref[rows, :])
            upstream = grad_ref[rows, :].astype(jnp.float32)
            if head == 0:
                upstream = roll_lanes(upstream, VDIM)
            do_ref[head, rows, :] = jnp.where(lane < NOPE, 0.0, upstream).astype(jnp.bfloat16)
    for head in range(2):
        part = slice(head * LANES, (head + 1) * LANES)
        for rows in reversed(blocks):
            last = rows.stop == length
            query = q_ref[rows, part]
            upstream = do_ref[head, rows, :]
            log_total = lse_ref[0, head : head + 1, rows]
            pieces = [rows] + ([slice(0, rows.start)] if rows.start else [])
            held = []
            delta = None
            for piece in pieces:
                scores = product_right(k_ref[head, piece, :], query)
                probability = jnp.exp2(scores * (SCALE * LOG2E) - log_total)
                if piece is rows:
                    probability = jnp.where(causal, probability, 0.0)
                slope = product_right(kv_ref[piece, part], upstream)
                inner = jnp.sum(probability * slope, axis=0, keepdims=True)
                delta = inner if delta is None else delta + inner
                held.append((piece, probability, slope))
            query_grad = None
            for piece, probability, slope in held:
                score_grad = (probability * (slope - delta)).astype(jnp.bfloat16)
                key_grad = product(score_grad, query)
                value_grad = product(probability.astype(jnp.bfloat16), upstream)
                if last:
                    dk_ref[piece, :] = key_grad
                    dv_ref[piece, :] = value_grad
                else:
                    dk_ref[piece, :] += key_grad
                    dv_ref[piece, :] += value_grad
                term = product_left(score_grad, k_ref[head, piece, :])
                query_grad = term if query_grad is None else query_grad + term
            query_grad = query_grad * SCALE
            dq_ref[rows, part] = (
                query_grad * here_ref[rows, :]
                - roll_lanes(query_grad, -ROPE // 2) * low_ref[rows, :]
                - roll_lanes(query_grad, ROPE // 2) * high_ref[rows, :]
            ).astype(jnp.bfloat16)
        for rows in blocks:
            key_grad = dk_ref[rows, :] * SCALE
            dkv_ref[rows, part] = jnp.where(lane < NOPE, key_grad, dv_ref[rows, :]).astype(
                jnp.bfloat16
            )
            drope_ref[rows, :] += jnp.where(
                (lane >= NOPE) & (lane < NOPE + ROPE), key_grad, 0.0
            )


def attention_backward(query, key_value, grad, lse, rope, tables):
    length = query.shape[0]
    pairs = grad.shape[1] // LANES
    whole = lambda width: pl.BlockSpec((length, width), lambda j: (0, 0))
    mine = lambda width: pl.BlockSpec((length, width), lambda j: (0, j))
    low = jnp.bfloat16
    return pl.pallas_call(
        backward_kernel,
        grid=(pairs,),
        in_specs=[
            mine(2 * LANES), mine(2 * LANES), mine(LANES),
            pl.BlockSpec((1, 2, length), lambda j: (j, 0, 0)),
            whole(LANES), whole(LANES), whole(LANES), whole(LANES),
        ],
        out_specs=[mine(2 * LANES), mine(2 * LANES), whole(LANES)],
        out_shape=[
            jax.ShapeDtypeStruct((length, pairs * 2 * LANES), low),
            jax.ShapeDtypeStruct((length, pairs * 2 * LANES), low),
            jax.ShapeDtypeStruct((length, LANES), jnp.float32),
        ],
        scratch_shapes=[
            pltpu.VMEM((2, length, LANES), low),
            pltpu.VMEM((2, length, LANES), low),
            pltpu.VMEM((length, LANES), jnp.float32),
            pltpu.VMEM((length, LANES), jnp.float32),
        ],
        compiler_params=pltpu.CompilerParams(vmem_limit_bytes=ROOM),
        cost_estimate=lasting(31),
        name="attention_backward",
    )(query, key_value, grad, lse, rope, *tables)


def vector(width):
    return pl.BlockSpec((1, width), lambda *_: (0, 0))


def full(array):
    return pl.BlockSpec(array.shape, lambda *_: (0,) * array.ndim)


ANYWHERE = pl.BlockSpec(memory_space=pl.ANY)
SCALARS = pl.BlockSpec(memory_space=pltpu.SMEM)


def assemble_kernel(copies, count, *refs):
    spots_ref, pieces, outs, sems = refs[0], refs[1 : count + 1], refs[count + 1 : -1], refs[-1]
    started = []
    for number, (piece, row, rows, column, width, out, place) in enumerate(copies):
        start = place if isinstance(place, int) else spots_ref[place[0]] * place[1]
        start = pl.multiple_of(start, 16)
        copy = pltpu.make_async_copy(
            pieces[piece].at[pl.ds(row, rows), pl.ds(column, width)],
            outs[out].at[pl.ds(start, rows), :],
            sems.at[number],
        )
        copy.start()
        started.append(copy)
    for copy in started:
        copy.wait()


def assemble(spots, pieces, copies, shapes):
    return pl.pallas_call(
        functools.partial(assemble_kernel, copies, len(pieces)),
        in_specs=[SCALARS] + [ANYWHERE] * len(pieces),
        out_specs=[pl.BlockSpec(shape, lambda: (0, 0)) for shape in shapes],
        out_shape=[jax.ShapeDtypeStruct(shape, jnp.bfloat16) for shape in shapes],
        scratch_shapes=[pltpu.SemaphoreType.DMA((len(copies),))],
        compiler_params=pltpu.CompilerParams(vmem_limit_bytes=ROOM),
        cost_estimate=lasting(6),
        name="assemble",
    )(spots, *pieces)


def collect_kernel(copies, count, team_ref, *refs):
    pieces, (out_ref, sems) = refs[:count], refs[count:]
    width = out_ref.shape[1]
    started = []
    for number, (piece, row, block, team) in enumerate(copies):
        start = pl.multiple_of((block + team_ref[team]) * 16, 16)
        copy = pltpu.make_async_copy(
            pieces[piece].at[pl.ds(row, 16), pl.ds(pieces[piece].shape[1] - width, width)],
            out_ref.at[pl.ds(start, 16), :],
            sems.at[number],
        )
        copy.start()
        started.append(copy)
    for copy in started:
        copy.wait()


def collect_rows(teams, pieces, copies):
    return pl.pallas_call(
        functools.partial(collect_kernel, copies, len(pieces)),
        in_specs=[SCALARS] + [ANYWHERE] * len(pieces),
        out_specs=pl.BlockSpec((16 * len(copies), LANES), lambda: (0, 0)),
        out_shape=jax.ShapeDtypeStruct((16 * len(copies), LANES), jnp.bfloat16),
        scratch_shapes=[pltpu.SemaphoreType.DMA((len(copies),))],
        cost_estimate=lasting(3),
        name="collect",
    )(teams, *pieces)


def project_kernel(copies, count, rank, *refs):
    (team_ref, tokens_ref, gain_ref, gain_query_ref, gain_latent_ref, here_ref, low_ref, high_ref) = refs[:8]
    pieces = refs[8 : 8 + count]
    send_ref, raw_ref, input_ref, weights_ref, sems = refs[8 + count :]
    started = []
    for number, (piece, row, rows, block, team) in enumerate(copies):
        start = block if team is None else (block + team_ref[team]) * rows
        copy = pltpu.make_async_copy(
            pieces[piece].at[pl.ds(row, rows), :],
            weights_ref.at[pl.ds(pl.multiple_of(start, 16), rows), :],
            sems.at[number],
        )
        copy.start()
        started.append(copy)
    values = tokens_ref[...].astype(jnp.float32)
    input_ref[...] = normalize(values, gain_ref[...])[0].astype(jnp.bfloat16)
    for copy in started:
        copy.wait()
    raw = product(input_ref[...], weights_ref[...])
    raw_ref[...] = raw
    send_ref[:, :rank] = normalize(raw[:, :rank], gain_query_ref[...])[0].astype(jnp.bfloat16)
    send_ref[:, rank : rank + KVR] = normalize(
        raw[:, rank : rank + KVR], gain_latent_ref[...]
    )[0].astype(jnp.bfloat16)
    key = raw[:, rank + KVR :]
    send_ref[:, rank + KVR :] = (
        key * here_ref[...]
        + roll_lanes(key, -ROPE // 2) * low_ref[...]
        + roll_lanes(key, ROPE // 2) * high_ref[...]
    ).astype(jnp.bfloat16)


def project(teams, tokens, gains, tables, pieces, copies, rank):
    rows, width = tokens.shape
    out = rank + KVR + LANES
    low = jnp.bfloat16
    shapes = [((rows, out), low), ((rows, out), jnp.float32), ((rows, width), low), ((width, out), low)]
    return pl.pallas_call(
        functools.partial(project_kernel, copies, len(pieces), rank),
        in_specs=[SCALARS, full(tokens)]
        + [full(gain) for gain in gains]
        + [full(table) for table in tables]
        + [ANYWHERE] * len(pieces),
        out_specs=[pl.BlockSpec(shape, lambda: (0, 0)) for shape, _ in shapes],
        out_shape=[jax.ShapeDtypeStruct(*shape) for shape in shapes],
        scratch_shapes=[pltpu.SemaphoreType.DMA((len(copies),))],
        compiler_params=pltpu.CompilerParams(vmem_limit_bytes=ROOM),
        cost_estimate=lasting(10),
        name="project",
    )(teams, tokens, *gains, *tables, *pieces)


def joined(refs):
    if len(refs) == 1:
        return refs[0][...]
    return jnp.concatenate([ref[...] for ref in refs], axis=0)


def single_kernel(left_ref, *refs):
    refs[-1][...] = product(left_ref[...], joined(refs[:-1]))


def gate_kernel(count, last, left_ref, *refs):
    weights = joined(refs[:count])
    slope_ref, activated_ref, grads_ref = refs[count:]
    rows = left_ref.shape[0] // 2

    def work(width):
        for start in (0, rows):
            part = slice(start, start + rows)
            both = product(left_ref[part, :], weights[:, : 2 * width])
            gate, up = both[:, :width], both[:, width:]
            sigmoid = jax.nn.sigmoid(gate)
            swish = gate * sigmoid
            activated_ref[part, :width] = (swish * up).astype(jnp.bfloat16)
            upstream = slope_ref[part, :width]
            slope = sigmoid * (1.0 + gate * (1.0 - sigmoid))
            grads_ref[part, :width] = (upstream * up * slope).astype(jnp.bfloat16)
            grads_ref[part, width : 2 * width] = (upstream * swish).astype(jnp.bfloat16)
            rest = -width % LANES
            if rest:
                activated_ref[part, width : width + rest] = jnp.zeros((rows, rest), jnp.bfloat16)

    step, final = pl.program_id(0), pl.num_programs(0) - 1

    @pl.when(step < final)
    def _():
        work(TILE)

    @pl.when(step == final)
    def _():
        work(last)


TILE = 256


def piece_specs(pieces, width):
    return [pl.BlockSpec((piece.shape[0], width), lambda j: (0, j)) for piece in pieces]


def pair_columns(width):
    full_width = width
    if 2 * (width % TILE) % LANES:
        full_width = -(-width // LANES) * LANES
    return [
        (start, 2 * start, min(TILE, full_width - start), min(TILE, width - start))
        for start in range(0, full_width, TILE)
    ]


def paired_kernel(gate_ref, up_ref, out_ref):
    for start, place, size, real in pair_columns(gate_ref.shape[1]):
        for side, ref in enumerate((gate_ref, up_ref)):
            tile = ref[:, start : start + real]
            if real < size:
                rest = jnp.zeros((tile.shape[0], size - real), tile.dtype)
                tile = jnp.concatenate([tile, rest], axis=1)
            out_ref[:, place + side * size : place + (side + 1) * size] = tile


def paired(gate, up):
    width = sum(2 * size for _, _, size, _ in pair_columns(gate.shape[1]))
    shape = (gate.shape[0], width)
    return pl.pallas_call(
        paired_kernel,
        in_specs=[full(gate), full(up)],
        out_specs=pl.BlockSpec(shape, lambda: (0, 0)),
        out_shape=jax.ShapeDtypeStruct(shape, gate.dtype),
        compiler_params=pltpu.CompilerParams(vmem_limit_bytes=ROOM),
        cost_estimate=lasting(4),
        name="paired",
    )(gate, up)


def unpaired_kernel(own_ref, low_ref, high_ref, weights_ref, gate_ref, up_ref, sums_ref):
    sums = None
    for start, place, size, real in pair_columns(gate_ref.shape[1]):
        for side, out_ref in enumerate((gate_ref, up_ref)):
            part = slice(place + side * size, place + (side + 1) * size)
            total = own_ref[:, part].astype(jnp.float32) + low_ref[:, part].astype(jnp.float32)
            total = total + high_ref[:, part].astype(jnp.float32)
            out_ref[:, start : start + real] = total[:, :real]
            term = jnp.sum(total * weights_ref[:, part].astype(jnp.float32), axis=1, keepdims=True)
            sums = term if sums is None else sums + term
    sums_ref[...] = jnp.broadcast_to(sums, sums_ref.shape)


def unpaired(own, low, high, weights, width):
    rows = weights.shape[0]
    shapes = [(rows, width), (rows, width), (rows, LANES)]
    return pl.pallas_call(
        unpaired_kernel,
        grid=(1,),
        in_specs=[pl.BlockSpec(weights.shape, lambda _: (0, 0))] * 4,
        out_specs=[pl.BlockSpec(shape, lambda _: (0, 0)) for shape in shapes],
        out_shape=[jax.ShapeDtypeStruct(shape, jnp.float32) for shape in shapes],
        compiler_params=pltpu.CompilerParams(vmem_limit_bytes=ROOM),
        cost_estimate=lasting(5),
        name="unpaired",
    )(own, low, high, weights)


def feed_product(left, pieces):
    rows, width = left.shape[0], pieces[0].shape[1]
    return pl.pallas_call(
        single_kernel,
        grid=(pl.cdiv(width, TILE),),
        in_specs=[full(left)] + piece_specs(pieces, TILE),
        out_specs=pl.BlockSpec((rows, TILE), lambda j: (0, j)),
        out_shape=jax.ShapeDtypeStruct((rows, width), jnp.float32),
        compiler_params=pltpu.CompilerParams(vmem_limit_bytes=ROOM),
        cost_estimate=lasting(15),
        name="feed_product",
    )(left, *pieces)


def feed_gate(left, pieces, upstream):
    rows, width = upstream.shape
    pair_width = pieces[0].shape[1]
    column = lambda size: pl.BlockSpec((rows, size), lambda j: (0, j))
    return pl.pallas_call(
        functools.partial(gate_kernel, len(pieces), pair_width // 2 % TILE or TILE),
        grid=(pl.cdiv(width, TILE),),
        in_specs=[full(left)] + piece_specs(pieces, 2 * TILE) + [column(TILE)],
        out_specs=[column(TILE), column(2 * TILE)],
        out_shape=[
            jax.ShapeDtypeStruct((rows, width), jnp.bfloat16),
            jax.ShapeDtypeStruct((rows, pair_width), jnp.bfloat16),
        ],
        compiler_params=pltpu.CompilerParams(vmem_limit_bytes=ROOM),
        cost_estimate=lasting(26),
        name="feed_gate",
    )(left, *pieces, upstream)


def terms_kernel(count, *refs):
    arrays, out_ref = refs[: count + 1], refs[-4]
    left_ref, right_ref, sems = refs[-3:]
    rows = right_ref.shape[0] // count
    places = [left_ref]
    places += [right_ref.at[pl.ds(number * rows, rows), :] for number in range(count)]
    copies = [
        pltpu.make_async_copy(array, place, sems.at[number])
        for number, (array, place) in enumerate(zip(arrays, places))
    ]
    for copy in copies:
        copy.start()
    copies[0].wait()
    ready = 0
    for start in range(0, right_ref.shape[0], 2 * TILE):
        stop = min(start + 2 * TILE, right_ref.shape[0])
        while ready * rows < stop:
            copies[ready + 1].wait()
            ready += 1
        part = slice(start, stop)
        out_ref[:, part] = product_right(left_ref[...], right_ref[part, :]).astype(jnp.bfloat16)


def feed_terms(left, pieces, total, block, earlier=None, cost=lasting(18)):
    arrays = [left, *pieces]
    rows, width = left.shape
    columns = sum(piece.shape[0] for piece in pieces)
    low = jnp.bfloat16
    return pl.pallas_call(
        functools.partial(terms_kernel, len(pieces)),
        grid=(1,),
        in_specs=[ANYWHERE] * (len(arrays) + (earlier is not None)),
        out_specs=pl.BlockSpec((rows, columns), lambda _: (0, block)),
        out_shape=jax.ShapeDtypeStruct((rows, total), low),
        scratch_shapes=[
            pltpu.VMEM((rows, width), low),
            pltpu.VMEM((columns, width), low),
            pltpu.SemaphoreType.DMA((len(arrays),)),
        ],
        input_output_aliases={} if earlier is None else {len(arrays): 0},
        compiler_params=pltpu.CompilerParams(vmem_limit_bytes=ROOM),
        cost_estimate=cost,
        name="feed_terms",
    )(*arrays, *([] if earlier is None else [earlier]))


def latent_back_kernel(
    copies, rank, team_ref, back_ref, raw_ref, input_ref, gain_query_ref, gain_latent_ref,
    here_ref, low_ref, high_ref, *refs,
):
    outs, (grad_ref, held_ref, sems) = refs[:-3], refs[-3:]
    cuts = [(slice(0, rank), gain_query_ref), (slice(rank, rank + KVR), gain_latent_ref)]
    for part, gain_ref in cuts:
        values = raw_ref[:, part]
        inverse = normalize(values, gain_ref[...])[1]
        grad = normalize_back(
            values, inverse, gain_ref[...], back_ref[:, part].astype(jnp.float32)
        )
        grad_ref[:, part] = grad.astype(jnp.bfloat16)
    key = back_ref[:, rank + KVR :].astype(jnp.float32)
    grad_ref[:, rank + KVR :] = (
        key * here_ref[...]
        - roll_lanes(key, -ROPE // 2) * low_ref[...]
        - roll_lanes(key, ROPE // 2) * high_ref[...]
    ).astype(jnp.bfloat16)
    held_ref[...] = product_left(input_ref[...], grad_ref[...]).astype(jnp.bfloat16)
    started = []
    for number, (out, row, rows, block, team) in enumerate(copies):
        start = block if team is None else (block + team_ref[team]) * rows
        copy = pltpu.make_async_copy(
            held_ref.at[pl.ds(pl.multiple_of(start, 16), rows), :],
            outs[out].at[pl.ds(row, rows), :],
            sems.at[number],
        )
        copy.start()
        started.append(copy)
    for copy in started:
        copy.wait()


def latent_back(teams, back, raw, inputs, gains, tables, copies, heights, rank):
    rows, width = inputs.shape
    out = back.shape[1]
    low = jnp.bfloat16
    shapes = [((rows, out), low)]
    arrays = [back, raw, inputs, *gains, *tables]
    results = pl.pallas_call(
        functools.partial(latent_back_kernel, copies, rank),
        in_specs=[SCALARS] + [full(array) for array in arrays],
        out_specs=[ANYWHERE] * len(heights)
        + [pl.BlockSpec(shape, lambda: (0, 0)) for shape, _ in shapes],
        out_shape=[jax.ShapeDtypeStruct((height, out), low) for height in heights]
        + [jax.ShapeDtypeStruct(*shape) for shape in shapes],
        scratch_shapes=[pltpu.VMEM((width, out), low), pltpu.SemaphoreType.DMA((len(copies),))],
        compiler_params=pltpu.CompilerParams(vmem_limit_bytes=ROOM),
        cost_estimate=lasting(8),
        name="latent_back",
    )(teams, *arrays)
    return results[:-1], results[-1]


def head_sums_kernel(
    copies, rank, spots_ref, latents_ref, query_ref, key_value_ref, upstream_ref, heads_ref,
    out_ref, q_ref, kv_ref, o_ref, sems,
):
    q_ref[...] = product_left(latents_ref[:, :rank], query_ref[...]).astype(jnp.bfloat16)
    kv_ref[...] = product_left(latents_ref[:, rank : rank + KVR], key_value_ref[...]).astype(
        jnp.bfloat16
    )
    started = []

    def send(wanted):
        for number, (side, row, rows, place, column) in enumerate(copies):
            if side not in wanted:
                continue
            start = row if isinstance(row, int) else spots_ref[row[0]] * rows
            held = (q_ref, kv_ref, o_ref)[side]
            copy = pltpu.make_async_copy(
                held.at[pl.ds(pl.multiple_of(start, 16), rows), :],
                out_ref.at[pl.ds(place, rows), pl.ds(column, held.shape[1])],
                sems.at[number],
            )
            copy.start()
            started.append(copy)

    send((0, 1))
    o_ref[...] = product_left(upstream_ref[...], heads_ref[...]).astype(jnp.bfloat16)
    send((2,))
    for copy in started:
        copy.wait()


def head_sums(spots, latents, query, key_value, upstream, heads, rank, query_rows, latent_rows, out_rows):
    width, out_width = query.shape[1], heads.shape[1]
    count = spots.shape[0]
    rows = query_rows + latent_rows + out_rows // 2
    copies = []
    for spot in range(count):
        start = spot * rows
        copies.append((0, (spot,), query_rows, start, 0))
        copies.append((1, (spot,), latent_rows, start + query_rows, 0))
        for side in (0, 1):
            copies.append(
                (2, spot * out_rows + side * (out_rows // 2), out_rows // 2,
                 start + query_rows + latent_rows, side * out_width)
            )
    low = jnp.bfloat16
    arrays = [latents, query, key_value, upstream, heads]
    return pl.pallas_call(
        functools.partial(head_sums_kernel, copies, rank),
        in_specs=[SCALARS] + [full(array) for array in arrays],
        out_specs=pl.BlockSpec((count * rows, width), lambda: (0, 0)),
        out_shape=jax.ShapeDtypeStruct((count * rows, width), low),
        scratch_shapes=[
            pltpu.VMEM((rank, width), low),
            pltpu.VMEM((KVR, width), low),
            pltpu.VMEM((upstream.shape[1], out_width), low),
            pltpu.SemaphoreType.DMA((len(copies),)),
        ],
        compiler_params=pltpu.CompilerParams(vmem_limit_bytes=ROOM),
        cost_estimate=lasting(20),
        name="head_sums",
    )(spots, *arrays)


def token_back_kernel(grad_ref, weights_ref, tokens_ref, hidden_ref, gain_ref, out_ref):
    upstream = product_right(grad_ref[...], weights_ref[...])
    values = tokens_ref[...].astype(jnp.float32)
    inverse = normalize(values, gain_ref[...])[1]
    out_ref[...] = hidden_ref[...] + normalize_back(values, inverse, gain_ref[...], upstream)


def token_back(grad, weights, tokens, hidden_grad, gain):
    arrays = [grad, weights, tokens, hidden_grad, gain]
    return pl.pallas_call(
        token_back_kernel,
        in_specs=[full(array) for array in arrays],
        out_specs=full(hidden_grad),
        out_shape=jax.ShapeDtypeStruct(hidden_grad.shape, jnp.float32),
        compiler_params=pltpu.CompilerParams(vmem_limit_bytes=ROOM),
        cost_estimate=lasting(8),
        name="token_back",
    )(*arrays)


def reorder_kernel(spots_ref, in_ref, out_ref):
    width = in_ref.shape[1]
    count = spots_ref.shape[0]
    size = width // count
    window = min(-(-(size + LANES - 1) // LANES) * LANES, width)
    for place in range(count):
        start = spots_ref[place] * size
        base = jnp.minimum(start // LANES * LANES, width - window)
        held = in_ref[:, pl.ds(pl.multiple_of(base, LANES), window)].astype(jnp.float32)
        held = pltpu.roll(held, lax.rem(window - (start - base), window), 1)
        out_ref[:, place * size : (place + 1) * size] = held[:, :size].astype(out_ref.dtype)


def reorder(values, spots):
    return pl.pallas_call(
        reorder_kernel,
        in_specs=[SCALARS, full(values)],
        out_specs=full(values),
        out_shape=jax.ShapeDtypeStruct(values.shape, values.dtype),
        compiler_params=pltpu.CompilerParams(vmem_limit_bytes=ROOM),
        cost_estimate=lasting(4),
        name="reorder",
    )(spots, values)


class Ring:
    def __init__(self, axis):
        self.axis = axis
        self.count = lax.axis_size(axis)
        self.half = self.count // 2
        order = list(range(0, self.count, 2)) + list(range(self.count - 1, 0, -2))
        self.me = lax.axis_index(axis)
        self.spot = self.place(self.me)
        indices = jnp.arange(self.count, dtype=jnp.int32)
        self.ahead = self.owner(indices)
        self.behind = lax.rem(self.place(indices) - self.spot + self.count, self.count)
        self.up = [(order[i], order[(i + 1) % self.count]) for i in range(self.count)]
        self.down = [(b, a) for a, b in self.up]

    def place(self, index):
        return jnp.where(index % 2 == 0, index // 2, self.count - (index + 1) // 2)

    def owner(self, step):
        spot = lax.rem(self.spot + step + self.count, self.count)
        return jnp.where(spot < self.half, 2 * spot, 2 * self.count - 1 - 2 * spot)

    def send_up(self, block):
        return lax.ppermute(block, self.axis, self.up)

    def send_down(self, block):
        return lax.ppermute(block, self.axis, self.down)


class Gather:
    def __init__(self, ring, shard):
        self.ring = ring
        self.rows = shard.shape[0]
        self.low = self.high = shard
        self.blocks = {0: shard}
        self.step = 0

    def advance(self):
        ring = self.ring
        if self.done:
            return
        self.step += 1
        if self.step < ring.half:
            self.low = ring.send_up(self.low)
            self.high = ring.send_down(self.high)
            self.blocks[self.step] = self.high
            self.blocks[ring.count - self.step] = self.low
        else:
            cut = self.rows // 2
            self.low = ring.send_up(self.low[:cut])
            self.high = ring.send_down(self.high[cut:])
            self.blocks[ring.half] = None

    @property
    def done(self):
        return self.step >= self.ring.half

    def finish(self):
        while not self.done:
            self.advance()
        self.blocks[self.ring.half] = jnp.concatenate([self.low, self.high], axis=0)
        return [self.blocks[spot] for spot in range(self.ring.count)]


class Scatter:
    def __init__(self, ring, take, rows):
        self.ring = ring
        self.take = lambda step, start, size: take(step % ring.count, start, size)
        self.rows = rows
        self.step = 0
        self.low = self.high = None

    def add(self, a, b):
        return (a.astype(jnp.float32) + b.astype(jnp.float32)).astype(b.dtype)

    def advance(self):
        ring, rows, cut = self.ring, self.rows, self.rows // 2
        if self.done:
            return
        ahead = ring.half - self.step
        if self.step:
            self.low, self.high = lax.optimization_barrier((self.low, self.high))
        self.step += 1
        if ahead == ring.half:
            low = self.take(ahead, 0, cut)
            high = self.take(ahead, cut, rows - cut)
        elif ahead == ring.half - 1:
            low = self.take(ahead, 0, rows)
            high = self.take(-ahead, 0, rows)
            low = jnp.concatenate([self.add(self.low, low[:cut]), low[cut:]], axis=0)
            high = jnp.concatenate([high[:cut], self.add(self.high, high[cut:])], axis=0)
        else:
            low = self.add(self.low, self.take(ahead, 0, rows))
            high = self.add(self.high, self.take(-ahead, 0, rows))
        self.sent = (low, high)
        self.low = ring.send_up(low)
        self.high = ring.send_down(high)

    @property
    def done(self):
        return self.step >= self.ring.half

    def finish(self):
        while not self.done:
            self.advance()
        own = self.take(0, 0, self.rows).astype(jnp.float32)
        return own + self.low.astype(jnp.float32) + self.high.astype(jnp.float32)


def stacked(ring, grads):
    rows = grads.shape[0] // ring.count

    def take(spot, start, size):
        return lax.slice_in_dim(grads, spot * rows + start, spot * rows + start + size, axis=0)

    return Scatter(ring, take, rows)


def staged(ring, left, right):
    size = left.shape[1] // ring.count
    low, high = ring.count // 4, ring.count // 4 + ring.half
    parts = {}
    held = [right]

    def take(spot, start, rows):
        name = 1 if low <= spot < high else 0 if spot < low else 2
        first = (0, low, high)[name]
        if name not in parts:
            last = (low, high, ring.count)[name]
            columns = lax.slice_in_dim(left, first * size, last * size, axis=1)
            parts[name] = product_left(columns, held[0]).astype(jnp.bfloat16)
        begin = (spot - first) * size + start
        return lax.slice_in_dim(parts[name], begin, begin + rows, axis=0)

    scatter = Scatter(ring, take, size)
    scatter.held = held
    scatter.parts = parts
    return scatter


def delay(scatter, *others):
    scatter.held[0] = follow(scatter.held[0], *others)


def follow(values, *others):
    return lax.optimization_barrier((values, others))[0]


def ends(*streams):
    return [(stream.low, stream.high) for stream in streams]


def hold(stream, *others):
    stream.low, stream.high = follow((stream.low, stream.high), *others)


def swap(values, bit):
    count = lax.axis_size("tensor")
    return lax.ppermute(values, "tensor", [(i, i ^ bit) for i in range(count)])


def pad_heads(weights, heads):
    rows = weights.shape[0]
    width = weights.shape[1] // heads
    padded = jnp.pad(weights.reshape(rows, heads, width), ((0, 0), (0, 0), (0, LANES - width)))
    return padded.reshape(rows, heads * LANES)


def on_device(
    tokens,
    segments,
    positions,
    norm_input,
    norm_query,
    norm_latent,
    norm_hidden,
    query_down,
    latent_down,
    query_up,
    latent_up,
    attention_out,
    gate_weight,
    up_weight,
    down_weight,
    cotangent,
):
    low = jnp.bfloat16
    local_rows = tokens.shape[0]
    shard = lax.axis_index("tensor")
    offset = shard * local_rows
    length = segments.shape[0]
    local_heads = HEADS // lax.axis_size("tensor")
    pairs = local_heads // 2
    rank = query_down.shape[1]
    ring = Ring("fsdp")
    everyone = lax.axis_size("fsdp") * lax.axis_size("tensor")
    teams = lax.axis_size("tensor")
    gains_own = jnp.concatenate([norm_input, norm_hidden, norm_query, norm_latent])
    gain_sizes = [norm_input.shape[0], norm_hidden.shape[0], norm_query.shape[0], norm_latent.shape[0]]
    gain_width = -(-gains_own.shape[0] // LANES) * LANES
    spare = LANES - NOPE - ROPE
    gain_rows = -(-gains_own.shape[0] // spare)
    down_rows = query_down.shape[0]
    down_width = rank + KVR + LANES
    gain_part = jnp.pad(gains_own, (0, gain_rows * spare - gains_own.shape[0]))
    gain_part = jnp.pad(gain_part.reshape(gain_rows, spare), ((0, down_rows - gain_rows), (0, 0)))
    packed = jnp.concatenate(
        [
            query_down,
            latent_down[:, :KVR],
            jnp.zeros((down_rows, NOPE), low),
            latent_down[:, KVR:],
            gain_part,
        ],
        axis=1,
    )
    feed_width = gate_weight.shape[1]
    feed_rows = gate_weight.shape[0]
    feed_pad = -feed_width % LANES
    widen = lambda weights: jnp.pad(weights, ((0, 0), (0, feed_pad)))
    head_width = 2 * pairs * LANES
    query_rows, latent_rows, out_rows = query_up.shape[0], latent_up.shape[0], attention_out.shape[1]
    out_width = attention_out.shape[0]
    out_t = attention_out.T
    mixed = jnp.concatenate(
        [
            pad_heads(query_up, local_heads),
            latent_up,
            jnp.concatenate([out_t[: out_rows // 2], out_t[out_rows // 2 :]], axis=1),
        ],
        axis=0,
    )
    mixed_up = Gather(ring, mixed)
    down_up = Gather(ring, widen(down_weight.T))
    pair_own = paired(gate_weight, up_weight)
    pair_up = Gather(ring, pair_own)

    tokens_ring = reorder(tokens, ring.ahead)
    upstream = reorder(cotangent, ring.ahead)
    here, turn_low, turn_high = rotary_lanes(positions)
    tables = (here, turn_low, turn_high)
    local_tables = [lax.dynamic_slice_in_dim(table, offset, local_rows) for table in tables]
    query_feat, key_feat = segment_lanes(segments)
    key_feat = key_feat.astype(low)
    ahead, behind = ring.ahead, ring.behind
    team_ids = shard ^ jnp.asarray([0, 2, 1, 3], jnp.int32)

    small_up = Gather(ring, packed)
    pieces, copies = [], []

    def collect(block, spot, first):
        across = swap(block, 2)
        for team, piece in enumerate((block, across, swap(block, 1), swap(across, 1))):
            rows = block.shape[0]
            copies.append((len(pieces), 0, rows, spot * teams, team, first))
            pieces.append(piece)

    collect(small_up.low, 0, 0)
    while not small_up.done:
        swapped = [piece for place, piece in enumerate(pieces) if place % 4]
        small_up.advance()
        mixed_up.advance()
        if not small_up.done:
            collect(small_up.high, small_up.step, 0)
            collect(small_up.low, ring.count - small_up.step, 0)
            hold(small_up, ends(mixed_up), swapped)
            hold(mixed_up, ends(small_up))
    collect(jnp.concatenate([small_up.low, small_up.high], axis=0), ring.half, 0)
    copies = [(piece, row, rows, block, team) for piece, row, rows, block, team, _ in copies]
    hold(down_up, ends(mixed_up, small_up))
    down_up.advance()
    if down_rows % 16:
        table = [[None] * teams for _ in range(ring.count)]
        for piece, row, _, block, team in copies:
            table[block // teams][team] = pieces[piece][row : row + gain_rows, down_width - spare :]
        table = jnp.stack([part for group in zip(*table) for part in group])
        table = table.reshape(teams, ring.count, gain_rows * spare)
        places = shard ^ jnp.arange(teams, dtype=jnp.int32)
        places = jnp.where(places == 1, 2, jnp.where(places == 2, 1, places))
        table = jnp.take(table, places, axis=0)
    else:
        table = collect_rows(
            team_ids, pieces, [(piece, row, block, team) for piece, row, _, block, team in copies]
        )
        table = table.reshape(ring.count, teams, 16, LANES)[:, :, :gain_rows, LANES - spare :]
        table = jnp.transpose(table, (1, 0, 2, 3)).reshape(teams, ring.count, gain_rows * spare)
    table = table.astype(jnp.float32)
    gain_parts = []
    start = 0
    for number, size in enumerate(gain_sizes):
        part = jnp.transpose(table[:, :, start : start + size], (1, 0, 2))
        if number >= 2:
            part = jnp.take(part, behind, axis=0)
        gain_parts.append(part.reshape(1, -1))
        start += size
    gain_in, gain_hidden, gain_query, gain_latent = gain_parts
    if down_rows % 16:
        whole = jnp.zeros((everyone * down_rows, down_width), low)
        for piece, row, rows, block, team in copies:
            whole = lax.dynamic_update_slice(
                whole, pieces[piece][row : row + rows], ((block + team_ids[team]) * rows, 0)
            )
        pieces, copies = [whole], [(0, 0, whole.shape[0], 0, None)]
    latent_send, latent_raw, attention_input, down_projections = project(
        team_ids, tokens_ring, (gain_in, gain_query, gain_latent), local_tables, pieces, copies, rank
    )
    latent_send = follow(latent_send, ends(down_up))
    latents = lax.all_gather(latent_send, "tensor", axis=0, tiled=True)
    hold(down_up, latent_send)
    down_up.advance()
    latents = follow(latents, ends(down_up))
    hold(pair_up, ends(down_up))
    mixed_blocks = mixed_up.finish()
    if query_rows % 16 or latent_rows % 16 or out_rows % 32:
        mixed_all = jnp.stack([mixed_blocks[0]] * ring.count)
        for spot, block in enumerate(mixed_blocks):
            mixed_all = lax.dynamic_update_slice(mixed_all, block[None], (ring.owner(spot), 0, 0))
        wq = mixed_all[:, :query_rows].reshape(-1, head_width)
        wkv = mixed_all[:, query_rows : query_rows + latent_rows].reshape(-1, head_width)
        outs = [block[query_rows + latent_rows :] for block in mixed_blocks]
        attention_out_t = jnp.concatenate(
            [block[:, side * out_width : (side + 1) * out_width] for block in outs for side in (0, 1)],
            axis=0,
        )
    else:
        copies = []
        for spot in range(ring.count):
            copies.append((spot, 0, query_rows, 0, head_width, 0, (spot, query_rows)))
            copies.append((spot, query_rows, latent_rows, 0, head_width, 1, (spot, latent_rows)))
            for side in (0, 1):
                copies.append(
                    (spot, query_rows + latent_rows, out_rows // 2, side * out_width, out_width, 2,
                     spot * out_rows + side * (out_rows // 2))
                )
        wq, wkv, attention_out_t = assemble(
            ahead,
            mixed_blocks,
            copies,
            [(ring.count * query_rows, head_width), (ring.count * latent_rows, head_width),
             (ring.count * out_rows, out_width)],
        )
    down_up.advance()
    pair_up.advance()
    feed_upstream = follow(RESIDUAL * upstream.astype(jnp.float32), latents).astype(low)
    feed_upstream = lax.all_gather(feed_upstream, "tensor", axis=0, tiled=True)
    rope = latents[:, rank + KVR :] + key_feat
    heads, query_heads, key_value, log_totals = attention_forward(
        latents, wq, wkv, rope, query_feat, tables, pairs
    )
    branch_terms = product_right(heads, attention_out_t).astype(low)
    branch_terms = follow(branch_terms, feed_upstream, ends(pair_up))
    attention_branch = lax.psum_scatter(branch_terms, "tensor", scatter_dimension=0, tiled=True)
    attention_branch = follow(attention_branch, ends(down_up))
    downs = down_up.finish()
    if ring.count > 8:
        downs = [jnp.concatenate(downs, axis=0)]
    activated_grad = feed_product(feed_upstream, downs)
    hidden = tokens_ring.astype(jnp.float32) + RESIDUAL * attention_branch.astype(jnp.float32)
    feed_normed, inverse_hidden = normalize(hidden, gain_hidden)
    pair_up.advance()
    feed_normed = follow(feed_normed.astype(low), ends(pair_up))
    feed_seq = lax.all_gather(feed_normed, "tensor", axis=0, tiled=True)
    hold(pair_up, ends(down_up))
    pair_up.advance()
    hold(pair_up, activated_grad)
    weights = pair_up.finish()
    if ring.count > 8:
        weights = [jnp.concatenate(weights, axis=0)]
    activated, pair_grad = feed_gate(feed_seq, weights, activated_grad)

    grad_down = staged(ring, feed_upstream, activated)
    grad_down.advance()
    grad_pair = staged(ring, feed_seq, follow(pair_grad, grad_down.sent))
    grad_pair.advance()
    hold(grad_down, grad_pair.sent)
    grad_down.advance()
    half = max(len(weights) // 2, 1)
    width = feed_seq.shape[1]
    pair_grad = follow(pair_grad, grad_down.sent)
    terms = feed_terms(pair_grad, weights[:half], width, 0)
    hold(grad_pair, terms)
    grad_pair.advance()
    if len(weights) > half:
        terms = follow(terms, grad_pair.sent)
        terms = feed_terms(pair_grad, weights[half:], width, 1, terms)
    terms = follow(terms, ends(grad_down))
    feed_back = lax.psum_scatter(terms, "tensor", scatter_dimension=0, tiled=True)
    activated = follow(activated, terms)
    feed_branch = feed_terms(activated, downs[:half], width, 0, None, lasting(11))
    delay(grad_down, terms)
    hold(grad_down, terms)
    grad_down.advance()
    feed_back = follow(feed_back, grad_down.sent)
    delay(grad_pair, grad_down.sent)
    grad_pair.advance()
    grad_pair.take(0, 0, 1), grad_down.take(0, 0, 1)
    feed_back = follow(feed_back, grad_pair.parts[0], grad_down.parts[0], feed_branch)
    hidden_back = normalize_back(
        hidden, inverse_hidden, gain_hidden, feed_back.astype(jnp.float32)
    )
    hidden_grad = upstream.astype(jnp.float32) + hidden_back
    upstream_send = follow((RESIDUAL * hidden_grad).astype(low), grad_pair.sent, ends(grad_down))
    attention_upstream = lax.all_gather(upstream_send, "tensor", axis=0, tiled=True)
    attention_upstream = follow(attention_upstream, ends(grad_pair))
    heads_grad = product(attention_upstream, attention_out_t).astype(low)
    grad_pair.advance()
    heads_grad = follow(heads_grad, grad_pair.sent)
    query_raw_grad, key_value_grad, key_rope_grad = attention_backward(
        query_heads, key_value, heads_grad, log_totals, rope, tables
    )
    query_raw_grad, key_value_grad = follow((query_raw_grad, key_value_grad), ends(grad_pair))
    hold(grad_down, query_raw_grad)
    grad_down.advance()
    latent_terms = jnp.concatenate(
        [
            product_right(query_raw_grad, wq),
            product_right(key_value_grad, wkv),
            key_rope_grad,
        ],
        axis=1,
    ).astype(low)
    latent_grad = lax.psum_scatter(latent_terms, "tensor", scatter_dimension=0, tiled=True)
    upstream_late, query_raw_grad, key_value_grad = follow(
        (attention_upstream, query_raw_grad, key_value_grad), latent_terms, grad_down.sent
    )
    if query_rows % 16 or latent_rows % 16 or out_rows % 32:
        sums = [
            jnp.take(product_left(left, right).astype(low).reshape(ring.count, -1, head_width), ahead, axis=0)
            for left, right in (
                (latents[:, :rank], query_raw_grad),
                (latents[:, rank : rank + KVR], key_value_grad),
            )
        ]
        out_sums = product_left(upstream_late, heads).astype(low)
        out_sums = out_sums.reshape(ring.count, 2, out_rows // 2, out_width)
        sums.append(jnp.concatenate([out_sums[:, 0], out_sums[:, 1]], axis=2))
        mixed_sums = jnp.concatenate(sums, axis=1).reshape(-1, head_width)
    else:
        mixed_sums = head_sums(
            ahead, latents, query_raw_grad, key_value_grad, upstream_late, heads,
            rank, query_rows, latent_rows, out_rows,
        )
    grad_mixed = stacked(ring, follow(mixed_sums, ends(grad_down)))
    grad_mixed.advance()
    if len(downs) > half:
        activated = follow(activated, grad_mixed.sent)
        feed_branch = feed_terms(activated, downs[half:], width, 1, feed_branch, lasting(11))
    latent_grad = follow(latent_grad, ends(grad_mixed), feed_branch)
    feed_branch = lax.psum_scatter(feed_branch, "tensor", scatter_dimension=0, tiled=True)
    pair = 2 * down_rows
    height = ring.count * pair
    heights = [height, height]
    copies = [
        (team // 2, spot * pair + (team % 2) * down_rows, down_rows, spot * teams, team)
        for spot in range(ring.count)
        for team in range(teams)
    ]
    aligned = down_rows % 16 == 0
    if not aligned:
        copies, heights = [(0, 0, 2 * height, 0, None)], [2 * height]
    sent, latent_low = latent_back(
        team_ids, latent_grad, latent_raw, attention_input, (gain_query, gain_latent),
        local_tables, copies, heights, rank,
    )
    if not aligned:
        blocks = jnp.take(
            sent[0].reshape(ring.count, teams, down_rows, down_width), team_ids, axis=1
        )
        sent = [blocks[:, :2].reshape(height, -1), blocks[:, 2:].reshape(height, -1)]

    def add_low(a, b):
        return (a.astype(jnp.float32) + b.astype(jnp.float32)).astype(low)

    other_sums = swap(sent[1], 1)
    hold(grad_mixed, latent_low)
    grad_mixed.advance()
    token_grad = token_back(
        latent_low, down_projections, tokens_ring, hidden_grad, gain_in
    )
    other_sums = follow(other_sums, token_grad)
    grad_small = stacked(ring, add_low(sent[0], other_sums))
    grad_small.advance()
    hold(grad_mixed, grad_small.sent)
    grad_mixed.advance()
    grad_small.advance()
    token_grad = reorder(follow(token_grad, grad_small.sent), ring.behind)
    hold(grad_mixed, grad_small.sent)
    hold(grad_down, ends(grad_small))
    hold(grad_small, token_grad)
    grad_small.advance()
    feed_branch = follow(feed_branch, grad_small.sent)
    output = hidden + RESIDUAL * feed_branch.astype(jnp.float32)
    output = reorder(output.astype(low), ring.behind)
    grad_mixed.advance()
    hold(grad_small, output)
    grad_small.advance()
    hold(grad_pair, grad_small.sent)
    small_own = grad_small.finish()
    small_other = follow(small_own[down_rows:].astype(low), ends(grad_mixed))
    packed_own = small_own[:down_rows] + swap(small_other, 2).astype(jnp.float32)
    rope_from = rank + KVR + NOPE
    lanes = jnp.arange(down_width) < rope_from + ROPE
    grad_gain_input = jnp.sum(
        jnp.where(lanes, packed.astype(jnp.float32) * packed_own, 0.0), axis=1
    ) / norm_input.astype(jnp.float32)
    grad_mixed_own = grad_mixed.finish()
    while not grad_pair.done:
        grad_pair.advance()
    grad_query_own = grad_mixed_own[:query_rows].reshape(query_rows, local_heads, LANES)
    grad_out_own = grad_mixed_own[query_rows + latent_rows :]
    grad_out_own = jnp.concatenate(
        [grad_out_own[:, :out_width], grad_out_own[:, out_width:]], axis=0
    )
    grad_gate_own, grad_up_own, pair_sums = unpaired(
        grad_pair.parts[0], grad_pair.low, grad_pair.high, pair_own, feed_width
    )
    row_sums = lambda weights, grads: jnp.sum(weights.astype(jnp.float32) * grads, axis=1)
    head_rows = query_rows + latent_rows
    gain_sums = jnp.concatenate(
        [pair_sums[:, 0], row_sums(mixed[:head_rows], grad_mixed_own[:head_rows])]
    )
    gain_sums = jnp.pad(gain_sums, (0, -gain_sums.shape[0] % LANES))[None]
    gain_sums = follow(gain_sums, small_other)
    gain_sums = gain_sums + swap(gain_sums, 1)
    gain_sums = (gain_sums + swap(gain_sums, 2))[0]
    gain_grads = []
    start = 0
    for gain in (norm_hidden, norm_query, norm_latent):
        size = gain.shape[0]
        own = lax.dynamic_slice_in_dim(gain_sums, start + shard * size, size)
        gain_grads.append(own / gain.astype(jnp.float32))
        start += size * teams
    return (
        output,
        token_grad,
        grad_gain_input,
        gain_grads[1],
        gain_grads[2],
        gain_grads[0],
        packed_own[:, :rank],
        jnp.concatenate(
            [packed_own[:, rank : rank + KVR], packed_own[:, rope_from : rope_from + ROPE]],
            axis=1,
        ),
        grad_query_own[:, :, : NOPE + ROPE].reshape(query_rows, -1),
        grad_mixed_own[query_rows : query_rows + latent_rows],
        grad_out_own.T,
        grad_gate_own,
        grad_up_own,
        grad_down.finish()[:, :feed_width].T,
    )


def solution(mesh):
    return jax.shard_map(
        on_device,
        mesh=mesh,
        in_specs=(
            P(("fsdp", "tensor"), None),
            P("fsdp"),
            P("fsdp"),
            P(("fsdp", "tensor")),
            P(("fsdp", "tensor")),
            P(("fsdp", "tensor")),
            P(("fsdp", "tensor")),
            P(("fsdp", "tensor"), None),
            P(("fsdp", "tensor"), None),
            P("fsdp", "tensor"),
            P("fsdp", "tensor"),
            P("tensor", "fsdp"),
            P("fsdp", "tensor"),
            P("fsdp", "tensor"),
            P("tensor", "fsdp"),
            P(("fsdp", "tensor"), None),
        ),
        out_specs=(
            P(("fsdp", "tensor"), None),
            P(("fsdp", "tensor"), None),
            P(("fsdp", "tensor")),
            P(("fsdp", "tensor")),
            P(("fsdp", "tensor")),
            P(("fsdp", "tensor")),
            P(("fsdp", "tensor"), None),
            P(("fsdp", "tensor"), None),
            P("fsdp", "tensor"),
            P("fsdp", "tensor"),
            P("tensor", "fsdp"),
            P("fsdp", "tensor"),
            P("fsdp", "tensor"),
            P("tensor", "fsdp"),
        ),
        check_vma=False,
    )
```

```python
import functools
import math

import jax
import jax.numpy as jnp
from jax import lax
from jax.experimental import pallas as pl
from jax.experimental.pallas import tpu as pltpu
from jax.sharding import PartitionSpec as P

HEADS = 40
NOPE = 64
ROPE = 32
VDIM = 64
KVR = 256
LANES = 128
BLOCK = 256


EPSILON = 1e-05
RESIDUAL = 1.4 / math.sqrt(62.0)
NEGATIVE = -1e30
APART = -(2.0**96)
SCALE = 1.0 / math.sqrt(NOPE + ROPE)
LOG2E = math.log2(math.e)
ROOM = 56 * 1024 * 1024
BRIEF = pl.CostEstimate(flops=1, bytes_accessed=1, transcendentals=0)


def lasting(microseconds):
    return pl.CostEstimate(flops=1, bytes_accessed=microseconds * 3 * 10**6, transcendentals=0)


def normalize(values, gain):
    inverse = lax.rsqrt(jnp.mean(values * values, axis=-1, keepdims=True) + EPSILON)
    return (values * inverse * gain, inverse)


def normalize_back(values, inverse, gain, upstream):
    scaled = upstream * gain
    inner = jnp.mean(scaled * values, axis=-1, keepdims=True)
    return inverse * scaled - values * (inverse * inverse * inverse) * inner


def product(left, right):
    return jnp.dot(left, right, preferred_element_type=jnp.float32)


def product_left(left, right):
    return lax.dot_general(
        left, right, (((0,), (0,)), ((), ())), preferred_element_type=jnp.float32
    )


def product_right(left, right):
    return lax.dot_general(
        left, right, (((1,), (1,)), ((), ())), preferred_element_type=jnp.float32
    )


def rotary_lanes(positions):
    lane = jnp.arange(LANES, dtype=jnp.int32)
    steps = ((lane - NOPE) % (ROPE // 2)).astype(jnp.float32)
    frequency = jnp.exp(steps * (-2.0 * math.log(10000.0) / ROPE))
    angles = positions.astype(jnp.float32)[:, None] * frequency[None, :]
    first = ((lane >= NOPE) & (lane < NOPE + ROPE // 2))[None, :]
    second = ((lane >= NOPE + ROPE // 2) & (lane < NOPE + ROPE))[None, :]
    cosine = jnp.cos(angles)
    sine = jnp.sin(angles)
    here = jnp.where((lane < NOPE)[None, :], 1.0, jnp.where(first | second, cosine, 0.0))
    return (here, jnp.where(first, -sine, 0.0), jnp.where(second, sine, 0.0))


def segment_lanes(segment_ids):
    lane = jnp.arange(LANES, dtype=jnp.int32) - (NOPE + ROPE)
    same = lane[None, :] == segment_ids[:, None]
    used = ((lane >= 0) & (lane < 4))[None, :]
    query = jnp.where(used & same, 1.0, 0.0)
    key = jnp.where(used & ~same, APART, 0.0)
    return (query, key)


def roll_lanes(values, amount):
    return pltpu.roll(values, amount % LANES, 1)


def forward_kernel(
    xq_ref, lat_ref, wq_ref, wkv_ref, rope_ref, feat_ref, here_ref, low_ref, high_ref,
    out_ref, q_ref, kv_ref, lse_ref, k_ref,
):
    length = xq_ref.shape[0]
    lane = lax.broadcasted_iota(jnp.int32, (BLOCK, LANES), 1)
    causal = lax.broadcasted_iota(jnp.int32, (BLOCK, BLOCK), 1) <= lax.broadcasted_iota(
        jnp.int32, (BLOCK, BLOCK), 0
    )
    blocks = [slice(start, start + BLOCK) for start in range(0, length, BLOCK)]
    for rows in blocks:
        q_raw = product(xq_ref[rows, :], wq_ref[...])
        kv_ref[rows, :] = product(lat_ref[rows, :], wkv_ref[...]).astype(jnp.bfloat16)
        for head in range(2):
            part = slice(head * LANES, (head + 1) * LANES)
            raw = q_raw[:, part]
            turned = (
                raw * here_ref[rows, :]
                + roll_lanes(raw, -ROPE // 2) * low_ref[rows, :]
                + roll_lanes(raw, ROPE // 2) * high_ref[rows, :]
                + feat_ref[rows, :]
            )
            q_ref[rows, part] = turned.astype(jnp.bfloat16)
            k_ref[head, rows, :] = jnp.where(lane < NOPE, kv_ref[rows, part], rope_ref[rows, :])
    for rows in blocks:
        results = []
        for head in range(2):
            part = slice(head * LANES, (head + 1) * LANES)
            query = q_ref[rows, part]
            near = product_right(query, k_ref[head, rows, :])
            near = jnp.where(causal, near, NEGATIVE)
            top = jnp.max(near, axis=1, keepdims=True)
            if rows.start:
                far = product_right(query, k_ref[head, : rows.start, :])
                top = jnp.maximum(top, jnp.max(far, axis=1, keepdims=True))
            weights = jnp.exp2((near - top) * (SCALE * LOG2E))
            total = jnp.sum(weights, axis=1, keepdims=True)
            result = product(weights.astype(jnp.bfloat16), kv_ref[rows, part])
            if rows.start:
                weights = jnp.exp2((far - top) * (SCALE * LOG2E))
                total = total + jnp.sum(weights, axis=1, keepdims=True)
                result = result + product(
                    weights.astype(jnp.bfloat16), kv_ref[: rows.start, part]
                )
            results.append(result / total)
            log_total = top * (SCALE * LOG2E) + jnp.log2(total)
            lse_ref[0, head : head + 1, rows] = jnp.transpose(
                jnp.broadcast_to(log_total, (BLOCK, LANES))
            )[0:1, :]
        out_ref[rows, :] = jnp.where(
            lane < VDIM, roll_lanes(results[0], VDIM), results[1]
        ).astype(jnp.bfloat16)


def attention_forward(latents, wq, wkv, rope, feat, tables, pairs):
    length = latents.shape[0]
    rank = wq.shape[0]
    whole = lambda width, at=0: pl.BlockSpec((length, width), lambda j: (0, at))
    mine = lambda width: pl.BlockSpec((length, width), lambda j: (0, j))
    tall = lambda rows: pl.BlockSpec((rows, 2 * LANES), lambda j: (0, j))
    low = jnp.bfloat16
    return pl.pallas_call(
        forward_kernel,
        grid=(pairs,),
        in_specs=[
            whole(rank), whole(KVR, rank // KVR), tall(rank), tall(KVR),
            whole(LANES), whole(LANES), whole(LANES), whole(LANES), whole(LANES),
        ],
        out_specs=[
            mine(LANES), mine(2 * LANES), mine(2 * LANES),
            pl.BlockSpec((1, 2, length), lambda j: (j, 0, 0)),
        ],
        out_shape=[
            jax.ShapeDtypeStruct((length, pairs * LANES), low),
            jax.ShapeDtypeStruct((length, pairs * 2 * LANES), low),
            jax.ShapeDtypeStruct((length, pairs * 2 * LANES), low),
            jax.ShapeDtypeStruct((pairs, 2, length), jnp.float32),
        ],
        scratch_shapes=[pltpu.VMEM((2, length, LANES), low)],
        compiler_params=pltpu.CompilerParams(vmem_limit_bytes=ROOM),
        cost_estimate=lasting(23),
        name="attention_forward",
    )(latents, latents, wq, wkv, rope, feat, *tables)


def backward_kernel(
    q_ref, kv_ref, grad_ref, lse_ref, rope_ref, here_ref, low_ref, high_ref,
    dq_ref, dkv_ref, drope_ref, k_ref, do_ref, dk_ref, dv_ref,
):
    length = q_ref.shape[0]
    lane = lax.broadcasted_iota(jnp.int32, (BLOCK, LANES), 1)
    causal = lax.broadcasted_iota(jnp.int32, (BLOCK, BLOCK), 0) <= lax.broadcasted_iota(
        jnp.int32, (BLOCK, BLOCK), 1
    )
    blocks = [slice(start, start + BLOCK) for start in range(0, length, BLOCK)]

    @pl.when(pl.program_id(0) == 0)
    def _():
        drope_ref[...] = jnp.zeros_like(drope_ref)

    for rows in blocks:
        for head in range(2):
            part = slice(head * LANES, (head + 1) * LANES)
            k_ref[head, rows, :] = jnp.where(lane < NOPE, kv_ref[rows, part], rope_ref[rows, :])
            upstream = grad_ref[rows, :].astype(jnp.float32)
            if head == 0:
                upstream = roll_lanes(upstream, VDIM)
            do_ref[head, rows, :] = jnp.where(lane < NOPE, 0.0, upstream).astype(jnp.bfloat16)
    for head in range(2):
        part = slice(head * LANES, (head + 1) * LANES)
        for rows in reversed(blocks):
            last = rows.stop == length
            query = q_ref[rows, part]
            upstream = do_ref[head, rows, :]
            log_total = lse_ref[0, head : head + 1, rows]
            pieces = [rows] + ([slice(0, rows.start)] if rows.start else [])
            held = []
            delta = None
            for piece in pieces:
                scores = product_right(k_ref[head, piece, :], query)
                probability = jnp.exp2(scores * (SCALE * LOG2E) - log_total)
                if piece is rows:
                    probability = jnp.where(causal, probability, 0.0)
                slope = product_right(kv_ref[piece, part], upstream)
                inner = jnp.sum(probability * slope, axis=0, keepdims=True)
                delta = inner if delta is None else delta + inner
                held.append((piece, probability, slope))
            query_grad = None
            for piece, probability, slope in held:
                score_grad = (probability * (slope - delta)).astype(jnp.bfloat16)
                key_grad = product(score_grad, query)
                value_grad = product(probability.astype(jnp.bfloat16), upstream)
                if last:
                    dk_ref[piece, :] = key_grad
                    dv_ref[piece, :] = value_grad
                else:
                    dk_ref[piece, :] += key_grad
                    dv_ref[piece, :] += value_grad
                term = product_left(score_grad, k_ref[head, piece, :])
                query_grad = term if query_grad is None else query_grad + term
            query_grad = query_grad * SCALE
            dq_ref[rows, part] = (
                query_grad * here_ref[rows, :]
                - roll_lanes(query_grad, -ROPE // 2) * low_ref[rows, :]
                - roll_lanes(query_grad, ROPE // 2) * high_ref[rows, :]
            ).astype(jnp.bfloat16)
        for rows in blocks:
            key_grad = dk_ref[rows, :] * SCALE
            dkv_ref[rows, part] = jnp.where(lane < NOPE, key_grad, dv_ref[rows, :]).astype(
                jnp.bfloat16
            )
            drope_ref[rows, :] += jnp.where(
                (lane >= NOPE) & (lane < NOPE + ROPE), key_grad, 0.0
            )


def attention_backward(query, key_value, grad, lse, rope, tables):
    length = query.shape[0]
    pairs = grad.shape[1] // LANES
    whole = lambda width: pl.BlockSpec((length, width), lambda j: (0, 0))
    mine = lambda width: pl.BlockSpec((length, width), lambda j: (0, j))
    low = jnp.bfloat16
    return pl.pallas_call(
        backward_kernel,
        grid=(pairs,),
        in_specs=[
            mine(2 * LANES), mine(2 * LANES), mine(LANES),
            pl.BlockSpec((1, 2, length), lambda j: (j, 0, 0)),
            whole(LANES), whole(LANES), whole(LANES), whole(LANES),
        ],
        out_specs=[mine(2 * LANES), mine(2 * LANES), whole(LANES)],
        out_shape=[
            jax.ShapeDtypeStruct((length, pairs * 2 * LANES), low),
            jax.ShapeDtypeStruct((length, pairs * 2 * LANES), low),
            jax.ShapeDtypeStruct((length, LANES), jnp.float32),
        ],
        scratch_shapes=[
            pltpu.VMEM((2, length, LANES), low),
            pltpu.VMEM((2, length, LANES), low),
            pltpu.VMEM((length, LANES), jnp.float32),
            pltpu.VMEM((length, LANES), jnp.float32),
        ],
        compiler_params=pltpu.CompilerParams(vmem_limit_bytes=ROOM),
        cost_estimate=lasting(31),
        name="attention_backward",
    )(query, key_value, grad, lse, rope, *tables)


def vector(width):
    return pl.BlockSpec((1, width), lambda *_: (0, 0))


def full(array):
    return pl.BlockSpec(array.shape, lambda *_: (0,) * array.ndim)


ANYWHERE = pl.BlockSpec(memory_space=pl.ANY)
SCALARS = pl.BlockSpec(memory_space=pltpu.SMEM)


def assemble_kernel(copies, count, *refs):
    spots_ref, pieces, outs, sems = refs[0], refs[1 : count + 1], refs[count + 1 : -1], refs[-1]
    started = []
    for number, (piece, row, rows, column, width, out, place) in enumerate(copies):
        start = place if isinstance(place, int) else spots_ref[place[0]] * place[1]
        start = pl.multiple_of(start, 16)
        copy = pltpu.make_async_copy(
            pieces[piece].at[pl.ds(row, rows), pl.ds(column, width)],
            outs[out].at[pl.ds(start, rows), :],
            sems.at[number],
        )
        copy.start()
        started.append(copy)
    for copy in started:
        copy.wait()


def assemble(spots, pieces, copies, shapes):
    return pl.pallas_call(
        functools.partial(assemble_kernel, copies, len(pieces)),
        in_specs=[SCALARS] + [ANYWHERE] * len(pieces),
        out_specs=[pl.BlockSpec(shape, lambda: (0, 0)) for shape in shapes],
        out_shape=[jax.ShapeDtypeStruct(shape, jnp.bfloat16) for shape in shapes],
        scratch_shapes=[pltpu.SemaphoreType.DMA((len(copies),))],
        compiler_params=pltpu.CompilerParams(vmem_limit_bytes=ROOM),
        cost_estimate=lasting(6),
        name="assemble",
    )(spots, *pieces)


def collect_kernel(copies, count, team_ref, *refs):
    pieces, (out_ref, sems) = refs[:count], refs[count:]
    width = out_ref.shape[1]
    started = []
    for number, (piece, row, block, team) in enumerate(copies):
        start = pl.multiple_of((block + team_ref[team]) * 16, 16)
        copy = pltpu.make_async_copy(
            pieces[piece].at[pl.ds(row, 16), pl.ds(pieces[piece].shape[1] - width, width)],
            out_ref.at[pl.ds(start, 16), :],
            sems.at[number],
        )
        copy.start()
        started.append(copy)
    for copy in started:
        copy.wait()


def collect_rows(teams, pieces, copies):
    return pl.pallas_call(
        functools.partial(collect_kernel, copies, len(pieces)),
        in_specs=[SCALARS] + [ANYWHERE] * len(pieces),
        out_specs=pl.BlockSpec((16 * len(copies), LANES), lambda: (0, 0)),
        out_shape=jax.ShapeDtypeStruct((16 * len(copies), LANES), jnp.bfloat16),
        scratch_shapes=[pltpu.SemaphoreType.DMA((len(copies),))],
        cost_estimate=lasting(3),
        name="collect",
    )(teams, *pieces)


def project_kernel(copies, count, rank, *refs):
    (team_ref, tokens_ref, gain_ref, gain_query_ref, gain_latent_ref, here_ref, low_ref, high_ref) = refs[:8]
    pieces = refs[8 : 8 + count]
    send_ref, raw_ref, input_ref, weights_ref, sems = refs[8 + count :]
    started = []
    for number, (piece, row, rows, block, team) in enumerate(copies):
        start = block if team is None else (block + team_ref[team]) * rows
        copy = pltpu.make_async_copy(
            pieces[piece].at[pl.ds(row, rows), :],
            weights_ref.at[pl.ds(pl.multiple_of(start, 16), rows), :],
            sems.at[number],
        )
        copy.start()
        started.append(copy)
    values = tokens_ref[...].astype(jnp.float32)
    input_ref[...] = normalize(values, gain_ref[...])[0].astype(jnp.bfloat16)
    for copy in started:
        copy.wait()
    raw = product(input_ref[...], weights_ref[...])
    raw_ref[...] = raw
    send_ref[:, :rank] = normalize(raw[:, :rank], gain_query_ref[...])[0].astype(jnp.bfloat16)
    send_ref[:, rank : rank + KVR] = normalize(
        raw[:, rank : rank + KVR], gain_latent_ref[...]
    )[0].astype(jnp.bfloat16)
    key = raw[:, rank + KVR :]
    send_ref[:, rank + KVR :] = (
        key * here_ref[...]
        + roll_lanes(key, -ROPE // 2) * low_ref[...]
        + roll_lanes(key, ROPE // 2) * high_ref[...]
    ).astype(jnp.bfloat16)


def project(teams, tokens, gains, tables, pieces, copies, rank):
    rows, width = tokens.shape
    out = rank + KVR + LANES
    low = jnp.bfloat16
    shapes = [((rows, out), low), ((rows, out), jnp.float32), ((rows, width), low), ((width, out), low)]
    return pl.pallas_call(
        functools.partial(project_kernel, copies, len(pieces), rank),
        in_specs=[SCALARS, full(tokens)]
        + [full(gain) for gain in gains]
        + [full(table) for table in tables]
        + [ANYWHERE] * len(pieces),
        out_specs=[pl.BlockSpec(shape, lambda: (0, 0)) for shape, _ in shapes],
        out_shape=[jax.ShapeDtypeStruct(*shape) for shape in shapes],
        scratch_shapes=[pltpu.SemaphoreType.DMA((len(copies),))],
        compiler_params=pltpu.CompilerParams(vmem_limit_bytes=ROOM),
        cost_estimate=lasting(10),
        name="project",
    )(teams, tokens, *gains, *tables, *pieces)


def joined(refs):
    if len(refs) == 1:
        return refs[0][...]
    return jnp.concatenate([ref[...] for ref in refs], axis=0)


def single_kernel(left_ref, *refs):
    refs[-1][...] = product(left_ref[...], joined(refs[:-1]))


def gate_kernel(count, last, left_ref, *refs):
    weights = joined(refs[:count])
    slope_ref, activated_ref, grads_ref = refs[count:]
    rows = left_ref.shape[0] // 2

    def work(width):
        for start in (0, rows):
            part = slice(start, start + rows)
            both = product(left_ref[part, :], weights[:, : 2 * width])
            gate, up = both[:, :width], both[:, width:]
            sigmoid = jax.nn.sigmoid(gate)
            swish = gate * sigmoid
            activated_ref[part, :width] = (swish * up).astype(jnp.bfloat16)
            upstream = slope_ref[part, :width]
            slope = sigmoid * (1.0 + gate * (1.0 - sigmoid))
            grads_ref[part, :width] = (upstream * up * slope).astype(jnp.bfloat16)
            grads_ref[part, width : 2 * width] = (upstream * swish).astype(jnp.bfloat16)
            rest = -width % LANES
            if rest:
                activated_ref[part, width : width + rest] = jnp.zeros((rows, rest), jnp.bfloat16)

    step, final = pl.program_id(0), pl.num_programs(0) - 1

    @pl.when(step < final)
    def _():
        work(TILE)

    @pl.when(step == final)
    def _():
        work(last)


TILE = 256


def piece_specs(pieces, width):
    return [pl.BlockSpec((piece.shape[0], width), lambda j: (0, j)) for piece in pieces]


def pair_columns(width):
    full_width = width
    if 2 * (width % TILE) % LANES:
        full_width = -(-width // LANES) * LANES
    return [
        (start, 2 * start, min(TILE, full_width - start), min(TILE, width - start))
        for start in range(0, full_width, TILE)
    ]


def paired_kernel(gate_ref, up_ref, out_ref):
    for start, place, size, real in pair_columns(gate_ref.shape[1]):
        for side, ref in enumerate((gate_ref, up_ref)):
            tile = ref[:, start : start + real]
            if real < size:
                rest = jnp.zeros((tile.shape[0], size - real), tile.dtype)
                tile = jnp.concatenate([tile, rest], axis=1)
            out_ref[:, place + side * size : place + (side + 1) * size] = tile


def paired(gate, up):
    width = sum(2 * size for _, _, size, _ in pair_columns(gate.shape[1]))
    shape = (gate.shape[0], width)
    return pl.pallas_call(
        paired_kernel,
        in_specs=[full(gate), full(up)],
        out_specs=pl.BlockSpec(shape, lambda: (0, 0)),
        out_shape=jax.ShapeDtypeStruct(shape, gate.dtype),
        compiler_params=pltpu.CompilerParams(vmem_limit_bytes=ROOM),
        cost_estimate=lasting(4),
        name="paired",
    )(gate, up)


def unpaired_kernel(own_ref, low_ref, high_ref, weights_ref, gate_ref, up_ref, sums_ref):
    sums = None
    for start, place, size, real in pair_columns(gate_ref.shape[1]):
        for side, out_ref in enumerate((gate_ref, up_ref)):
            part = slice(place + side * size, place + (side + 1) * size)
            total = own_ref[:, part].astype(jnp.float32) + low_ref[:, part].astype(jnp.float32)
            total = total + high_ref[:, part].astype(jnp.float32)
            out_ref[:, start : start + real] = total[:, :real]
            term = jnp.sum(total * weights_ref[:, part].astype(jnp.float32), axis=1, keepdims=True)
            sums = term if sums is None else sums + term
    sums_ref[...] = jnp.broadcast_to(sums, sums_ref.shape)


def unpaired(own, low, high, weights, width):
    rows = weights.shape[0]
    shapes = [(rows, width), (rows, width), (rows, LANES)]
    return pl.pallas_call(
        unpaired_kernel,
        grid=(1,),
        in_specs=[pl.BlockSpec(weights.shape, lambda _: (0, 0))] * 4,
        out_specs=[pl.BlockSpec(shape, lambda _: (0, 0)) for shape in shapes],
        out_shape=[jax.ShapeDtypeStruct(shape, jnp.float32) for shape in shapes],
        compiler_params=pltpu.CompilerParams(vmem_limit_bytes=ROOM),
        cost_estimate=lasting(5),
        name="unpaired",
    )(own, low, high, weights)


def feed_product(left, pieces):
    rows, width = left.shape[0], pieces[0].shape[1]
    return pl.pallas_call(
        single_kernel,
        grid=(pl.cdiv(width, TILE),),
        in_specs=[full(left)] + piece_specs(pieces, TILE),
        out_specs=pl.BlockSpec((rows, TILE), lambda j: (0, j)),
        out_shape=jax.ShapeDtypeStruct((rows, width), jnp.float32),
        compiler_params=pltpu.CompilerParams(vmem_limit_bytes=ROOM),
        cost_estimate=lasting(15),
        name="feed_product",
    )(left, *pieces)


def feed_gate(left, pieces, upstream):
    rows, width = upstream.shape
    pair_width = pieces[0].shape[1]
    column = lambda size: pl.BlockSpec((rows, size), lambda j: (0, j))
    return pl.pallas_call(
        functools.partial(gate_kernel, len(pieces), pair_width // 2 % TILE or TILE),
        grid=(pl.cdiv(width, TILE),),
        in_specs=[full(left)] + piece_specs(pieces, 2 * TILE) + [column(TILE)],
        out_specs=[column(TILE), column(2 * TILE)],
        out_shape=[
            jax.ShapeDtypeStruct((rows, width), jnp.bfloat16),
            jax.ShapeDtypeStruct((rows, pair_width), jnp.bfloat16),
        ],
        compiler_params=pltpu.CompilerParams(vmem_limit_bytes=ROOM),
        cost_estimate=lasting(26),
        name="feed_gate",
    )(left, *pieces, upstream)


def terms_kernel(count, *refs):
    arrays, out_ref = refs[: count + 1], refs[-4]
    left_ref, right_ref, sems = refs[-3:]
    rows = right_ref.shape[0] // count
    places = [left_ref]
    places += [right_ref.at[pl.ds(number * rows, rows), :] for number in range(count)]
    copies = [
        pltpu.make_async_copy(array, place, sems.at[number])
        for number, (array, place) in enumerate(zip(arrays, places))
    ]
    for copy in copies:
        copy.start()
    copies[0].wait()
    ready = 0
    for start in range(0, right_ref.shape[0], 2 * TILE):
        stop = min(start + 2 * TILE, right_ref.shape[0])
        while ready * rows < stop:
            copies[ready + 1].wait()
            ready += 1
        part = slice(start, stop)
        out_ref[:, part] = product_right(left_ref[...], right_ref[part, :]).astype(jnp.bfloat16)


def feed_terms(left, pieces, total, block, earlier=None, cost=lasting(18)):
    arrays = [left, *pieces]
    rows, width = left.shape
    columns = sum(piece.shape[0] for piece in pieces)
    low = jnp.bfloat16
    return pl.pallas_call(
        functools.partial(terms_kernel, len(pieces)),
        grid=(1,),
        in_specs=[ANYWHERE] * (len(arrays) + (earlier is not None)),
        out_specs=pl.BlockSpec((rows, columns), lambda _: (0, block)),
        out_shape=jax.ShapeDtypeStruct((rows, total), low),
        scratch_shapes=[
            pltpu.VMEM((rows, width), low),
            pltpu.VMEM((columns, width), low),
            pltpu.SemaphoreType.DMA((len(arrays),)),
        ],
        input_output_aliases={} if earlier is None else {len(arrays): 0},
        compiler_params=pltpu.CompilerParams(vmem_limit_bytes=ROOM),
        cost_estimate=cost,
        name="feed_terms",
    )(*arrays, *([] if earlier is None else [earlier]))


def latent_back_kernel(
    copies, rank, team_ref, back_ref, raw_ref, input_ref, gain_query_ref, gain_latent_ref,
    here_ref, low_ref, high_ref, *refs,
):
    outs, (grad_ref, held_ref, sems) = refs[:-3], refs[-3:]
    cuts = [(slice(0, rank), gain_query_ref), (slice(rank, rank + KVR), gain_latent_ref)]
    for part, gain_ref in cuts:
        values = raw_ref[:, part]
        inverse = normalize(values, gain_ref[...])[1]
        grad = normalize_back(
            values, inverse, gain_ref[...], back_ref[:, part].astype(jnp.float32)
        )
        grad_ref[:, part] = grad.astype(jnp.bfloat16)
    key = back_ref[:, rank + KVR :].astype(jnp.float32)
    grad_ref[:, rank + KVR :] = (
        key * here_ref[...]
        - roll_lanes(key, -ROPE // 2) * low_ref[...]
        - roll_lanes(key, ROPE // 2) * high_ref[...]
    ).astype(jnp.bfloat16)
    held_ref[...] = product_left(input_ref[...], grad_ref[...]).astype(jnp.bfloat16)
    started = []
    for number, (out, row, rows, block, team) in enumerate(copies):
        start = block if team is None else (block + team_ref[team]) * rows
        copy = pltpu.make_async_copy(
            held_ref.at[pl.ds(pl.multiple_of(start, 16), rows), :],
            outs[out].at[pl.ds(row, rows), :],
            sems.at[number],
        )
        copy.start()
        started.append(copy)
    for copy in started:
        copy.wait()


def latent_back(teams, back, raw, inputs, gains, tables, copies, heights, rank):
    rows, width = inputs.shape
    out = back.shape[1]
    low = jnp.bfloat16
    shapes = [((rows, out), low)]
    arrays = [back, raw, inputs, *gains, *tables]
    results = pl.pallas_call(
        functools.partial(latent_back_kernel, copies, rank),
        in_specs=[SCALARS] + [full(array) for array in arrays],
        out_specs=[ANYWHERE] * len(heights)
        + [pl.BlockSpec(shape, lambda: (0, 0)) for shape, _ in shapes],
        out_shape=[jax.ShapeDtypeStruct((height, out), low) for height in heights]
        + [jax.ShapeDtypeStruct(*shape) for shape in shapes],
        scratch_shapes=[pltpu.VMEM((width, out), low), pltpu.SemaphoreType.DMA((len(copies),))],
        compiler_params=pltpu.CompilerParams(vmem_limit_bytes=ROOM),
        cost_estimate=lasting(8),
        name="latent_back",
    )(teams, *arrays)
    return results[:-1], results[-1]


def head_sums_kernel(
    copies, rank, spots_ref, latents_ref, query_ref, key_value_ref, upstream_ref, heads_ref,
    out_ref, q_ref, kv_ref, o_ref, sems,
):
    q_ref[...] = product_left(latents_ref[:, :rank], query_ref[...]).astype(jnp.bfloat16)
    kv_ref[...] = product_left(latents_ref[:, rank : rank + KVR], key_value_ref[...]).astype(
        jnp.bfloat16
    )
    started = []

    def send(wanted):
        for number, (side, row, rows, place, column) in enumerate(copies):
            if side not in wanted:
                continue
            start = row if isinstance(row, int) else spots_ref[row[0]] * rows
            held = (q_ref, kv_ref, o_ref)[side]
            copy = pltpu.make_async_copy(
                held.at[pl.ds(pl.multiple_of(start, 16), rows), :],
                out_ref.at[pl.ds(place, rows), pl.ds(column, held.shape[1])],
                sems.at[number],
            )
            copy.start()
            started.append(copy)

    send((0, 1))
    o_ref[...] = product_left(upstream_ref[...], heads_ref[...]).astype(jnp.bfloat16)
    send((2,))
    for copy in started:
        copy.wait()


def head_sums(spots, latents, query, key_value, upstream, heads, rank, query_rows, latent_rows, out_rows):
    width, out_width = query.shape[1], heads.shape[1]
    count = spots.shape[0]
    rows = query_rows + latent_rows + out_rows // 2
    copies = []
    for spot in range(count):
        start = spot * rows
        copies.append((0, (spot,), query_rows, start, 0))
        copies.append((1, (spot,), latent_rows, start + query_rows, 0))
        for side in (0, 1):
            copies.append(
                (2, spot * out_rows + side * (out_rows // 2), out_rows // 2,
                 start + query_rows + latent_rows, side * out_width)
            )
    low = jnp.bfloat16
    arrays = [latents, query, key_value, upstream, heads]
    return pl.pallas_call(
        functools.partial(head_sums_kernel, copies, rank),
        in_specs=[SCALARS] + [full(array) for array in arrays],
        out_specs=pl.BlockSpec((count * rows, width), lambda: (0, 0)),
        out_shape=jax.ShapeDtypeStruct((count * rows, width), low),
        scratch_shapes=[
            pltpu.VMEM((rank, width), low),
            pltpu.VMEM((KVR, width), low),
            pltpu.VMEM((upstream.shape[1], out_width), low),
            pltpu.SemaphoreType.DMA((len(copies),)),
        ],
        compiler_params=pltpu.CompilerParams(vmem_limit_bytes=ROOM),
        cost_estimate=lasting(20),
        name="head_sums",
    )(spots, *arrays)


def token_back_kernel(grad_ref, weights_ref, tokens_ref, hidden_ref, gain_ref, out_ref):
    upstream = product_right(grad_ref[...], weights_ref[...])
    values = tokens_ref[...].astype(jnp.float32)
    inverse = normalize(values, gain_ref[...])[1]
    out_ref[...] = hidden_ref[...] + normalize_back(values, inverse, gain_ref[...], upstream)


def token_back(grad, weights, tokens, hidden_grad, gain):
    arrays = [grad, weights, tokens, hidden_grad, gain]
    return pl.pallas_call(
        token_back_kernel,
        in_specs=[full(array) for array in arrays],
        out_specs=full(hidden_grad),
        out_shape=jax.ShapeDtypeStruct(hidden_grad.shape, jnp.float32),
        compiler_params=pltpu.CompilerParams(vmem_limit_bytes=ROOM),
        cost_estimate=lasting(8),
        name="token_back",
    )(*arrays)


def reorder_kernel(spots_ref, in_ref, out_ref):
    width = in_ref.shape[1]
    count = spots_ref.shape[0]
    size = width // count
    window = min(-(-(size + LANES - 1) // LANES) * LANES, width)
    for place in range(count):
        start = spots_ref[place] * size
        base = jnp.minimum(start // LANES * LANES, width - window)
        held = in_ref[:, pl.ds(pl.multiple_of(base, LANES), window)].astype(jnp.float32)
        held = pltpu.roll(held, lax.rem(window - (start - base), window), 1)
        out_ref[:, place * size : (place + 1) * size] = held[:, :size].astype(out_ref.dtype)


def reorder(values, spots):
    return pl.pallas_call(
        reorder_kernel,
        in_specs=[SCALARS, full(values)],
        out_specs=full(values),
        out_shape=jax.ShapeDtypeStruct(values.shape, values.dtype),
        compiler_params=pltpu.CompilerParams(vmem_limit_bytes=ROOM),
        cost_estimate=lasting(4),
        name="reorder",
    )(spots, values)


class Ring:
    def __init__(self, axis):
        self.axis = axis
        self.count = lax.axis_size(axis)
        self.half = self.count // 2
        order = list(range(0, self.count, 2)) + list(range(self.count - 1, 0, -2))
        self.me = lax.axis_index(axis)
        self.spot = self.place(self.me)
        indices = jnp.arange(self.count, dtype=jnp.int32)
        self.ahead = self.owner(indices)
        self.behind = lax.rem(self.place(indices) - self.spot + self.count, self.count)
        self.up = [(order[i], order[(i + 1) % self.count]) for i in range(self.count)]
        self.down = [(b, a) for a, b in self.up]

    def place(self, index):
        return jnp.where(index % 2 == 0, index // 2, self.count - (index + 1) // 2)

    def owner(self, step):
        spot = lax.rem(self.spot + step + self.count, self.count)
        return jnp.where(spot < self.half, 2 * spot, 2 * self.count - 1 - 2 * spot)

    def send_up(self, block):
        return lax.ppermute(block, self.axis, self.up)

    def send_down(self, block):
        return lax.ppermute(block, self.axis, self.down)


class Gather:
    def __init__(self, ring, shard):
        self.ring = ring
        self.rows = shard.shape[0]
        self.low = self.high = shard
        self.blocks = {0: shard}
        self.step = 0

    def advance(self):
        ring = self.ring
        if self.done:
            return
        self.step += 1
        if self.step < ring.half:
            self.low = ring.send_up(self.low)
            self.high = ring.send_down(self.high)
            self.blocks[self.step] = self.high
            self.blocks[ring.count - self.step] = self.low
        else:
            cut = self.rows // 2
            self.low = ring.send_up(self.low[:cut])
            self.high = ring.send_down(self.high[cut:])
            self.blocks[ring.half] = None

    @property
    def done(self):
        return self.step >= self.ring.half

    def finish(self):
        while not self.done:
            self.advance()
        self.blocks[self.ring.half] = jnp.concatenate([self.low, self.high], axis=0)
        return [self.blocks[spot] for spot in range(self.ring.count)]


class Scatter:
    def __init__(self, ring, take, rows):
        self.ring = ring
        self.take = lambda step, start, size: take(step % ring.count, start, size)
        self.rows = rows
        self.step = 0
        self.low = self.high = None

    def add(self, a, b):
        return (a.astype(jnp.float32) + b.astype(jnp.float32)).astype(b.dtype)

    def advance(self):
        ring, rows, cut = self.ring, self.rows, self.rows // 2
        if self.done:
            return
        ahead = ring.half - self.step
        if self.step:
            self.low, self.high = lax.optimization_barrier((self.low, self.high))
        self.step += 1
        if ahead == ring.half:
            low = self.take(ahead, 0, cut)
            high = self.take(ahead, cut, rows - cut)
        elif ahead == ring.half - 1:
            low = self.take(ahead, 0, rows)
            high = self.take(-ahead, 0, rows)
            low = jnp.concatenate([self.add(self.low, low[:cut]), low[cut:]], axis=0)
            high = jnp.concatenate([high[:cut], self.add(self.high, high[cut:])], axis=0)
        else:
            low = self.add(self.low, self.take(ahead, 0, rows))
            high = self.add(self.high, self.take(-ahead, 0, rows))
        self.sent = (low, high)
        self.low = ring.send_up(low)
        self.high = ring.send_down(high)

    @property
    def done(self):
        return self.step >= self.ring.half

    def finish(self):
        while not self.done:
            self.advance()
        own = self.take(0, 0, self.rows).astype(jnp.float32)
        return own + self.low.astype(jnp.float32) + self.high.astype(jnp.float32)


def stacked(ring, grads):
    rows = grads.shape[0] // ring.count

    def take(spot, start, size):
        return lax.slice_in_dim(grads, spot * rows + start, spot * rows + start + size, axis=0)

    return Scatter(ring, take, rows)


def staged(ring, left, right):
    size = left.shape[1] // ring.count
    low, high = ring.count // 4, ring.count // 4 + ring.half
    parts = {}
    held = [right]

    def take(spot, start, rows):
        name = 1 if low <= spot < high else 0 if spot < low else 2
        first = (0, low, high)[name]
        if name not in parts:
            last = (low, high, ring.count)[name]
            columns = lax.slice_in_dim(left, first * size, last * size, axis=1)
            parts[name] = product_left(columns, held[0]).astype(jnp.bfloat16)
        begin = (spot - first) * size + start
        return lax.slice_in_dim(parts[name], begin, begin + rows, axis=0)

    scatter = Scatter(ring, take, size)
    scatter.held = held
    scatter.parts = parts
    return scatter


def delay(scatter, *others):
    scatter.held[0] = follow(scatter.held[0], *others)


def follow(values, *others):
    return lax.optimization_barrier((values, others))[0]


def ends(*streams):
    return [(stream.low, stream.high) for stream in streams]


def hold(stream, *others):
    stream.low, stream.high = follow((stream.low, stream.high), *others)


def swap(values, bit):
    count = lax.axis_size("tensor")
    return lax.ppermute(values, "tensor", [(i, i ^ bit) for i in range(count)])


def pad_heads(weights, heads):
    rows = weights.shape[0]
    width = weights.shape[1] // heads
    padded = jnp.pad(weights.reshape(rows, heads, width), ((0, 0), (0, 0), (0, LANES - width)))
    return padded.reshape(rows, heads * LANES)


def on_device(
    tokens,
    segments,
    positions,
    norm_input,
    norm_query,
    norm_latent,
    norm_hidden,
    query_down,
    latent_down,
    query_up,
    latent_up,
    attention_out,
    gate_weight,
    up_weight,
    down_weight,
    cotangent,
):
    low = jnp.bfloat16
    local_rows = tokens.shape[0]
    shard = lax.axis_index("tensor")
    offset = shard * local_rows
    length = segments.shape[0]
    local_heads = HEADS // lax.axis_size("tensor")
    pairs = local_heads // 2
    rank = query_down.shape[1]
    ring = Ring("fsdp")
    everyone = lax.axis_size("fsdp") * lax.axis_size("tensor")
    teams = lax.axis_size("tensor")
    gains_own = jnp.concatenate([norm_input, norm_hidden, norm_query, norm_latent])
    gain_sizes = [norm_input.shape[0], norm_hidden.shape[0], norm_query.shape[0], norm_latent.shape[0]]
    gain_width = -(-gains_own.shape[0] // LANES) * LANES
    spare = LANES - NOPE - ROPE
    gain_rows = -(-gains_own.shape[0] // spare)
    down_rows = query_down.shape[0]
    down_width = rank + KVR + LANES
    gain_part = jnp.pad(gains_own, (0, gain_rows * spare - gains_own.shape[0]))
    gain_part = jnp.pad(gain_part.reshape(gain_rows, spare), ((0, down_rows - gain_rows), (0, 0)))
    packed = jnp.concatenate(
        [
            query_down,
            latent_down[:, :KVR],
            jnp.zeros((down_rows, NOPE), low),
            latent_down[:, KVR:],
            gain_part,
        ],
        axis=1,
    )
    feed_width = gate_weight.shape[1]
    feed_rows = gate_weight.shape[0]
    feed_pad = -feed_width % LANES
    widen = lambda weights: jnp.pad(weights, ((0, 0), (0, feed_pad)))
    head_width = 2 * pairs * LANES
    query_rows, latent_rows, out_rows = query_up.shape[0], latent_up.shape[0], attention_out.shape[1]
    out_width = attention_out.shape[0]
    out_t = attention_out.T
    mixed = jnp.concatenate(
        [
            pad_heads(query_up, local_heads),
            latent_up,
            jnp.concatenate([out_t[: out_rows // 2], out_t[out_rows // 2 :]], axis=1),
        ],
        axis=0,
    )
    mixed_up = Gather(ring, mixed)
    down_up = Gather(ring, widen(down_weight.T))
    pair_own = paired(gate_weight, up_weight)
    pair_up = Gather(ring, pair_own)

    tokens_ring = reorder(tokens, ring.ahead)
    upstream = reorder(cotangent, ring.ahead)
    here, turn_low, turn_high = rotary_lanes(positions)
    tables = (here, turn_low, turn_high)
    local_tables = [lax.dynamic_slice_in_dim(table, offset, local_rows) for table in tables]
    query_feat, key_feat = segment_lanes(segments)
    key_feat = key_feat.astype(low)
    ahead, behind = ring.ahead, ring.behind
    team_ids = shard ^ jnp.asarray([0, 2, 1, 3], jnp.int32)

    small_up = Gather(ring, packed)
    pieces, copies = [], []

    def collect(block, spot, first):
        across = swap(block, 2)
        for team, piece in enumerate((block, across, swap(block, 1), swap(across, 1))):
            rows = block.shape[0]
            copies.append((len(pieces), 0, rows, spot * teams, team, first))
            pieces.append(piece)

    collect(small_up.low, 0, 0)
    while not small_up.done:
        swapped = [piece for place, piece in enumerate(pieces) if place % 4]
        small_up.advance()
        mixed_up.advance()
        if not small_up.done:
            collect(small_up.high, small_up.step, 0)
            collect(small_up.low, ring.count - small_up.step, 0)
            hold(small_up, ends(mixed_up), swapped)
            hold(mixed_up, ends(small_up))
    collect(jnp.concatenate([small_up.low, small_up.high], axis=0), ring.half, 0)
    copies = [(piece, row, rows, block, team) for piece, row, rows, block, team, _ in copies]
    hold(down_up, ends(mixed_up, small_up))
    down_up.advance()
    if down_rows % 16:
        table = [[None] * teams for _ in range(ring.count)]
        for piece, row, _, block, team in copies:
            table[block // teams][team] = pieces[piece][row : row + gain_rows, down_width - spare :]
        table = jnp.stack([part for group in zip(*table) for part in group])
        table = table.reshape(teams, ring.count, gain_rows * spare)
        places = shard ^ jnp.arange(teams, dtype=jnp.int32)
        places = jnp.where(places == 1, 2, jnp.where(places == 2, 1, places))
        table = jnp.take(table, places, axis=0)
    else:
        table = collect_rows(
            team_ids, pieces, [(piece, row, block, team) for piece, row, _, block, team in copies]
        )
        table = table.reshape(ring.count, teams, 16, LANES)[:, :, :gain_rows, LANES - spare :]
        table = jnp.transpose(table, (1, 0, 2, 3)).reshape(teams, ring.count, gain_rows * spare)
    table = table.astype(jnp.float32)
    gain_parts = []
    start = 0
    for number, size in enumerate(gain_sizes):
        part = jnp.transpose(table[:, :, start : start + size], (1, 0, 2))
        if number >= 2:
            part = jnp.take(part, behind, axis=0)
        gain_parts.append(part.reshape(1, -1))
        start += size
    gain_in, gain_hidden, gain_query, gain_latent = gain_parts
    if down_rows % 16:
        whole = jnp.zeros((everyone * down_rows, down_width), low)
        for piece, row, rows, block, team in copies:
            whole = lax.dynamic_update_slice(
                whole, pieces[piece][row : row + rows], ((block + team_ids[team]) * rows, 0)
            )
        pieces, copies = [whole], [(0, 0, whole.shape[0], 0, None)]
    latent_send, latent_raw, attention_input, down_projections = project(
        team_ids, tokens_ring, (gain_in, gain_query, gain_latent), local_tables, pieces, copies, rank
    )
    latent_send = follow(latent_send, ends(down_up))
    latents = lax.all_gather(latent_send, "tensor", axis=0, tiled=True)
    hold(down_up, latent_send)
    down_up.advance()
    latents = follow(latents, ends(down_up))
    hold(pair_up, ends(down_up))
    mixed_blocks = mixed_up.finish()
    if query_rows % 16 or latent_rows % 16 or out_rows % 32:
        mixed_all = jnp.stack([mixed_blocks[0]] * ring.count)
        for spot, block in enumerate(mixed_blocks):
            mixed_all = lax.dynamic_update_slice(mixed_all, block[None], (ring.owner(spot), 0, 0))
        wq = mixed_all[:, :query_rows].reshape(-1, head_width)
        wkv = mixed_all[:, query_rows : query_rows + latent_rows].reshape(-1, head_width)
        outs = [block[query_rows + latent_rows :] for block in mixed_blocks]
        attention_out_t = jnp.concatenate(
            [block[:, side * out_width : (side + 1) * out_width] for block in outs for side in (0, 1)],
            axis=0,
        )
    else:
        copies = []
        for spot in range(ring.count):
            copies.append((spot, 0, query_rows, 0, head_width, 0, (spot, query_rows)))
            copies.append((spot, query_rows, latent_rows, 0, head_width, 1, (spot, latent_rows)))
            for side in (0, 1):
                copies.append(
                    (spot, query_rows + latent_rows, out_rows // 2, side * out_width, out_width, 2,
                     spot * out_rows + side * (out_rows // 2))
                )
        wq, wkv, attention_out_t = assemble(
            ahead,
            mixed_blocks,
            copies,
            [(ring.count * query_rows, head_width), (ring.count * latent_rows, head_width),
             (ring.count * out_rows, out_width)],
        )
    down_up.advance()
    pair_up.advance()
    feed_upstream = follow(RESIDUAL * upstream.astype(jnp.float32), latents).astype(low)
    feed_upstream = lax.all_gather(feed_upstream, "tensor", axis=0, tiled=True)
    rope = latents[:, rank + KVR :] + key_feat
    heads, query_heads, key_value, log_totals = attention_forward(
        latents, wq, wkv, rope, query_feat, tables, pairs
    )
    branch_terms = product_right(heads, attention_out_t).astype(low)
    branch_terms = follow(branch_terms, feed_upstream, ends(pair_up))
    attention_branch = lax.psum_scatter(branch_terms, "tensor", scatter_dimension=0, tiled=True)
    attention_branch = follow(attention_branch, ends(down_up))
    downs = down_up.finish()
    if ring.count > 8:
        downs = [jnp.concatenate(downs, axis=0)]
    activated_grad = feed_product(feed_upstream, downs)
    hidden = tokens_ring.astype(jnp.float32) + RESIDUAL * attention_branch.astype(jnp.float32)
    feed_normed, inverse_hidden = normalize(hidden, gain_hidden)
    pair_up.advance()
    feed_normed = follow(feed_normed.astype(low), ends(pair_up))
    feed_seq = lax.all_gather(feed_normed, "tensor", axis=0, tiled=True)
    hold(pair_up, ends(down_up))
    pair_up.advance()
    hold(pair_up, activated_grad)
    weights = pair_up.finish()
    if ring.count > 8:
        weights = [jnp.concatenate(weights, axis=0)]
    activated, pair_grad = feed_gate(feed_seq, weights, activated_grad)

    grad_down = staged(ring, feed_upstream, activated)
    grad_down.advance()
    grad_pair = staged(ring, feed_seq, follow(pair_grad, grad_down.sent))
    grad_pair.advance()
    hold(grad_down, grad_pair.sent)
    grad_down.advance()
    half = max(len(weights) // 2, 1)
    width = feed_seq.shape[1]
    pair_grad = follow(pair_grad, grad_down.sent)
    terms = feed_terms(pair_grad, weights[:half], width, 0)
    hold(grad_pair, terms)
    grad_pair.advance()
    if len(weights) > half:
        terms = follow(terms, grad_pair.sent)
        terms = feed_terms(pair_grad, weights[half:], width, 1, terms)
    terms = follow(terms, ends(grad_down))
    feed_back = lax.psum_scatter(terms, "tensor", scatter_dimension=0, tiled=True)
    activated = follow(activated, terms)
    feed_branch = feed_terms(activated, downs[:half], width, 0, None, lasting(11))
    delay(grad_down, terms)
    hold(grad_down, terms)
    grad_down.advance()
    feed_back = follow(feed_back, grad_down.sent)
    delay(grad_pair, grad_down.sent)
    grad_pair.advance()
    grad_pair.take(0, 0, 1), grad_down.take(0, 0, 1)
    feed_back = follow(feed_back, grad_pair.parts[0], grad_down.parts[0], feed_branch)
    hidden_back = normalize_back(
        hidden, inverse_hidden, gain_hidden, feed_back.astype(jnp.float32)
    )
    hidden_grad = upstream.astype(jnp.float32) + hidden_back
    upstream_send = follow((RESIDUAL * hidden_grad).astype(low), grad_pair.sent, ends(grad_down))
    attention_upstream = lax.all_gather(upstream_send, "tensor", axis=0, tiled=True)
    attention_upstream = follow(attention_upstream, ends(grad_pair))
    heads_grad = product(attention_upstream, attention_out_t).astype(low)
    grad_pair.advance()
    heads_grad = follow(heads_grad, grad_pair.sent)
    query_raw_grad, key_value_grad, key_rope_grad = attention_backward(
        query_heads, key_value, heads_grad, log_totals, rope, tables
    )
    query_raw_grad, key_value_grad = follow((query_raw_grad, key_value_grad), ends(grad_pair))
    hold(grad_down, query_raw_grad)
    grad_down.advance()
    latent_terms = jnp.concatenate(
        [
            product_right(query_raw_grad, wq),
            product_right(key_value_grad, wkv),
            key_rope_grad,
        ],
        axis=1,
    ).astype(low)
    latent_grad = lax.psum_scatter(latent_terms, "tensor", scatter_dimension=0, tiled=True)
    upstream_late, query_raw_grad, key_value_grad = follow(
        (attention_upstream, query_raw_grad, key_value_grad), latent_terms, grad_down.sent
    )
    if query_rows % 16 or latent_rows % 16 or out_rows % 32:
        sums = [
            jnp.take(product_left(left, right).astype(low).reshape(ring.count, -1, head_width), ahead, axis=0)
            for left, right in (
                (latents[:, :rank], query_raw_grad),
                (latents[:, rank : rank + KVR], key_value_grad),
            )
        ]
        out_sums = product_left(upstream_late, heads).astype(low)
        out_sums = out_sums.reshape(ring.count, 2, out_rows // 2, out_width)
        sums.append(jnp.concatenate([out_sums[:, 0], out_sums[:, 1]], axis=2))
        mixed_sums = jnp.concatenate(sums, axis=1).reshape(-1, head_width)
    else:
        mixed_sums = head_sums(
            ahead, latents, query_raw_grad, key_value_grad, upstream_late, heads,
            rank, query_rows, latent_rows, out_rows,
        )
    grad_mixed = stacked(ring, follow(mixed_sums, ends(grad_down)))
    grad_mixed.advance()
    grad_mixed.advance()
    if len(downs) > half:
        activated = follow(activated, grad_mixed.sent)
        feed_branch = feed_terms(activated, downs[half:], width, 1, feed_branch, lasting(11))
    latent_grad = follow(latent_grad, feed_branch, ends(grad_mixed))
    feed_branch = lax.psum_scatter(feed_branch, "tensor", scatter_dimension=0, tiled=True)
    pair = 2 * down_rows
    height = ring.count * pair
    heights = [height, height]
    copies = [
        (team // 2, spot * pair + (team % 2) * down_rows, down_rows, spot * teams, team)
        for spot in range(ring.count)
        for team in range(teams)
    ]
    aligned = down_rows % 16 == 0
    if not aligned:
        copies, heights = [(0, 0, 2 * height, 0, None)], [2 * height]
    sent, latent_low = latent_back(
        team_ids, latent_grad, latent_raw, attention_input, (gain_query, gain_latent),
        local_tables, copies, heights, rank,
    )
    if not aligned:
        blocks = jnp.take(
            sent[0].reshape(ring.count, teams, down_rows, down_width), team_ids, axis=1
        )
        sent = [blocks[:, :2].reshape(height, -1), blocks[:, 2:].reshape(height, -1)]

    def add_low(a, b):
        return (a.astype(jnp.float32) + b.astype(jnp.float32)).astype(low)

    other_sums = swap(sent[1], 1)
    token_grad = token_back(
        latent_low, down_projections, tokens_ring, hidden_grad, gain_in
    )
    hold(grad_mixed, latent_low)
    grad_mixed.advance()
    other_sums = follow(other_sums, token_grad)
    grad_small = stacked(ring, add_low(sent[0], other_sums))
    grad_small.advance()
    hold(grad_mixed, grad_small.sent)
    grad_mixed.advance()
    grad_small.advance()
    token_grad = reorder(follow(token_grad, grad_small.sent), ring.behind)
    hold(grad_down, ends(grad_small))
    hold(grad_small, token_grad)
    grad_small.advance()
    while not grad_pair.done:
        grad_pair.advance()
    hold(grad_pair, grad_small.sent)
    grad_gate_own, grad_up_own, pair_sums = unpaired(
        grad_pair.parts[0], grad_pair.low, grad_pair.high, pair_own, feed_width
    )
    hold(grad_small, pair_sums)
    grad_small.advance()
    feed_branch = follow(feed_branch, grad_small.sent)
    output = hidden + RESIDUAL * feed_branch.astype(jnp.float32)
    output = reorder(output.astype(low), ring.behind)
    grad_mixed_own = grad_mixed.finish()
    row_sums = lambda weights, grads: jnp.sum(weights.astype(jnp.float32) * grads, axis=1)
    head_rows = query_rows + latent_rows
    gain_sums = jnp.concatenate(
        [pair_sums[:, 0], row_sums(mixed[:head_rows], grad_mixed_own[:head_rows])]
    )
    gain_sums = jnp.pad(gain_sums, (0, -gain_sums.shape[0] % LANES))[None]
    gain_sums = gain_sums + swap(gain_sums, 1)
    gain_sums = (gain_sums + swap(gain_sums, 2))[0]
    hold(grad_small, output, gain_sums)
    small_own = grad_small.finish()
    small_other = small_own[down_rows:].astype(low)
    packed_own = small_own[:down_rows] + swap(small_other, 2).astype(jnp.float32)
    rope_from = rank + KVR + NOPE
    lanes = jnp.arange(down_width) < rope_from + ROPE
    grad_gain_input = jnp.sum(
        jnp.where(lanes, packed.astype(jnp.float32) * packed_own, 0.0), axis=1
    ) / norm_input.astype(jnp.float32)
    grad_query_own = grad_mixed_own[:query_rows].reshape(query_rows, local_heads, LANES)
    grad_out_own = grad_mixed_own[query_rows + latent_rows :]
    grad_out_own = jnp.concatenate(
        [grad_out_own[:, :out_width], grad_out_own[:, out_width:]], axis=0
    )
    gain_grads = []
    start = 0
    for gain in (norm_hidden, norm_query, norm_latent):
        size = gain.shape[0]
        own = lax.dynamic_slice_in_dim(gain_sums, start + shard * size, size)
        gain_grads.append(own / gain.astype(jnp.float32))
        start += size * teams
    return (
        output,
        token_grad,
        grad_gain_input,
        gain_grads[1],
        gain_grads[2],
        gain_grads[0],
        packed_own[:, :rank],
        jnp.concatenate(
            [packed_own[:, rank : rank + KVR], packed_own[:, rope_from : rope_from + ROPE]],
            axis=1,
        ),
        grad_query_own[:, :, : NOPE + ROPE].reshape(query_rows, -1),
        grad_mixed_own[query_rows : query_rows + latent_rows],
        grad_out_own.T,
        grad_gate_own,
        grad_up_own,
        grad_down.finish()[:, :feed_width].T,
    )


def solution(mesh):
    return jax.shard_map(
        on_device,
        mesh=mesh,
        in_specs=(
            P(("fsdp", "tensor"), None),
            P("fsdp"),
            P("fsdp"),
            P(("fsdp", "tensor")),
            P(("fsdp", "tensor")),
            P(("fsdp", "tensor")),
            P(("fsdp", "tensor")),
            P(("fsdp", "tensor"), None),
            P(("fsdp", "tensor"), None),
            P("fsdp", "tensor"),
            P("fsdp", "tensor"),
            P("tensor", "fsdp"),
            P("fsdp", "tensor"),
            P("fsdp", "tensor"),
            P("tensor", "fsdp"),
            P(("fsdp", "tensor"), None),
        ),
        out_specs=(
            P(("fsdp", "tensor"), None),
            P(("fsdp", "tensor"), None),
            P(("fsdp", "tensor")),
            P(("fsdp", "tensor")),
            P(("fsdp", "tensor")),
            P(("fsdp", "tensor")),
            P(("fsdp", "tensor"), None),
            P(("fsdp", "tensor"), None),
            P("fsdp", "tensor"),
            P("fsdp", "tensor"),
            P("tensor", "fsdp"),
            P("fsdp", "tensor"),
            P("fsdp", "tensor"),
            P("tensor", "fsdp"),
        ),
        check_vma=False,
    )
```
